32 devices in a mesh: row: 4 (over y, x), col: 8 (over z, core).
Axes of the slice: x: 2, y: 2, z: 4, core: 2. Of those that a mesh axis runs over, the one named last changes fastest.
Arguments:
- queries: bfloat16 [16384, 768], P(('col', 'row')), may hold values from -11 to 11
- key_vectors: bfloat16 [16384, 768], P(('col', 'row')), may hold values from -11 to 11
- value_vectors: bfloat16 [16384, 768], P(('col', 'row')), may hold values from -6 to 6
- out_grad: bfloat16 [16384, 768], P(('col', 'row')), may hold values from -6 to 6
- near_offsets: int32 [12], replicated, may hold values from 0 to 15, as said below
- far_offsets: int32 [12], replicated, may hold values from 0 to 255, as said below
Outputs:
- attended: bfloat16 [16384, 768], P(('col', 'row'))
- query_grad: bfloat16 [16384, 768], P(('col', 'row'))
- key_grad: bfloat16 [16384, 768], P(('col', 'row'))
- value_grad: bfloat16 [16384, 768], P(('col', 'row'))
The draws below stay inside these ranges and needn't reach their ends.
Inputs may be any that keep to these rules, and one draw needn't show every extreme that they name: `near_offsets`: some head has offset 0 and some head offset 16 - 1. `far_offsets`: some head has offset 0 and some head offset 256 - 1.
All inputs are finite; a program needn't handle non-finite values.
Results may differ from the reference program's by a relative error of at most 0.022.
Values may be sent and summed in bfloat16 or wider, within the bound.
No kernel may reach another device: no remote copies, remote signals or barrier semaphores. Data moves between devices by JAX's collectives and lax.ppermute only.
A program may use at most 128 MiB of HBM per device.

```python
import jax
import jax.numpy as jnp
from jax import lax

H = 12
HD = 64
R2 = 16
R3 = 256
S1 = 512
SEG2 = 2048
TOKENS = 16384


def offset_set(subkey, dilation):
    first, second, third = jax.random.split(subkey, 3)
    chosen = jax.random.permutation(first, dilation)[:H]
    low_head = jax.random.randint(second, (), 0, H)
    advance = jax.random.randint(third, (), 1, H)
    high_head = (low_head + advance) % H
    chosen = chosen.at[low_head].set(0)
    chosen = chosen.at[high_head].set(dilation - 1)
    return chosen.astype(jnp.int32)


def offsets_pair(key):
    return (offset_set(jax.random.fold_in(key, 11), R2), offset_set(jax.random.fold_in(key, 12), R3))


def draw_near_offsets(key, part):
    return offsets_pair(key)[0]


def draw_far_offsets(key, part):
    return offsets_pair(key)[1]


def draw_queries(key, part):
    key = jax.random.fold_in(key, 3)
    result = jnp.clip(jax.random.normal(key, (TOKENS, H, HD), jnp.float32), -5.0, 5.0)
    return result.reshape(TOKENS, H * HD).astype(jnp.bfloat16)


def draw_key_vectors(key, part):
    key = jax.random.fold_in(key, 4)
    result = jnp.clip(jax.random.normal(key, (TOKENS, H, HD), jnp.float32), -5.0, 5.0)
    return result.reshape(TOKENS, H * HD).astype(jnp.bfloat16)


def block_scale(rng, shape, cuts, smallest, top_value):
    def one(axis_at, shards_of):
        steps = jax.random.uniform(jax.random.fold_in(jax.random.fold_in(rng, 6), axis_at), (shards_of,), jnp.float32, smallest / len(cuts), top_value / len(cuts))
        return jnp.repeat(jnp.exp(steps), shape[axis_at] // shards_of).reshape((-1,) + (1,) * (len(shape) - axis_at - 1))

    gain = one(*cuts[0])
    for cut in cuts[1:]:
        gain = gain * one(*cut)
    return gain


def gaussian(own_key, dims, width, limit, shards=(), dtype=jnp.bfloat16):
    array = width * jax.random.normal(own_key, dims, jnp.float32)
    if shards:
        array = array * block_scale(own_key, dims, shards, -0.22, 0.18)
    return jnp.clip(array, -limit, limit).astype(dtype)


def setup_inputs(seed: int = 0) -> dict:
    key_of = jax.random.split(jax.random.key(seed), 7)
    queries = draw_queries(jax.random.fold_in(key_of[6], 71), 0)
    key_vectors = draw_key_vectors(jax.random.fold_in(key_of[6], 71), 0)
    value_vectors = gaussian(key_of[2], (TOKENS, H * HD), 1.0, 6.0, ((0, 32),))
    out_grad = gaussian(key_of[3], (TOKENS, H * HD), 1.0, 6.0, ((0, 32),))
    near_offsets = draw_near_offsets(jax.random.fold_in(key_of[6], 71), 0)
    far_offsets = draw_far_offsets(jax.random.fold_in(key_of[6], 71), 0)
    return dict(queries=queries, key_vectors=key_vectors, value_vectors=value_vectors, out_grad=out_grad, near_offsets=near_offsets, far_offsets=far_offsets)


NEG = -1e30


def lower(count):
    return lax.broadcasted_iota(jnp.int32, (count, count), 1) <= lax.broadcasted_iota(jnp.int32, (count, count), 0)


def attend(queries, keys_block, values_block, allowed):
    scale = queries.shape[-1] ** -0.5
    scores = jnp.einsum("...qd,...kd->...qk", queries.astype(jnp.float32), keys_block.astype(jnp.float32)) * scale
    scores = jnp.where(allowed, scores, NEG)
    highest = jnp.max(scores, axis=-1)
    weights = jnp.exp(scores - highest[..., None])
    total = jnp.sum(weights, axis=-1)
    weights_half = weights.astype(jnp.bfloat16)
    mixed = jnp.einsum("...qk,...kd->...qd", weights_half.astype(jnp.float32), values_block.astype(jnp.float32))
    return highest, total, mixed


def backward_block(queries, keys_block, values_block, grad_out, log_total, row_dot, allowed):
    scale = queries.shape[-1] ** -0.5
    scores = jnp.einsum("...qd,...kd->...qk", queries.astype(jnp.float32), keys_block.astype(jnp.float32)) * scale
    scores = jnp.where(allowed, scores, NEG)
    probs = jnp.exp(scores - log_total[..., None])
    grad_prob = jnp.einsum("...qd,...kd->...qk", grad_out.astype(jnp.float32), values_block.astype(jnp.float32))
    grad_score = probs * (grad_prob - row_dot[..., None])
    score_half = grad_score.astype(jnp.bfloat16).astype(jnp.float32)
    prob_half = probs.astype(jnp.bfloat16).astype(jnp.float32)
    grad_query = scale * jnp.einsum("...qk,...kd->...qd", score_half, keys_block.astype(jnp.float32))
    grad_key = scale * jnp.einsum("...qk,...qd->...kd", score_half, queries.astype(jnp.float32))
    grad_value = jnp.einsum("...qk,...qd->...kd", prob_half, grad_out.astype(jnp.float32))
    return grad_query, grad_key, grad_value


def pick(source, offsets, dilation):
    head_count, length = source.shape[0], source.shape[1]
    trailing = source.shape[2:]
    shaped = source.reshape((head_count, length // dilation, dilation) + trailing)
    position = offsets.astype(jnp.int32).reshape((head_count, 1, 1) + (1,) * len(trailing))
    position = jnp.broadcast_to(position, (head_count, length // dilation, 1) + trailing)
    return jnp.take_along_axis(shaped, position, axis=2)[:, :, 0]


def spread(values, offsets, dilation, filler):
    head_count, rows = values.shape[0], values.shape[1]
    trailing = values.shape[2:]
    lanes = lax.broadcasted_iota(jnp.int32, (1, 1, dilation) + (1,) * len(trailing), 2)
    chosen = lanes == offsets.astype(jnp.int32).reshape((head_count, 1, 1) + (1,) * len(trailing))
    placed = jnp.where(chosen, values[:, :, None], filler)
    return placed.reshape((head_count, rows * dilation) + trailing)


def reference(queries, key_vectors, value_vectors, out_grad, near_offsets, far_offsets):
    length = queries.shape[0]

    def heads_first(source):
        return jnp.moveaxis(source.reshape(length, H, HD), 1, 0)

    def tokens_first(source):
        return jnp.moveaxis(source, 0, 1).reshape(length, H * HD)

    query_h = heads_first(queries)
    key_h = heads_first(key_vectors)
    value_h = heads_first(value_vectors)
    grad_h = heads_first(out_grad)
    seg_count = length // S1

    def segments(source):
        return jnp.moveaxis(source.reshape((H, seg_count, S1) + source.shape[2:]), 1, 0)

    def joined(source):
        return jnp.moveaxis(source, 0, 1).reshape((H, length) + source.shape[3:])

    near_count = length // SEG2
    near_width = SEG2 // R2

    def near(source):
        chosen = pick(source, near_offsets, R2)
        return chosen.reshape((H, near_count, near_width) + chosen.shape[2:])

    def near_back(source, filler):
        return spread(source.reshape((H, length // R2) + source.shape[3:]), near_offsets, R2, filler)

    def far(source):
        return pick(source, far_offsets, R3)

    def far_back(source, filler):
        return spread(source, far_offsets, R3, filler)

    causal_one = lower(S1)
    first = lax.map(lambda parts: attend(parts[0], parts[1], parts[2], causal_one), (segments(query_h), segments(key_h), segments(value_h)))
    second = attend(near(query_h), near(key_h), near(value_h), lower(near_width))
    third = attend(far(query_h), far(key_h), far(value_h), lower(length // R3))
    high_one, total_one, mixed_one = joined(first[0]), joined(first[1]), joined(first[2])
    high_two, total_two, mixed_two = near_back(second[0], NEG), near_back(second[1], 0.0), near_back(second[2], 0.0)
    high_three, total_three, mixed_three = far_back(third[0], NEG), far_back(third[1], 0.0), far_back(third[2], 0.0)
    top = jnp.maximum(jnp.maximum(high_one, high_two), high_three)
    weight_one = jnp.exp(high_one - top)
    weight_two = jnp.exp(high_two - top)
    weight_three = jnp.exp(high_three - top)
    total = weight_one * total_one + weight_two * total_two + weight_three * total_three
    mixed = weight_one[..., None] * mixed_one + weight_two[..., None] * mixed_two + weight_three[..., None] * mixed_three
    attended_h = (mixed / total[..., None]).astype(jnp.bfloat16)
    log_total = top + jnp.log(total)
    row_dot = jnp.sum(grad_h.astype(jnp.float32) * attended_h.astype(jnp.float32), axis=-1)
    first_grads = lax.map(lambda parts: backward_block(parts[0], parts[1], parts[2], parts[3], parts[4], parts[5], causal_one), (segments(query_h), segments(key_h), segments(value_h), segments(grad_h), segments(log_total), segments(row_dot)))
    second_grads = backward_block(near(query_h), near(key_h), near(value_h), near(grad_h), near(log_total), near(row_dot), lower(near_width))
    third_grads = backward_block(far(query_h), far(key_h), far(value_h), far(grad_h), far(log_total), far(row_dot), lower(length // R3))
    results = []
    for which in range(3):
        summed = joined(first_grads[which]) + near_back(second_grads[which], 0.0) + far_back(third_grads[which], 0.0)
        results.append(tokens_first(summed.astype(jnp.bfloat16)))
    return tokens_first(attended_h), results[0], results[1], results[2]
```

```python
import functools

import jax
import jax.numpy as jnp
from jax import lax
from jax.experimental import pallas as pl
from jax.experimental.pallas import tpu as pltpu
from jax.sharding import PartitionSpec as P

H = 12
HD = 64
R2 = 16
R3 = 256
S1 = 512
SEG2 = 2048

NEG = -1e30
SCALE = HD**-0.5
GH = 4
GW = GH * HD
PW = 2 * HD
FM = 16
F32 = jnp.float32
BF = jnp.bfloat16
VMEM_LIMIT = 48 * 1024 * 1024


def iota(shape, axis):
    return lax.broadcasted_iota(jnp.int32, shape, axis)


def nn(a, b):
    return lax.dot_general(a, b, (((1,), (0,)), ((), ())), preferred_element_type=F32)


def nt(a, b):
    return lax.dot_general(a, b, (((1,), (1,)), ((), ())), preferred_element_type=F32)


def tn(a, b):
    return lax.dot_general(a, b, (((0,), (0,)), ((), ())), preferred_element_type=F32)


def onehot(cond):
    return jnp.where(cond, 1.0, 0.0).astype(BF)


def lane_offsets(ref, group):
    head = iota((1, GW), 1) // HD
    out = jnp.zeros((1, GW), jnp.int32)
    for h in range(GH):
        out = jnp.where(head == h, ref[group * GH + h], out)
    return out


def expand(x):
    head = iota((1, GW), 1) // HD
    return jnp.concatenate([x * onehot(head == h) for h in range(GH)], axis=0)


def collapse(x):
    n = x.shape[0] // GH
    head = iota((1, GW), 1) // HD
    out = x[:n]
    for h in range(1, GH):
        out = jnp.where(head == h, x[h * n : (h + 1) * n], out)
    return out


def split3(x):
    hi = x.astype(BF)
    rest = x - hi.astype(F32)
    mid = rest.astype(BF)
    low = (rest - mid.astype(F32)).astype(BF)
    return hi.astype(F32), mid.astype(F32), low.astype(F32)


def pack_aux(log_total, row_dot):
    lane = iota((1, log_total.shape[1]), 1) % HD
    out = jnp.zeros(log_total.shape, F32)
    for at, piece in enumerate(split3(log_total) + split3(row_dot)):
        out = jnp.where(lane == at, piece, out)
    return out


def piece_rows(rows, width, which):
    head = iota((rows, width), 1) // HD
    lane = iota((rows, width), 1) % HD // 3
    return head, lane == which


def spread_sum(x, width):
    block = onehot(iota((width, width), 0) // HD == iota((width, width), 1) // HD)
    hi = x.astype(BF)
    low = (x - hi.astype(F32)).astype(BF)
    return nn(hi, block) + nn(low, block)


def piece_spread(aux, which):
    a = iota((GW, GW), 0)
    sel = onehot((a // HD == iota((GW, GW), 1) // HD) & (a % HD // 3 == which))
    return nn(aux, sel)


def piece_column(aux_expanded, which):
    a = iota((GW, 128), 0)
    return nn(aux_expanded, onehot(a % HD // 3 == which))[:, :1]


def near_select(n, length):
    return onehot(iota((n, length), 1) // R2 == iota((n, length), 0))


def near_place(n, length):
    return onehot(iota((length, n), 0) // R2 == iota((length, n), 1))


def far_select(rows, length, first):
    return onehot(iota((rows, length), 1) // R3 == iota((rows, length), 0) - first)


def far_place(length):
    return onehot(iota((length, FM), 0) // R3 == iota((length, FM), 1))


def token_masks(near_ref, far_ref, group, length):
    t = iota((length, GW), 0)
    near = t % R2 == lane_offsets(near_ref, group)
    far = t % R3 == lane_offsets(far_ref, group)
    return near, far


def pick_kernel(peers, near_ref, far_ref, q_ref, k_ref, v_ref, g_ref, kv_ref, qg_ref, fr_ref, *msg_refs):
    group = pl.program_id(0)
    length = q_ref.shape[0]
    n, f = length // R2, length // R3
    near, far = token_masks(near_ref, far_ref, group, length)
    near, far = onehot(near), onehot(far)
    sel = near_select(n, length)
    q, k, v, g = q_ref[...], k_ref[...], v_ref[...], g_ref[...]
    picked = [nn(sel, x * near).astype(BF) for x in (k, v, q, g)]
    kv = jnp.concatenate(picked[:2], axis=0)
    qg = jnp.concatenate(picked[2:], axis=0)
    kv_ref[...] = kv
    qg_ref[...] = qg
    fr = jnp.zeros((FM, GW), F32)
    for at, x in enumerate((q, k, v, g)):
        fr += nn(far_select(FM, length, at * f), x * far)
    fr_ref[...] = fr.astype(BF)
    own = lax.axis_index("row") % peers
    for slot in range(1, peers):
        later = (own ^ slot) > own

        @pl.when(later)
        def _(slot=slot):
            msg_refs[slot - 1][...] = kv

        @pl.when(jnp.logical_not(later))
        def _(slot=slot):
            msg_refs[slot - 1][...] = qg


def forward_kernel(strip, q_ref, k_ref, v_ref, g_ref, att_ref, aux_ref):
    length = q_ref.shape[0]
    lane = iota((1, PW), 1)
    first = lane < HD
    in_head = (onehot(first), onehot(jnp.logical_not(first)))
    k = k_ref[...]
    v = v_ref[...]
    with_ones = [v * in_head[h] + in_head[1 - h] for h in range(2)]
    diag = iota((strip, strip), 1) <= iota((strip, strip), 0)
    for r in range(length // strip):
        rows = slice(r * strip, (r + 1) * strip)
        width = (r + 1) * strip
        q = q_ref[rows, :] * jnp.asarray(SCALE, BF)
        tops, outs = [], []
        for h in range(2):
            s = nt(q * in_head[h], k[:width])
            last = jnp.where(diag, s[:, r * strip :], NEG)
            s = jnp.concatenate([s[:, : r * strip], last], axis=1) if r else last
            top = jnp.max(s, axis=1, keepdims=True)
            w = jnp.exp(s - top).astype(BF)
            tops.append(top)
            outs.append(nn(w, with_ones[h][:width]))
        total = pltpu.roll(jnp.where(first, outs[1], outs[0]), HD, 1)
        att = jnp.where(first, outs[0], outs[1]) / total
        log_total = jnp.where(first, tops[0], tops[1]) + jnp.log(total)
        row_dot = spread_sum(g_ref[rows, :].astype(F32) * att, PW)
        att_ref[rows, :] = att.astype(BF)
        aux_ref[rows, :] = pack_aux(log_total, row_dot).astype(BF)


def near_valid_queries(shape, n, own):
    row, lane = iota(shape, 0) % n, iota(shape, 1)
    slot, key = lane // n, lane % n
    return ((slot ^ own) < own) | ((slot == 0) & (key <= row))


def near_valid_keys(shape, n, own):
    row, lane = iota(shape, 0) % n, iota(shape, 1)
    slot, query = lane // n, lane % n
    return ((slot ^ own) > own) | ((slot == 0) & (row <= query))


def merge_kernel(peers, near_ref, far_ref, kv_ref, qg_ref, *rest):
    got, (aux_ref, att_ref, fr_ref, out_ref, aux_out_ref, att_out_ref) = rest[: peers - 1], rest[peers - 1 :]
    group = pl.program_id(0)
    length = aux_ref.shape[0]
    n, f = length // R2, length // R3
    own = lax.axis_index("row") % peers
    near, far = token_masks(near_ref, far_ref, group, length)
    keys = jnp.concatenate([r[:n, :] for r in (kv_ref, *got)], axis=0)
    values = jnp.concatenate([r[n:, :] for r in (kv_ref, *got)], axis=0)
    queries = expand(qg_ref[:n, :] * jnp.asarray(SCALE, BF))
    s = nt(queries, keys)
    s = jnp.where(near_valid_queries(s.shape, n, own), s, NEG)
    top = jnp.max(s, axis=1, keepdims=True)
    w = jnp.exp(s - top)
    total = jnp.sum(w, axis=1, keepdims=True)
    out2 = collapse(nn(w.astype(BF), values) / total)
    log2 = collapse(jnp.broadcast_to(top + jnp.log(total), (GH * n, GW)))

    sel = near_select(n, length)
    nearh = onehot(near)
    aux = aux_ref[...]
    att = att_ref[...]
    log1 = piece_spread(nn(sel, aux * nearh).astype(BF), 0)
    out1 = nn(sel, att * nearh)
    top = jnp.maximum(log1, log2)
    e1, e2 = jnp.exp(log1 - top), jnp.exp(log2 - top)
    both = e1 + e2
    log12 = top + jnp.log(both)
    out12 = (e1 * out1 + e2 * out2) / both
    dot12 = spread_sum(qg_ref[n:, :].astype(F32) * out12, GW)
    aux12 = pack_aux(log12, dot12).astype(BF)
    place = near_place(n, length)
    att_out_ref[...] = jnp.where(near, nn(place, out12.astype(BF)), att.astype(F32)).astype(BF)
    aux_all = jnp.where(near, nn(place, aux12), aux.astype(F32))
    far_aux = nn(far_select(FM, length, 4 * f), aux_all.astype(BF) * onehot(far))
    out_ref[:n, :] = aux12
    out_ref[n:, :] = (fr_ref[...].astype(F32) + far_aux).astype(BF)
    lane = iota((1, GW), 1) % HD
    aux_out_ref[...] = jnp.where(far, jnp.where(lane == 0, -NEG, 0.0), aux_all).astype(BF)


def backward_kernel(strip, aliased, q_ref, k_ref, v_ref, g_ref, aux_ref, *rest):
    dq_ref, dk_ref, dv_ref = rest[aliased:]
    length = q_ref.shape[0]
    first = iota((1, PW), 1) < HD
    in_head = (onehot(first), onehot(jnp.logical_not(first)))
    q = q_ref[...] * jnp.asarray(SCALE, BF)
    g = g_ref[...]
    k = k_ref[...]
    v = v_ref[...]
    row, lane = iota((8, PW), 0), iota((8, PW), 1)
    pieces = onehot((lane // HD == row % 2) & (lane % HD // 3 == row // 2) & (row < 4))
    stats = nt(pieces, aux_ref[...])
    eye = onehot(iota((PW, PW), 0) == iota((PW, PW), 1))
    k_t = (nt(eye, k) * SCALE).astype(BF)
    diag = iota((strip, strip), 0) <= iota((strip, strip), 1)
    dq_t = [[jnp.zeros((HD, strip), F32) for _ in range(length // strip)] for _ in range(2)]
    for c in range(length // strip):
        rows = slice(c * strip, (c + 1) * strip)
        dks, dvs = [], []
        for h in range(2):
            s = nt(k[rows] * in_head[h], q[c * strip :])
            p = jnp.exp(s - stats[h : h + 1, c * strip :])
            head = jnp.where(diag, p[:, :strip], 0.0)
            p = jnp.concatenate([head, p[:, strip:]], axis=1) if p.shape[1] > strip else head
            dp = nt(v[rows] * in_head[h], g[c * strip :])
            ds = (p * (dp - stats[2 + h : 3 + h, c * strip :])).astype(BF)
            dvs.append(nn(p.astype(BF), g[c * strip :]))
            dks.append(nn(ds, q[c * strip :]))
            part = nn(k_t[h * HD : (h + 1) * HD, rows], ds)
            for r in range(c, length // strip):
                at = (r - c) * strip
                dq_t[h][r] += part[:, at : at + strip]
        dk_ref[rows, :] = jnp.where(first, dks[0], dks[1]).astype(BF)
        dv_ref[rows, :] = jnp.where(first, dvs[0], dvs[1]).astype(BF)
    for r in range(length // strip):
        both = jnp.concatenate([dq_t[0][r], dq_t[1][r]], axis=0)
        dq_ref[r * strip : (r + 1) * strip, :] = both.T.astype(BF)


def far_seq(index, f, peers, masks, own):
    slot = index // f
    seq = own ^ (slot % peers)
    bits = slot // peers
    for at, mask in enumerate(masks):
        seq = seq ^ (((bits >> at) & 1) * mask)
    return seq * f + index % f


def final_kernel(peers, masks, near_ref, far_ref, kv_ref, qg_ref, *rest):
    got, rest = rest[: peers - 1], rest[peers - 1 :]
    auxs, rest = rest[:peers], rest[peers:]
    fa_ref, k_ref, v_ref, dq1_ref, dk1_ref, dv1_ref, att_ref, att_out, dq_out, dk_out, dv_out = rest
    group = pl.program_id(0)
    length = k_ref.shape[0]
    n, f = length // R2, length // R3
    blocks = fa_ref.shape[0] // FM
    F = blocks * f
    row_here = lax.axis_index("row")
    own = row_here % peers
    seq = lax.axis_index("col") * lax.axis_size("row") + row_here
    near, far = token_masks(near_ref, far_ref, group, length)
    scale = jnp.asarray(SCALE, BF)

    r, c = iota((5 * F, blocks * FM), 0), iota((5 * F, blocks * FM), 1)
    i, at = r // F, r % F
    sel = onehot(c == at // f * FM + i * f + at % f)
    fa = nn(sel, fa_ref[...]).astype(BF)
    fq, fk, fv, fg, faux = (fa[i * F : (i + 1) * F] for i in range(5))
    qx, gx, ax = expand(fq * scale), expand(fg), expand(faux)
    s = nt(qx, fk)
    dp = nt(gx, fv)
    place_q = far_seq(iota(s.shape, 0) % F, f, peers, masks, seq)
    place_k = far_seq(iota(s.shape, 1), f, peers, masks, seq)
    ok = place_k <= place_q
    s = jnp.where(ok, s, NEG)
    top = jnp.max(s, axis=1, keepdims=True)
    w = jnp.exp(s - top)
    total = jnp.sum(w, axis=1, keepdims=True)
    log3 = top + jnp.log(total)
    dot3 = jnp.sum(w * dp, axis=1, keepdims=True) / total
    log12, dot12 = piece_column(ax, 0), piece_column(ax, 1)
    top = jnp.maximum(log12, log3)
    e12, e3 = jnp.exp(log12 - top), jnp.exp(log3 - top)
    both = e12 + e3
    log_all = top + jnp.log(both)
    dot_all = (e12 * dot12 + e3 * dot3) / both
    p = jnp.exp(s - log_all)
    ds = p * (dp - dot_all)
    pb, dsb = p.astype(BF), ds.astype(BF)
    far_dv = tn(pb, gx)[:FM]
    far_dk = tn(dsb, qx)[:FM]
    far_dq = collapse(nn(dsb, fk))[:FM] * SCALE
    far_out = collapse(nn(pb, fv))[:FM]
    keep = collapse(jnp.broadcast_to(e12 / both, (GH * F, GW)))[:FM]
    att = att_ref[...]
    far_out += keep * nn(far_select(FM, length, 0), att * onehot(far))

    def own_rows(x):
        return jnp.concatenate([x[h * F : h * F + FM] for h in range(GH)], axis=0)

    qx, gx, log_own, dot_own = own_rows(qx), own_rows(gx), own_rows(log_all), own_rows(dot_all)
    k, v = k_ref[...], v_ref[...]
    r = iota((GH * FM, 1), 0)
    reach = jnp.zeros((GH * FM, 1), jnp.int32)
    for h in range(GH):
        reach = jnp.where(r // FM == h, far_ref[group * GH + h], reach)
    reach = jnp.where(r % FM < f, reach + r % FM * R3, -1)
    ok = iota((GH * FM, length), 1) <= reach
    p = jnp.where(ok, jnp.exp(nt(qx, k) - log_own), 0.0)
    ds = (p * (nt(gx, v) - dot_own)).astype(BF)
    far_dq += collapse(nn(ds, k)) * SCALE
    dk = tn(ds, qx)
    dv = tn(p.astype(BF), gx)

    rows = peers * n
    final_aux = collapse(
        pack_aux(jnp.broadcast_to(log_all, (GH * F, GW)), jnp.broadcast_to(dot_all, (GH * F, GW)))
    )[:FM].astype(BF)
    r, c = iota((rows, FM), 0), iota((rows, FM), 1)
    subst = nn(onehot(c == r // n * f + r % n * R2 // R3), final_aux)
    noff, foff = lane_offsets(near_ref, group), lane_offsets(far_ref, group)
    also_far = (iota((rows, GW), 0) % (R3 // R2) == foff // R2) & (foff % R2 == noff)
    naux = jnp.concatenate([a[:n, :] for a in auxs], axis=0)
    naux = jnp.where(also_far, subst, naux.astype(F32)).astype(BF)
    heads = [kv_ref, *got]
    keys = jnp.concatenate([x[:n, :] for x in heads], axis=0)
    values = jnp.concatenate([x[n:, :] for x in heads], axis=0)
    heads = [qg_ref, *got]
    queries = jnp.concatenate([x[:n, :] for x in heads], axis=0) * scale
    grads = jnp.concatenate([x[n:, :] for x in heads], axis=0)

    ax = expand(naux[:n])
    s = nt(expand(queries[:n]), keys)
    dp = nt(expand(grads[:n]), values)
    ok = near_valid_queries(s.shape, n, own)
    p = jnp.where(ok, jnp.exp(s - piece_column(ax, 0)), 0.0)
    ds = (p * (dp - piece_column(ax, 1))).astype(BF)
    near_dq = collapse(nn(ds, keys)) * SCALE

    s = nt(expand(keys[:n]), queries)
    dp = nt(expand(values[:n]), grads)
    ok = near_valid_keys(s.shape, n, own)
    r, c = iota((GH * n, GW), 0), iota((GH * n, GW), 1)
    mine = c // HD == r // n
    log_k = nt(onehot(mine & (c % HD // 3 == 0)), naux)
    dot_k = nt(onehot(mine & (c % HD // 3 == 1)), naux)
    p = jnp.where(ok, jnp.exp(s - log_k), 0.0)
    ds = (p * (dp - dot_k)).astype(BF)
    near_dk = collapse(nn(ds, queries))
    near_dv = collapse(nn(p.astype(BF), grads))

    place_n, place_f = near_place(n, length), far_place(length)

    def terms(near_part, far_part):
        return jnp.where(near, nn(place_n, near_part.astype(BF)), 0.0) + jnp.where(
            far, nn(place_f, far_part.astype(BF)), 0.0
        )

    att_out[...] = jnp.where(far, nn(place_f, far_out.astype(BF)), att.astype(F32)).astype(BF)
    dq_out[...] = (dq1_ref[...].astype(F32) + terms(near_dq, far_dq)).astype(BF)
    dk_out[...] = (dk1_ref[...].astype(F32) + dk + terms(near_dk, far_dk)).astype(BF)
    dv_out[...] = (dv1_ref[...].astype(F32) + dv + terms(near_dv, far_dv)).astype(BF)


def smem():
    return pl.BlockSpec(memory_space=pltpu.SMEM)


def group_block(rows):
    return pl.BlockSpec((rows, GW), lambda g: (0, g))


def params():
    return pltpu.CompilerParams(vmem_limit_bytes=VMEM_LIMIT)


def shards(queries, key_vectors, value_vectors, out_grad, near_offsets, far_offsets):
    length, width = queries.shape
    row_count = lax.axis_size("row")
    col_count = lax.axis_size("col")
    peers = SEG2 // length
    n, f = length // R2, length // R3
    groups = width // GW
    pairs = width // PW

    def like(rows):
        return jax.ShapeDtypeStruct((rows, width), BF)

    def swap(x, axis, mask):
        size = lax.axis_size(axis)
        return lax.ppermute(x, axis, [(i, i ^ mask) for i in range(size)])

    picked = pl.pallas_call(
        functools.partial(pick_kernel, peers),
        grid=(groups,),
        in_specs=[smem(), smem()] + [group_block(length)] * 4,
        out_specs=[group_block(2 * n)] * 2 + [group_block(FM)] + [group_block(2 * n)] * (peers - 1),
        out_shape=[like(2 * n)] * 2 + [like(FM)] + [like(2 * n)] * (peers - 1),
        compiler_params=params(),
        name="pick",
    )(near_offsets, far_offsets, queries, key_vectors, value_vectors, out_grad)
    kv, qg, fr, msgs = picked[0], picked[1], picked[2], picked[3:]
    got = [swap(msgs[s - 1], "row", s) for s in range(1, peers)]

    pair_block = pl.BlockSpec((length, PW), lambda p: (0, p))
    ops = 2 * H * length * length * HD
    att1, aux1 = pl.pallas_call(
        functools.partial(forward_kernel, 256),
        grid=(pairs,),
        in_specs=[pair_block] * 4,
        out_specs=[pair_block] * 2,
        out_shape=[like(length)] * 2,
        compiler_params=params(),
        cost_estimate=pl.CostEstimate(flops=2 * ops * 4, bytes_accessed=6 * length * width * 2, transcendentals=0),
        name="forward",
    )(queries, key_vectors, value_vectors, out_grad)

    mine, aux, att12 = pl.pallas_call(
        functools.partial(merge_kernel, peers),
        grid=(groups,),
        in_specs=[smem(), smem()] + [group_block(2 * n)] * (peers + 1) + [group_block(length)] * 2 + [group_block(FM)],
        out_specs=[group_block(n + FM)] + [group_block(length)] * 2,
        out_shape=[like(n + FM)] + [like(length)] * 2,
        compiler_params=params(),
        name="merge",
    )(near_offsets, far_offsets, kv, qg, *got, aux1, att1, fr)
    theirs = [swap(mine, "row", s) for s in range(1, peers)]

    pieces = 3
    per = pairs // pieces
    grads = []
    for piece in range(pieces):
        block = pl.BlockSpec((length, PW), lambda p, piece=piece: (0, piece * per + p))
        any_spec = pl.BlockSpec(memory_space=pl.ANY)
        aliased = len(grads)
        grads = pl.pallas_call(
            functools.partial(backward_kernel, 256, aliased),
            grid=(per,),
            in_specs=[block] * 5 + [any_spec] * aliased,
            out_specs=[block] * 3,
            out_shape=[like(length)] * 3,
            input_output_aliases={5 + i: i for i in range(aliased)},
            compiler_params=params(),
            cost_estimate=pl.CostEstimate(
                flops=5 * ops * 4 // pieces, bytes_accessed=8 * length * width * 2 // pieces, transcendentals=0
            ),
            name="backward",
        )(queries, key_vectors, value_vectors, out_grad, aux, *grads)

    far_all = jnp.concatenate([x[n:] for x in (mine, *theirs)], axis=0)
    masks = []
    for axis, size, least in (("row", row_count, peers), ("col", col_count, 1)):
        mask = size // 2
        while mask >= least:
            far_all = jnp.concatenate([far_all, swap(far_all, axis, mask)], axis=0)
            masks.append(mask if axis == "row" else mask * row_count)
            mask //= 2

    return pl.pallas_call(
        functools.partial(final_kernel, peers, tuple(masks)),
        grid=(groups,),
        in_specs=[smem(), smem()]
        + [group_block(2 * n)] * (peers + 1)
        + [group_block(n + FM)] * peers
        + [group_block(far_all.shape[0])]
        + [group_block(length)] * 6,
        out_specs=[group_block(length)] * 4,
        out_shape=[like(length)] * 4,
        compiler_params=params(),
        name="final",
    )(near_offsets, far_offsets, kv, qg, *got, mine, *theirs, far_all, key_vectors, value_vectors, *grads, att12)


def solution(mesh):
    placed = (
        P(("col", "row"), None),
        P(("col", "row"), None),
        P(("col", "row"), None),
        P(("col", "row"), None),
        P(),
        P(),
    )
    return jax.shard_map(
        shards,
        mesh=mesh,
        in_specs=placed,
        out_specs=(
            P(("col", "row"), None),
            P(("col", "row"), None),
            P(("col", "row"), None),
            P(("col", "row"), None),
        ),
        check_vma=False,
    )
```

```python
import functools

import jax
import jax.numpy as jnp
from jax import lax
from jax.experimental import pallas as pl
from jax.experimental.pallas import tpu as pltpu
from jax.sharding import PartitionSpec as P

H = 12
HD = 64
R2 = 16
R3 = 256
S1 = 512
SEG2 = 2048

NEG = -1e30
SCALE = HD**-0.5
GH = 4
GW = GH * HD
PW = 2 * HD
FM = 16
F32 = jnp.float32
BF = jnp.bfloat16
VMEM_LIMIT = 40
PICK_LIMIT = 62


def iota(shape, axis):
    return lax.broadcasted_iota(jnp.int32, shape, axis)


def nn(a, b):
    return lax.dot_general(a, b, (((1,), (0,)), ((), ())), preferred_element_type=F32)


def nt(a, b):
    return lax.dot_general(a, b, (((1,), (1,)), ((), ())), preferred_element_type=F32)


def tn(a, b):
    return lax.dot_general(a, b, (((0,), (0,)), ((), ())), preferred_element_type=F32)


def onehot(cond):
    return jnp.where(cond, 1.0, 0.0).astype(BF)


def lane_offsets(ref, group):
    head = iota((1, GW), 1) // HD
    out = jnp.zeros((1, GW), jnp.int32)
    for h in range(GH):
        out = jnp.where(head == h, ref[group * GH + h], out)
    return out


def expand(x):
    head = iota((1, GW), 1) // HD
    return jnp.concatenate([x * onehot(head == h) for h in range(GH)], axis=0)


def collapse(x):
    n = x.shape[0] // GH
    head = iota((1, GW), 1) // HD
    out = x[:n]
    for h in range(1, GH):
        out = jnp.where(head == h, x[h * n : (h + 1) * n], out)
    return out


def split3(x):
    hi = x.astype(BF)
    rest = x - hi.astype(F32)
    mid = rest.astype(BF)
    low = (rest - mid.astype(F32)).astype(BF)
    return hi.astype(F32), mid.astype(F32), low.astype(F32)


def pack_aux(log_total, row_dot):
    lane = iota((1, log_total.shape[1]), 1) % HD
    out = jnp.zeros(log_total.shape, F32)
    for at, piece in enumerate(split3(log_total) + split3(row_dot)):
        out = jnp.where(lane == at, piece, out)
    return out


def spread_sum(x, width):
    block = onehot(iota((width, width), 0) // HD == iota((width, width), 1) // HD)
    hi = x.astype(BF)
    low = (x - hi.astype(F32)).astype(BF)
    return nn(hi, block) + nn(low, block)


def piece_column(aux_expanded, which):
    a = iota((GW, 128), 0)
    return nn(aux_expanded, onehot(a % HD // 3 == which))[:, :1]


def near_select(n, length):
    return onehot(iota((n, length), 1) // R2 == iota((n, length), 0))


def near_place(n, length):
    return onehot(iota((length, n), 0) // R2 == iota((length, n), 1))


def far_select(rows, length, first):
    return onehot(iota((rows, length), 1) // R3 == iota((rows, length), 0) - first)


def far_place(length):
    return onehot(iota((length, FM), 0) // R3 == iota((length, FM), 1))


def token_masks(near_ref, far_ref, group, length):
    t = iota((length, GW), 0)
    near = t % R2 == lane_offsets(near_ref, group)
    far = t % R3 == lane_offsets(far_ref, group)
    return near, far


def pick_kernel(peers, near_ref, far_ref, q_ref, k_ref, v_ref, g_ref, kv_ref, qg_ref, fr_ref, *msg_refs):
    group = pl.program_id(0)
    length = q_ref.shape[0]
    n, f = length // R2, length // R3
    near, far = token_masks(near_ref, far_ref, group, length)
    near, far = onehot(near), onehot(far)
    sel = near_select(n, length)
    q, k, v, g = q_ref[...], k_ref[...], v_ref[...], g_ref[...]
    picked = [nn(sel, x * near).astype(BF) for x in (k, v, q, g)]
    kv = jnp.concatenate(picked[:2], axis=0)
    qg = jnp.concatenate(picked[2:], axis=0)
    kv_ref[...] = kv
    qg_ref[...] = qg
    fr = jnp.zeros((FM, GW), F32)
    for at, x in enumerate((q, k, v, g)):
        fr += nn(far_select(FM, length, at * f), x * far)
    fr_ref[...] = fr.astype(BF)
    own = lax.axis_index("row") % peers
    for slot in range(1, peers):
        later = (own ^ slot) > own

        @pl.when(later)
        def _(slot=slot):
            msg_refs[slot - 1][...] = kv

        @pl.when(jnp.logical_not(later))
        def _(slot=slot):
            msg_refs[slot - 1][...] = qg


def staged(units, stages, skew):
    for t in range(len(units) + (len(stages) - 1) * skew):
        for i, stage in enumerate(stages):
            if 0 <= t - i * skew < len(units):
                stage(*units[t - i * skew])


def lockstep(bodies):
    bodies = list(bodies)
    while bodies:
        for body in list(bodies):
            try:
                next(body)
            except StopIteration:
                bodies.remove(body)


def head_masks():
    first = iota((1, PW), 1) < HD
    return first, (onehot(first), onehot(jnp.logical_not(first)))


def eye_of(n):
    return onehot(iota((n, n), 0) == iota((n, n), 1))


def pair_columns(p):
    return slice(p * PW, (p + 1) * PW)


def forward_kernel(strip, skew, q_ref, k_ref, v_ref, g_ref, att_ref, st_ref):
    length, width = q_ref.shape
    _, in_head = head_masks()
    diag = iota((strip, strip), 0) <= iota((strip, strip), 1)
    eye = eye_of(PW)
    kept = {}

    def score(p, r, h):
        cols, rows = pair_columns(p), slice(r * strip, (r + 1) * strip)
        if r == 0 and h == 0:
            kept["v", p] = nt(eye, v_ref[:, cols]).astype(BF)
            kept["g", p] = nt(eye, g_ref[:, cols])
        q = q_ref[rows, cols] * jnp.asarray(SCALE, BF) * in_head[h]
        kept["s", p, r, h] = nt(k_ref[: (r + 1) * strip, cols], q)

    def soften(p, r, h):
        s = kept.pop(("s", p, r, h))
        last = jnp.where(diag, s[r * strip :], NEG)
        s = jnp.concatenate([s[: r * strip], last], axis=0) if r else last
        top = jnp.max(s, axis=0, keepdims=True)
        w = jnp.exp(s - top)
        kept["w", p, r, h] = w.astype(BF), top, jnp.sum(w, axis=0, keepdims=True)

    def mix(p, r, h):
        cols, rows = pair_columns(p), slice(r * strip, (r + 1) * strip)
        lanes = slice(h * HD, (h + 1) * HD)
        w, top, total = kept.pop(("w", p, r, h))
        out = nn(kept["v", p][lanes, : (r + 1) * strip], w) / total
        kept["o", p, r, h] = out
        st_ref[p * 8 + h : p * 8 + h + 1, rows] = top + jnp.log(total)
        st_ref[p * 8 + 2 + h : p * 8 + 3 + h, rows] = jnp.sum(
            out * kept["g", p][lanes, rows], axis=0, keepdims=True
        )
        if h == 1:
            both = jnp.concatenate([kept.pop(("o", p, r, 0)), kept.pop(("o", p, r, 1))], axis=0)
            att_ref[rows, cols] = both.T.astype(BF)

    for p in range(width // PW):
        st_ref[p * 8 + 4 : p * 8 + 8, :] = jnp.zeros((4, length), F32)
    units = [(p, r, h) for p in range(width // PW) for r in range(length // strip) for h in range(2)]
    staged(units, (score, soften, mix), skew)


def near_valid_queries(shape, n, own):
    row, lane = iota(shape, 0) % n, iota(shape, 1)
    slot, key = lane // n, lane % n
    return ((slot ^ own) < own) | ((slot == 0) & (key <= row))


def near_valid_keys(shape, n, own):
    row, lane = iota(shape, 0) % n, iota(shape, 1)
    slot, query = lane // n, lane % n
    return ((slot ^ own) > own) | ((slot == 0) & (row <= query))


SR = GH // 2 * 8


def stat_row(shape, axis):
    r = iota(shape, axis) % SR
    return r // 8 * 2 + r % 2, r % 8 // 2


def stat_offsets(ref, group):
    head, _ = stat_row((SR, 1), 0)
    out = jnp.zeros((SR, 1), jnp.int32)
    for h in range(GH):
        out = jnp.where(head == h, ref[group * GH + h], out)
    return out


def pieces3(x):
    return jnp.concatenate([piece.astype(BF) for piece in split3(x)], axis=0)


def group_columns(group):
    return slice(group * GW, (group + 1) * GW)


def fetch(sources, targets, sems):
    copies = []
    for i, (source, target) in enumerate(zip(sources, targets)):
        copy = pltpu.make_async_copy(source, target, sems.at[i])
        copy.start()
        copies.append(copy)
    return copies


def merge_group(peers, group, near_ref, far_ref, kv_ref, qg_ref, got, st_ref, att_ref, fr_ref, out_ref, st_out, near_out):
    cols = group_columns(group)
    srows = slice(group * SR, (group + 1) * SR)
    length = att_ref.shape[0]
    n, f = length // R2, length // R3
    own = lax.axis_index("row") % peers
    heads = (kv_ref, *got)
    keys = jnp.concatenate([r[:n, cols] for r in heads], axis=0)
    values = jnp.concatenate([r[n:, cols] for r in heads], axis=0)
    s = nt(expand(qg_ref[:n, cols] * jnp.asarray(SCALE, BF)), keys)
    yield
    st = st_ref[srows, :]
    t = iota((SR, length), 1)
    near_st = t % R2 == stat_offsets(near_ref, group)
    far_st = t % R3 == stat_offsets(far_ref, group)
    sel = near_select(n, length)
    log1 = nt(sel, pieces3(jnp.where(near_st, st, 0.0)))
    near = onehot(iota((length, GW), 0) % R2 == lane_offsets(near_ref, group))
    out1 = nn(sel, att_ref[:, cols] * near)
    yield
    s = jnp.where(near_valid_queries(s.shape, n, own), s, NEG)
    top = jnp.max(s, axis=1, keepdims=True)
    yield
    w = jnp.exp(s - top)
    total = jnp.sum(w, axis=1, keepdims=True)
    out2 = nn(w.astype(BF), values)
    head, what = stat_row((3 * SR, GW), 0)
    lane = iota((3 * SR, GW), 1)
    log1 = nn(log1.astype(BF), onehot((lane // HD == head) & (what == 0)))
    yield
    out2 = collapse(out2 / total)
    log2 = collapse(jnp.broadcast_to(top + jnp.log(total), (GH * n, GW)))
    top = jnp.maximum(log1, log2)
    e1, e2 = jnp.exp(log1 - top), jnp.exp(log2 - top)
    both = e1 + e2
    log12 = top + jnp.log(both)
    out12 = (e1 * out1 + e2 * out2) / both
    near_out[:, cols] = out12.astype(BF)
    dot12 = spread_sum(qg_ref[n:, cols].astype(F32) * out12, GW)
    yield
    aux12 = pack_aux(log12, dot12).astype(BF)
    out_ref[:n, cols] = aux12
    head, what = stat_row((SR, GW), 0)
    lane = iota((SR, GW), 1)
    compact = nt(onehot((lane // HD == head) & (lane % HD // 3 == what)), aux12)
    yield
    place = onehot(iota((n, length), 1) // R2 == iota((n, length), 0))
    placed = nn(pieces3(compact), place)
    yield
    placed = placed[:SR] + placed[SR : 2 * SR] + placed[2 * SR :]
    st = jnp.where(near_st, placed, st)
    st_out[srows, :] = jnp.where(far_st, -NEG, st)
    far_aux = nt(far_select(FM, length, 4 * f), pieces3(jnp.where(far_st, st, 0.0)))
    yield
    head, what = stat_row((3 * SR, GW), 0)
    lane, piece = iota((3 * SR, GW), 1), iota((3 * SR, GW), 0) // SR
    far_aux = nn(far_aux.astype(BF), onehot((lane // HD == head) & (lane % HD == what * 3 + piece)))
    out_ref[n:, cols] = (fr_ref[:, cols].astype(F32) + far_aux).astype(BF)


def merge_kernel(peers, near_ref, far_ref, kv_ref, qg_ref, *rest):
    got, rest = rest[: peers - 1], rest[peers - 1 :]
    groups = kv_ref.shape[1] // GW
    lockstep(merge_group(peers, group, near_ref, far_ref, kv_ref, qg_ref, got, *rest) for group in range(groups))


def backward_kernel(strip, skew, aliased, q_ref, k_ref, v_ref, g_ref, st_ref, *rest):
    dq_ref, dk_ref, dv_ref = rest[aliased:]
    length, width = q_ref.shape
    first, in_head = head_masks()
    diag = iota((strip, strip), 0) <= iota((strip, strip), 1)
    eye = eye_of(PW)
    strips = length // strip
    kept = {}

    def score(p, c, h):
        cols, rows = pair_columns(p), slice(c * strip, (c + 1) * strip)
        if c == 0 and h == 0:
            kept["k", p] = (nt(eye, k_ref[:, cols]) * SCALE).astype(BF)
            kept["q", p] = q_ref[:, cols] * jnp.asarray(SCALE, BF)
        s = nt(k_ref[rows, cols] * in_head[h], kept["q", p][c * strip :])
        dp = nt(v_ref[rows, cols] * in_head[h], g_ref[c * strip :, cols])
        kept["s", p, c, h] = s, dp

    def soften(p, c, h):
        s, dp = kept.pop(("s", p, c, h))
        prob = jnp.exp(s - st_ref[p * 8 + h : p * 8 + h + 1, c * strip :])
        head = jnp.where(diag, prob[:, :strip], 0.0)
        prob = jnp.concatenate([head, prob[:, strip:]], axis=1) if c + 1 < strips else head
        ds = prob * (dp - st_ref[p * 8 + 2 + h : p * 8 + 3 + h, c * strip :])
        kept["p", p, c, h] = prob.astype(BF), ds.astype(BF)

    def mix(p, c, h):
        cols, rows = pair_columns(p), slice(c * strip, (c + 1) * strip)
        prob, ds = kept.pop(("p", p, c, h))
        dv = nn(prob, g_ref[c * strip :, cols])
        dk = nn(ds, kept["q", p][c * strip :])
        part = nn(kept["k", p][h * HD : (h + 1) * HD, rows], ds)
        for r in range(c, strips):
            term = part[:, (r - c) * strip : (r - c + 1) * strip]
            kept["dq", p, r, h] = kept["dq", p, r, h] + term if c else term
        kept["dkv", p, c, h] = dk, dv
        if h == 1:
            one, two = kept.pop(("dkv", p, c, 0)), kept.pop(("dkv", p, c, 1))
            dk_ref[rows, cols] = jnp.where(first, one[0], two[0]).astype(BF)
            dv_ref[rows, cols] = jnp.where(first, one[1], two[1]).astype(BF)
            both = jnp.concatenate([kept.pop(("dq", p, c, 0)), kept.pop(("dq", p, c, 1))], axis=0)
            dq_ref[rows, cols] = both.T.astype(BF)

    units = [(p, c, h) for p in range(width // PW) for c in range(strips) for h in range(2)]
    staged(units, (score, soften, mix), skew)


def far_seq(index, f, peers, masks, own):
    slot = index // f
    seq = own ^ (slot % peers)
    bits = slot // peers
    for at, mask in enumerate(masks):
        seq = seq ^ (((bits >> at) & 1) * mask)
    return seq * f + index % f


def final_group(
    peers, masks, group, near_ref, far_ref, got, auxs, fa_ref, k_ref, v_ref, base, near_out, outs, ready, done
):
    kv_ref, qg_ref, got = got[0], got[1], got[2:]
    cols = group_columns(group)
    length = k_ref.shape[0]
    n, f = length // R2, length // R3
    blocks = fa_ref.shape[0] // FM
    F = blocks * f
    row_here = lax.axis_index("row")
    own = row_here % peers
    seq = lax.axis_index("col") * lax.axis_size("row") + row_here
    scale = jnp.asarray(SCALE, BF)

    ready("far")
    r, c = iota((5 * F, blocks * FM), 0), iota((5 * F, blocks * FM), 1)
    i, at = r // F, r % F
    sel = onehot(c == at // f * FM + i * f + at % f)
    fa = nn(sel, fa_ref[:, cols])
    yield
    fa = fa.astype(BF)
    fq, fk, fv, fg, faux = (fa[i * F : (i + 1) * F] for i in range(5))
    qx, gx, ax = expand(fq * scale), expand(fg), expand(faux)
    s = nt(qx, fk)
    dp = nt(gx, fv)
    log12, dot12 = piece_column(ax, 0), piece_column(ax, 1)
    yield
    ready("near")
    heads = [kv_ref, *got]
    keys = jnp.concatenate([x[:n, cols] for x in heads], axis=0)
    values = jnp.concatenate([x[n:, cols] for x in heads], axis=0)
    heads = [qg_ref, *got]
    queries = jnp.concatenate([x[:n, cols] for x in heads], axis=0) * scale
    grads = jnp.concatenate([x[n:, cols] for x in heads], axis=0)
    near_s = nt(expand(queries[:n]), keys)
    near_dp = nt(expand(grads[:n]), values)
    near_s2 = nt(expand(keys[:n]), queries)
    near_dp2 = nt(expand(values[:n]), grads)
    yield
    place_q = far_seq(iota((GH * F, 1), 0) % F, f, peers, masks, seq)
    place_k = far_seq(iota((1, F), 1), f, peers, masks, seq)
    s = jnp.where(place_k <= place_q, s, NEG)
    top = jnp.max(s, axis=1, keepdims=True)
    yield
    w = jnp.exp(s - top)
    total = jnp.sum(w, axis=1, keepdims=True)
    dot3 = jnp.sum(w * dp, axis=1, keepdims=True)
    yield
    log3 = top + jnp.log(total)
    dot3 = dot3 / total
    top = jnp.maximum(log12, log3)
    e12, e3 = jnp.exp(log12 - top), jnp.exp(log3 - top)
    both = e12 + e3
    log_all = top + jnp.log(both)
    dot_all = (e12 * dot12 + e3 * dot3) / both
    p = jnp.exp(s - log_all)
    ds = p * (dp - dot_all)
    pb, dsb = p.astype(BF), ds.astype(BF)
    yield
    far_dv = tn(pb, gx)[:FM]
    far_dk = tn(dsb, qx)[:FM]
    far_dq = collapse(nn(dsb, fk))[:FM] * SCALE
    far_out = collapse(nn(pb, fv))[:FM]
    keep = collapse(jnp.broadcast_to(e12 / both, (GH * F, GW)))[:FM]
    yield

    def own_rows(x):
        return jnp.concatenate([x[h * F : h * F + FM] for h in range(GH)], axis=0)

    ready("local")
    qx, gx, log_own, dot_own = own_rows(qx), own_rows(gx), own_rows(log_all), own_rows(dot_all)
    k, v = k_ref[:, cols], v_ref[:, cols]
    s = nt(qx, k)
    dp = nt(gx, v)

    rows = peers * n
    final_aux = collapse(
        pack_aux(jnp.broadcast_to(log_all, (GH * F, GW)), jnp.broadcast_to(dot_all, (GH * F, GW)))
    )[:FM].astype(BF)
    r, c = iota((rows, FM), 0), iota((rows, FM), 1)
    subst = nn(onehot(c == r // n * f + r % n * R2 // R3), final_aux)
    yield
    noff, foff = lane_offsets(near_ref, group), lane_offsets(far_ref, group)
    also_far = (iota((rows, GW), 0) % (R3 // R2) == foff // R2) & (foff % R2 == noff)
    naux = jnp.concatenate([a[:n, cols] for a in auxs], axis=0)
    naux = jnp.where(also_far, subst, naux.astype(F32)).astype(BF)
    ax = expand(naux[:n])
    log_q, dot_q = piece_column(ax, 0), piece_column(ax, 1)
    r, c = iota((GH * n, GW), 0), iota((GH * n, GW), 1)
    mine = c // HD == r // n
    log_k = nt(onehot(mine & (c % HD // 3 == 0)), naux)
    dot_k = nt(onehot(mine & (c % HD // 3 == 1)), naux)
    yield
    r = iota((GH * FM, 1), 0)
    reach = jnp.zeros((GH * FM, 1), jnp.int32)
    for h in range(GH):
        reach = jnp.where(r // FM == h, far_ref[group * GH + h], reach)
    reach = jnp.where(r % FM < f, reach + r % FM * R3, -1)
    ok = iota((GH * FM, length), 1) <= reach
    p = jnp.where(ok, jnp.exp(s - log_own), 0.0)
    ds = (p * (dp - dot_own)).astype(BF)
    pb = p.astype(BF)
    yield
    far_dq += collapse(nn(ds, k)) * SCALE
    dk = tn(ds, qx)
    dv = tn(pb, gx)
    yield
    ok = near_valid_queries(near_s.shape, n, own)
    p = jnp.where(ok, jnp.exp(near_s - log_q), 0.0)
    ds = (p * (near_dp - dot_q)).astype(BF)
    ok = near_valid_keys(near_s2.shape, n, own)
    p2 = jnp.where(ok, jnp.exp(near_s2 - log_k), 0.0)
    ds2 = (p2 * (near_dp2 - dot_k)).astype(BF)
    yield
    near_dq = collapse(nn(ds, keys)) * SCALE
    near_dk = collapse(nn(ds2, queries))
    near_dv = collapse(nn(p2.astype(BF), grads))
    yield
    ready("base")
    near, far = token_masks(near_ref, far_ref, group, length)
    place_n, place_f = near_place(n, length), far_place(length)
    att = jnp.where(near, nn(place_n, near_out[:, cols]), base[0][:, cols].astype(F32))
    far_out += keep * nn(far_select(FM, length, 0), att.astype(BF) * onehot(far))
    yield

    def terms(near_part, far_part):
        return jnp.where(near, nn(place_n, near_part.astype(BF)), 0.0) + jnp.where(
            far, nn(place_f, far_part.astype(BF)), 0.0
        )

    outs[1][:, cols] = (base[1][:, cols].astype(F32) + terms(near_dq, far_dq)).astype(BF)
    done(1, cols)
    yield
    outs[2][:, cols] = (base[2][:, cols].astype(F32) + dk + terms(near_dk, far_dk)).astype(BF)
    done(2, cols)
    yield
    outs[3][:, cols] = (base[3][:, cols].astype(F32) + dv + terms(near_dv, far_dv)).astype(BF)
    done(3, cols)
    yield
    outs[0][:, cols] = jnp.where(far, nn(place_f, far_out.astype(BF)), att).astype(BF)
    done(0, cols)


def final_kernel(peers, masks, near_ref, far_ref, *refs):
    count = 1 + (peers + 1) + peers + 2 + 5
    sources, results = refs[:count], refs[count : count + 4]
    scratch = refs[count + 4 :]
    held, outs, sems, out_sems = scratch[:count], scratch[count : count + 4], scratch[-2], scratch[-1]
    copies = fetch(sources, held, sems)
    ends = {"far": (0, 1), "near": (1, 2 + 2 * peers)}
    ends["local"] = (ends["near"][1], ends["near"][1] + 2)
    ends["base"] = (ends["local"][1], count)
    waited = set()

    def ready(what):
        if what not in waited:
            waited.add(what)
            for copy in copies[slice(*ends[what])]:
                copy.wait()

    sent = []

    def done(which, cols):
        copy = pltpu.make_async_copy(
            outs[which].at[:, cols], results[which].at[:, cols], out_sems.at[which, cols.start // GW]
        )
        copy.start()
        sent.append(copy)

    far, near, local = (held[slice(*ends[what])] for what in ("far", "near", "local"))
    base = held[slice(*ends["base"])]
    groups = results[0].shape[1] // GW
    lockstep(
        final_group(
            peers, masks, group, near_ref, far_ref, near[: peers + 1], near[peers + 1 :], far[0], *local,
            base[:4], base[4], outs, ready, done,
        )
        for group in range(groups)
    )
    for copy in sent:
        copy.wait()


def smem():
    return pl.BlockSpec(memory_space=pltpu.SMEM)


def whole_block(rows, width):
    return pl.BlockSpec((rows, width), lambda g: (0, 0))


def group_block(rows):
    return pl.BlockSpec((rows, GW), lambda g: (0, g))


def params(limit=VMEM_LIMIT):
    return pltpu.CompilerParams(vmem_limit_bytes=limit * 1024 * 1024)


def shards(queries, key_vectors, value_vectors, out_grad, near_offsets, far_offsets):
    length, width = queries.shape
    row_count = lax.axis_size("row")
    col_count = lax.axis_size("col")
    peers = SEG2 // length
    n, f = length // R2, length // R3
    groups = width // GW
    pairs = width // PW

    def like(rows):
        return jax.ShapeDtypeStruct((rows, width), BF)

    def swap(x, axis, mask):
        size = lax.axis_size(axis)
        return lax.ppermute(x, axis, [(i, i ^ mask) for i in range(size)])

    picked = pl.pallas_call(
        functools.partial(pick_kernel, peers),
        grid=(groups,),
        in_specs=[smem(), smem()] + [group_block(length)] * 4,
        out_specs=[group_block(2 * n)] * 2 + [group_block(FM)] + [group_block(2 * n)] * (peers - 1),
        out_shape=[like(2 * n)] * 2 + [like(FM)] + [like(2 * n)] * (peers - 1),
        compiler_params=params(PICK_LIMIT),
        name="pick",
    )(near_offsets, far_offsets, queries, key_vectors, value_vectors, out_grad)
    kv, qg, fr, msgs = picked[0], picked[1], picked[2], picked[3:]
    got = [swap(msgs[s - 1], "row", s) for s in range(1, peers)]

    ops = 2 * H * length * length * HD
    stats = jax.ShapeDtypeStruct((pairs * 8, length), F32)
    per = 2

    def pair_block(first):
        return pl.BlockSpec((length, per * PW), lambda p: (0, first + p))

    def stat_block(first):
        return pl.BlockSpec((per * 8, length), lambda p: (first + p, 0))

    att1, st1 = pl.pallas_call(
        functools.partial(forward_kernel, 256, 2),
        grid=(pairs // per,),
        in_specs=[pair_block(0)] * 4,
        out_specs=[pair_block(0), stat_block(0)],
        out_shape=[like(length), stats],
        compiler_params=params(),
        cost_estimate=pl.CostEstimate(flops=2 * ops * 4, bytes_accessed=6 * length * width * 2, transcendentals=0),
        name="forward",
    )(queries, key_vectors, value_vectors, out_grad)

    mine, st12, near_out = pl.pallas_call(
        functools.partial(merge_kernel, peers),
        grid=(1,),
        in_specs=[smem(), smem()]
        + [whole_block(2 * n, width)] * (peers + 1)
        + [whole_block(*stats.shape), whole_block(length, width), whole_block(FM, width)],
        out_specs=[whole_block(n + FM, width), whole_block(*stats.shape), whole_block(n, width)],
        out_shape=[like(n + FM), stats, like(n)],
        compiler_params=params(),
        name="merge",
    )(near_offsets, far_offsets, kv, qg, *got, st1, att1, fr)
    theirs = [swap(mine, "row", s) for s in range(1, peers)]

    grads = []
    pieces = pairs // per

    def backward(piece, grads):
        any_spec = pl.BlockSpec(memory_space=pl.ANY)
        aliased = len(grads)
        return pl.pallas_call(
            functools.partial(backward_kernel, 256, 1, aliased),
            grid=(1,),
            in_specs=[pair_block(piece)] * 4 + [stat_block(piece)] + [any_spec] * aliased,
            out_specs=[pair_block(piece)] * 3,
            out_shape=[like(length)] * 3,
            input_output_aliases={5 + i: i for i in range(aliased)},
            compiler_params=params(),
            cost_estimate=pl.CostEstimate(
                flops=5 * ops * 4 // pieces, bytes_accessed=8 * length * width * 2 // pieces, transcendentals=0
            ),
            name="backward",
        )(queries, key_vectors, value_vectors, out_grad, st12, *grads)

    grads = backward(0, grads)
    grads, theirs = lax.optimization_barrier((grads, theirs))
    at = 1
    far_all = jnp.concatenate([x[n:] for x in (mine, *theirs)], axis=0)
    masks = []
    for axis, size, least in (("row", row_count, peers), ("col", col_count, 1)):
        mask = size // 2
        while mask >= least:
            other = swap(far_all, axis, mask)
            if at < pieces:
                grads = backward(at, grads)
                grads, other = lax.optimization_barrier((grads, other))
                at += 1
            far_all = jnp.concatenate([far_all, other], axis=0)
            masks.append(mask if axis == "row" else mask * row_count)
            mask //= 2
    while at < pieces:
        grads = backward(at, grads)
        at += 1

    operands = (far_all, kv, qg, *got, mine, *theirs, key_vectors, value_vectors, att1, *grads, near_out)
    return pl.pallas_call(
        functools.partial(final_kernel, peers, tuple(masks)),
        in_specs=[smem(), smem()] + [pl.BlockSpec(memory_space=pl.ANY)] * len(operands),
        out_specs=[pl.BlockSpec(memory_space=pl.ANY)] * 4,
        out_shape=[like(length)] * 4,
        scratch_shapes=[pltpu.VMEM(x.shape, x.dtype) for x in operands]
        + [pltpu.VMEM((length, width), BF)] * 4
        + [pltpu.SemaphoreType.DMA((len(operands),)), pltpu.SemaphoreType.DMA((4, groups))],
        compiler_params=params(),
        name="final",
    )(near_offsets, far_offsets, *operands)


def solution(mesh):
    placed = (
        P(("col", "row"), None),
        P(("col", "row"), None),
        P(("col", "row"), None),
        P(("col", "row"), None),
        P(),
        P(),
    )
    return jax.shard_map(
        shards,
        mesh=mesh,
        in_specs=placed,
        out_specs=(
            P(("col", "row"), None),
            P(("col", "row"), None),
            P(("col", "row"), None),
            P(("col", "row"), None),
        ),
        check_vma=False,
    )
```

```python
import functools

import jax
import jax.numpy as jnp
from jax import lax
from jax.experimental import pallas as pl
from jax.experimental.pallas import tpu as pltpu
from jax.sharding import PartitionSpec as P

H = 12
HD = 64
R2 = 16
R3 = 256
S1 = 512
SEG2 = 2048

NEG = -1e30
SCALE = HD**-0.5
GH = 4
GW = GH * HD
PW = 2 * HD
FM = 16
F32 = jnp.float32
BF = jnp.bfloat16
VMEM_LIMIT = 40
PICK_LIMIT = 58


def iota(shape, axis):
    return lax.broadcasted_iota(jnp.int32, shape, axis)


def nn(a, b):
    return lax.dot_general(a, b, (((1,), (0,)), ((), ())), preferred_element_type=F32)


def nt(a, b):
    return lax.dot_general(a, b, (((1,), (1,)), ((), ())), preferred_element_type=F32)


def tn(a, b):
    return lax.dot_general(a, b, (((0,), (0,)), ((), ())), preferred_element_type=F32)


def onehot(cond):
    return jnp.where(cond, 1.0, 0.0).astype(BF)


def lane_offsets(ref, group):
    head = iota((1, GW), 1) // HD
    out = jnp.zeros((1, GW), jnp.int32)
    for h in range(GH):
        out = jnp.where(head == h, ref[group * GH + h], out)
    return out


def expand(x):
    head = iota((1, GW), 1) // HD
    return jnp.concatenate([x * onehot(head == h) for h in range(GH)], axis=0)


def collapse(x):
    n = x.shape[0] // GH
    head = iota((1, GW), 1) // HD
    out = x[:n]
    for h in range(1, GH):
        out = jnp.where(head == h, x[h * n : (h + 1) * n], out)
    return out


def split3(x):
    hi = x.astype(BF)
    rest = x - hi.astype(F32)
    mid = rest.astype(BF)
    low = (rest - mid.astype(F32)).astype(BF)
    return hi.astype(F32), mid.astype(F32), low.astype(F32)


def pack_aux(log_total, row_dot):
    lane = iota((1, log_total.shape[1]), 1) % HD
    out = jnp.zeros(log_total.shape, F32)
    for at, piece in enumerate(split3(log_total) + split3(row_dot)):
        out = jnp.where(lane == at, piece, out)
    return out


def spread_sum(x, width):
    block = onehot(iota((width, width), 0) // HD == iota((width, width), 1) // HD)
    hi = x.astype(BF)
    low = (x - hi.astype(F32)).astype(BF)
    return nn(hi, block) + nn(low, block)


def piece_column(aux_expanded, which):
    a = iota((GW, 128), 0)
    return nn(aux_expanded, onehot(a % HD // 3 == which))[:, :1]


def near_select(n, length):
    return onehot(iota((n, length), 1) // R2 == iota((n, length), 0))


def near_place(n, length):
    return onehot(iota((length, n), 0) // R2 == iota((length, n), 1))


def far_select(rows, length, first):
    return onehot(iota((rows, length), 1) // R3 == iota((rows, length), 0) - first)


def far_place(length):
    return onehot(iota((length, FM), 0) // R3 == iota((length, FM), 1))


def token_masks(near_ref, far_ref, group, length):
    t = iota((length, GW), 0)
    near = t % R2 == lane_offsets(near_ref, group)
    far = t % R3 == lane_offsets(far_ref, group)
    return near, far


def pick_kernel(peers, near_ref, far_ref, q_ref, k_ref, v_ref, g_ref, kv_ref, qg_ref, fr_ref, *msg_refs):
    group = pl.program_id(0)
    length = q_ref.shape[0]
    n, f = length // R2, length // R3
    near, far = token_masks(near_ref, far_ref, group, length)
    near, far = onehot(near), onehot(far)
    sel = near_select(n, length)
    q, k, v, g = q_ref[...], k_ref[...], v_ref[...], g_ref[...]
    picked = [nn(sel, x * near).astype(BF) for x in (k, v, q, g)]
    kv = jnp.concatenate(picked[:2], axis=0)
    qg = jnp.concatenate(picked[2:], axis=0)
    kv_ref[...] = kv
    qg_ref[...] = qg
    fr = jnp.zeros((FM, GW), F32)
    for at, x in enumerate((q, k, v, g)):
        fr += nn(far_select(FM, length, at * f), x * far)
    fr_ref[...] = fr.astype(BF)
    own = lax.axis_index("row") % peers
    for slot in range(1, peers):
        later = (own ^ slot) > own

        @pl.when(later)
        def _(slot=slot):
            msg_refs[slot - 1][...] = kv

        @pl.when(jnp.logical_not(later))
        def _(slot=slot):
            msg_refs[slot - 1][...] = qg


def staged(units, stages, skew):
    for t in range(len(units) + (len(stages) - 1) * skew):
        for i, stage in enumerate(stages):
            if 0 <= t - i * skew < len(units):
                stage(*units[t - i * skew])


def lockstep(bodies):
    bodies = list(bodies)
    while bodies:
        for body in list(bodies):
            try:
                next(body)
            except StopIteration:
                bodies.remove(body)


def head_masks():
    first = iota((1, PW), 1) < HD
    return first, (onehot(first), onehot(jnp.logical_not(first)))


def eye_of(n):
    return onehot(iota((n, n), 0) == iota((n, n), 1))


def pair_columns(p):
    return slice(p * PW, (p + 1) * PW)


def forward_kernel(strip, skew, q_ref, k_ref, v_ref, g_ref, att_ref, st_ref):
    length, width = q_ref.shape
    _, in_head = head_masks()
    diag = iota((strip, strip), 0) <= iota((strip, strip), 1)
    eye = eye_of(PW)
    kept = {}

    def score(p, r, h):
        cols, rows = pair_columns(p), slice(r * strip, (r + 1) * strip)
        if r == 0 and h == 0:
            kept["v", p] = nt(eye, v_ref[:, cols]).astype(BF)
            kept["g", p] = nt(eye, g_ref[:, cols])
        q = q_ref[rows, cols] * jnp.asarray(SCALE, BF) * in_head[h]
        kept["s", p, r, h] = nt(k_ref[: (r + 1) * strip, cols], q)

    def soften(p, r, h):
        s = kept.pop(("s", p, r, h))
        last = jnp.where(diag, s[r * strip :], NEG)
        s = jnp.concatenate([s[: r * strip], last], axis=0) if r else last
        top = jnp.max(s, axis=0, keepdims=True)
        w = jnp.exp(s - top)
        kept["w", p, r, h] = w.astype(BF), top, jnp.sum(w, axis=0, keepdims=True)

    def mix(p, r, h):
        cols, rows = pair_columns(p), slice(r * strip, (r + 1) * strip)
        lanes = slice(h * HD, (h + 1) * HD)
        w, top, total = kept.pop(("w", p, r, h))
        out = nn(kept["v", p][lanes, : (r + 1) * strip], w) / total
        kept["o", p, r, h] = out
        st_ref[p * 8 + h : p * 8 + h + 1, rows] = top + jnp.log(total)
        st_ref[p * 8 + 2 + h : p * 8 + 3 + h, rows] = jnp.sum(
            out * kept["g", p][lanes, rows], axis=0, keepdims=True
        )
        if h == 1:
            both = jnp.concatenate([kept.pop(("o", p, r, 0)), kept.pop(("o", p, r, 1))], axis=0)
            att_ref[rows, cols] = both.T.astype(BF)

    for p in range(width // PW):
        st_ref[p * 8 + 4 : p * 8 + 8, :] = jnp.zeros((4, length), F32)
    units = [(p, r, h) for p in range(width // PW) for r in range(length // strip) for h in range(2)]
    staged(units, (score, soften, mix), skew)


def near_valid_queries(shape, n, own):
    row, lane = iota(shape, 0) % n, iota(shape, 1)
    slot, key = lane // n, lane % n
    return ((slot ^ own) < own) | ((slot == 0) & (key <= row))


def near_valid_keys(shape, n, own):
    row, lane = iota(shape, 0) % n, iota(shape, 1)
    slot, query = lane // n, lane % n
    return ((slot ^ own) > own) | ((slot == 0) & (row <= query))


SR = GH // 2 * 8


def stat_row(shape, axis):
    r = iota(shape, axis) % SR
    return r // 8 * 2 + r % 2, r % 8 // 2


def stat_offsets(ref, group):
    head, _ = stat_row((SR, 1), 0)
    out = jnp.zeros((SR, 1), jnp.int32)
    for h in range(GH):
        out = jnp.where(head == h, ref[group * GH + h], out)
    return out


def pieces3(x):
    return jnp.concatenate([piece.astype(BF) for piece in split3(x)], axis=0)


def group_columns(group):
    return slice(group * GW, (group + 1) * GW)


def pack_lanes(group):
    l, m = iota((GW, 128), 0), iota((GW, 128), 1)
    return onehot((l % HD < 6) & (m == (group * GH + l // HD) * 6 + l % HD))


def unpack_lanes(group):
    l, m = iota((128, GW), 1), iota((128, GW), 0)
    return onehot((l % HD < 6) & (m == (group * GH + l // HD) * 6 + l % HD))


def unpack_rows(peers, stride, n, f, fa_ref):
    per = fa_ref.shape[1] // 128
    rows = peers * stride * FM
    r, c = iota((peers * n, rows), 0), iota((peers * n, rows), 1)
    at_row = c == r // n * (stride * FM) + 5 * f + r % n // per
    out = jnp.zeros((peers * n, 128), F32)
    for at in range(per):
        out += nn(onehot(at_row & (r % n % per == at)), fa_ref[:rows, at * 128 : (at + 1) * 128])
    return out.astype(BF)


def merge_group(peers, group, near_ref, far_ref, kv_ref, qg_ref, got, st_ref, att_ref, fr_ref, out_ref, st_out, near_out, blocks, packs):
    cols = group_columns(group)
    srows = slice(group * SR, (group + 1) * SR)
    length = att_ref.shape[0]
    n, f = length // R2, length // R3
    own = lax.axis_index("row") % peers
    heads = (kv_ref, *got)
    keys = jnp.concatenate([r[:n, cols] for r in heads], axis=0)
    values = jnp.concatenate([r[n:, cols] for r in heads], axis=0)
    s = nt(expand(qg_ref[:n, cols] * jnp.asarray(SCALE, BF)), keys)
    yield
    st = st_ref[srows, :]
    t = iota((SR, length), 1)
    near_st = t % R2 == stat_offsets(near_ref, group)
    far_st = t % R3 == stat_offsets(far_ref, group)
    sel = near_select(n, length)
    log1 = nt(sel, pieces3(jnp.where(near_st, st, 0.0)))
    near = onehot(iota((length, GW), 0) % R2 == lane_offsets(near_ref, group))
    out1 = nn(sel, att_ref[:, cols] * near)
    yield
    s = jnp.where(near_valid_queries(s.shape, n, own), s, NEG)
    top = jnp.max(s, axis=1, keepdims=True)
    yield
    w = jnp.exp(s - top)
    total = jnp.sum(w, axis=1, keepdims=True)
    out2 = nn(w.astype(BF), values)
    head, what = stat_row((3 * SR, GW), 0)
    lane = iota((3 * SR, GW), 1)
    log1 = nn(log1.astype(BF), onehot((lane // HD == head) & (what == 0)))
    yield
    out2 = collapse(out2 / total)
    log2 = collapse(jnp.broadcast_to(top + jnp.log(total), (GH * n, GW)))
    top = jnp.maximum(log1, log2)
    e1, e2 = jnp.exp(log1 - top), jnp.exp(log2 - top)
    both = e1 + e2
    log12 = top + jnp.log(both)
    out12 = (e1 * out1 + e2 * out2) / both
    near_out[:, cols] = out12.astype(BF)
    dot12 = spread_sum(qg_ref[n:, cols].astype(F32) * out12, GW)
    yield
    aux12 = pack_aux(log12, dot12).astype(BF)
    packs.append(nn(aux12, pack_lanes(group)))
    head, what = stat_row((SR, GW), 0)
    lane = iota((SR, GW), 1)
    compact = nt(onehot((lane // HD == head) & (lane % HD // 3 == what)), aux12)
    yield
    place = onehot(iota((n, length), 1) // R2 == iota((n, length), 0))
    placed = nn(pieces3(compact), place)
    yield
    placed = placed[:SR] + placed[SR : 2 * SR] + placed[2 * SR :]
    st = jnp.where(near_st, placed, st)
    st_out[srows, :] = jnp.where(far_st, -NEG, st)
    far_aux = nt(far_select(FM, length, 4 * f), pieces3(jnp.where(far_st, st, 0.0)))
    yield
    head, what = stat_row((3 * SR, GW), 0)
    lane, piece = iota((3 * SR, GW), 1), iota((3 * SR, GW), 0) // SR
    far_aux = nn(far_aux.astype(BF), onehot((lane // HD == head) & (lane % HD == what * 3 + piece)))
    blocks[group] = fr_ref[:, cols].astype(F32) + far_aux


def merge_kernel(peers, near_ref, far_ref, kv_ref, qg_ref, *rest):
    got, rest = rest[: peers - 1], rest[peers - 1 :]
    groups = kv_ref.shape[1] // GW
    out_ref = rest[3]
    blocks, packs = {}, []
    lockstep(
        merge_group(peers, group, near_ref, far_ref, kv_ref, qg_ref, got, *rest, blocks, packs)
        for group in range(groups)
    )
    packed = sum(packs[1:], packs[0]).astype(BF)
    n, length = packed.shape[0], rest[1].shape[0]
    per = out_ref.shape[1] // 128
    r, c = iota((FM, n), 0) - 5 * (length // R3), iota((FM, n), 1)
    for at in range(per):
        block = blocks[at * 128 // GW][:, at * 128 % GW :][:, :128]
        rows = nn(onehot((c // per == r) & (c % per == at)), packed)
        out_ref[:, at * 128 : (at + 1) * 128] = (block + rows).astype(BF)


def backward_kernel(strip, skew, aliased, q_ref, k_ref, v_ref, g_ref, st_ref, *rest):
    dq_ref, dk_ref, dv_ref = rest[aliased:]
    length, width = q_ref.shape
    first, in_head = head_masks()
    diag = iota((strip, strip), 0) <= iota((strip, strip), 1)
    eye = eye_of(PW)
    strips = length // strip
    kept = {}

    def score(p, c, h):
        cols, rows = pair_columns(p), slice(c * strip, (c + 1) * strip)
        if c == 0 and h == 0:
            kept["k", p] = (nt(eye, k_ref[:, cols]) * SCALE).astype(BF)
            kept["q", p] = q_ref[:, cols] * jnp.asarray(SCALE, BF)
        s = nt(k_ref[rows, cols] * in_head[h], kept["q", p][c * strip :])
        dp = nt(v_ref[rows, cols] * in_head[h], g_ref[c * strip :, cols])
        kept["s", p, c, h] = s, dp

    def soften(p, c, h):
        s, dp = kept.pop(("s", p, c, h))
        prob = jnp.exp(s - st_ref[p * 8 + h : p * 8 + h + 1, c * strip :])
        head = jnp.where(diag, prob[:, :strip], 0.0)
        prob = jnp.concatenate([head, prob[:, strip:]], axis=1) if c + 1 < strips else head
        ds = prob * (dp - st_ref[p * 8 + 2 + h : p * 8 + 3 + h, c * strip :])
        kept["p", p, c, h] = prob.astype(BF), ds.astype(BF)

    def mix(p, c, h):
        cols, rows = pair_columns(p), slice(c * strip, (c + 1) * strip)
        prob, ds = kept.pop(("p", p, c, h))
        dv = nn(prob, g_ref[c * strip :, cols])
        dk = nn(ds, kept["q", p][c * strip :])
        part = nn(kept["k", p][h * HD : (h + 1) * HD, rows], ds)
        for r in range(c, strips):
            term = part[:, (r - c) * strip : (r - c + 1) * strip]
            kept["dq", p, r, h] = kept["dq", p, r, h] + term if c else term
        kept["dkv", p, c, h] = dk, dv
        if h == 1:
            one, two = kept.pop(("dkv", p, c, 0)), kept.pop(("dkv", p, c, 1))
            dk_ref[rows, cols] = jnp.where(first, one[0], two[0]).astype(BF)
            dv_ref[rows, cols] = jnp.where(first, one[1], two[1]).astype(BF)
            both = jnp.concatenate([kept.pop(("dq", p, c, 0)), kept.pop(("dq", p, c, 1))], axis=0)
            dq_ref[rows, cols] = both.T.astype(BF)

    units = [(p, c, h) for p in range(width // PW) for c in range(strips) for h in range(2)]
    staged(units, (score, soften, mix), skew)


def far_seq(index, f, digits, own):
    slot = index // f
    seq = own
    for radix, unit in digits:
        seq = seq ^ (slot % radix * unit)
        slot = slot // radix
    return seq * f + index % f


def final_group(
    peers, stride, digits, group, near_ref, far_ref, got, packed, fa_ref, k_ref, v_ref, base, near_out, outs, done
):
    kv_ref, qg_ref, got = got[0], got[1], got[2:]
    cols = group_columns(group)
    length = k_ref.shape[0]
    n, f = length // R2, length // R3
    blocks = fa_ref.shape[0] // FM
    F = blocks * f
    row_here = lax.axis_index("row")
    own = row_here % peers
    seq = lax.axis_index("col") * lax.axis_size("row") + row_here
    scale = jnp.asarray(SCALE, BF)

    r, c = iota((5 * F, blocks * FM), 0), iota((5 * F, blocks * FM), 1)
    i, at = r // F, r % F
    sel = onehot(c == at // f * FM + i * f + at % f)
    fa = nn(sel, fa_ref[:, cols])
    yield
    fa = fa.astype(BF)
    fq, fk, fv, fg, faux = (fa[i * F : (i + 1) * F] for i in range(5))
    qx, gx, ax = expand(fq * scale), expand(fg), expand(faux)
    s = nt(qx, fk)
    dp = nt(gx, fv)
    log12, dot12 = piece_column(ax, 0), piece_column(ax, 1)
    yield
    heads = [kv_ref, *got]
    keys = jnp.concatenate([x[:n, cols] for x in heads], axis=0)
    values = jnp.concatenate([x[n:, cols] for x in heads], axis=0)
    heads = [qg_ref, *got]
    queries = jnp.concatenate([x[:n, cols] for x in heads], axis=0) * scale
    grads = jnp.concatenate([x[n:, cols] for x in heads], axis=0)
    naux = nn(packed(), unpack_lanes(group))
    near_s = nt(expand(queries[:n]), keys)
    near_dp = nt(expand(grads[:n]), values)
    near_s2 = nt(expand(keys[:n]), queries)
    near_dp2 = nt(expand(values[:n]), grads)
    yield
    place_q = far_seq(iota((GH * F, 1), 0) % F, f, digits, seq)
    place_k = far_seq(iota((1, F), 1), f, digits, seq)
    s = jnp.where(place_k <= place_q, s, NEG)
    top = jnp.max(s, axis=1, keepdims=True)
    yield
    w = jnp.exp(s - top)
    total = jnp.sum(w, axis=1, keepdims=True)
    dot3 = jnp.sum(w * dp, axis=1, keepdims=True)
    yield
    log3 = top + jnp.log(total)
    dot3 = dot3 / total
    top = jnp.maximum(log12, log3)
    e12, e3 = jnp.exp(log12 - top), jnp.exp(log3 - top)
    both = e12 + e3
    log_all = top + jnp.log(both)
    dot_all = (e12 * dot12 + e3 * dot3) / both
    p = jnp.exp(s - log_all)
    ds = p * (dp - dot_all)
    pb, dsb = p.astype(BF), ds.astype(BF)
    yield
    far_dv = tn(pb, gx)[:FM]
    far_dk = tn(dsb, qx)[:FM]
    far_dq = collapse(nn(dsb, fk))[:FM] * SCALE
    far_out = collapse(nn(pb, fv))[:FM]
    keep = collapse(jnp.broadcast_to(e12 / both, (GH * F, GW)))[:FM]
    yield

    def own_rows(x):
        return jnp.concatenate([x[h * F : h * F + FM] for h in range(GH)], axis=0)

    qx, gx, log_own, dot_own = own_rows(qx), own_rows(gx), own_rows(log_all), own_rows(dot_all)
    k, v = k_ref[:, cols], v_ref[:, cols]
    s = nt(qx, k)
    dp = nt(gx, v)

    rows = peers * n
    final_aux = collapse(
        pack_aux(jnp.broadcast_to(log_all, (GH * F, GW)), jnp.broadcast_to(dot_all, (GH * F, GW)))
    ).astype(BF)
    r, c = iota((rows, F), 0), iota((rows, F), 1)
    subst = nn(onehot(c == r // n * (stride * f) + r % n * R2 // R3), final_aux)
    yield
    noff, foff = lane_offsets(near_ref, group), lane_offsets(far_ref, group)
    also_far = (iota((rows, GW), 0) % (R3 // R2) == foff // R2) & (foff % R2 == noff)
    naux = jnp.where(also_far, subst, naux).astype(BF)
    ax = expand(naux[:n])
    log_q, dot_q = piece_column(ax, 0), piece_column(ax, 1)
    r, c = iota((GH * n, GW), 0), iota((GH * n, GW), 1)
    mine = c // HD == r // n
    log_k = nt(onehot(mine & (c % HD // 3 == 0)), naux)
    dot_k = nt(onehot(mine & (c % HD // 3 == 1)), naux)
    yield
    r = iota((GH * FM, 1), 0)
    reach = jnp.zeros((GH * FM, 1), jnp.int32)
    for h in range(GH):
        reach = jnp.where(r // FM == h, far_ref[group * GH + h], reach)
    reach = jnp.where(r % FM < f, reach + r % FM * R3, -1)
    ok = iota((GH * FM, length), 1) <= reach
    p = jnp.where(ok, jnp.exp(s - log_own), 0.0)
    ds = (p * (dp - dot_own)).astype(BF)
    pb = p.astype(BF)
    yield
    far_dq += collapse(nn(ds, k)) * SCALE
    dk = tn(ds, qx)
    dv = tn(pb, gx)
    yield
    ok = near_valid_queries(near_s.shape, n, own)
    p = jnp.where(ok, jnp.exp(near_s - log_q), 0.0)
    ds = (p * (near_dp - dot_q)).astype(BF)
    ok = near_valid_keys(near_s2.shape, n, own)
    p2 = jnp.where(ok, jnp.exp(near_s2 - log_k), 0.0)
    ds2 = (p2 * (near_dp2 - dot_k)).astype(BF)
    yield
    near_dq = collapse(nn(ds, keys)) * SCALE
    near_dk = collapse(nn(ds2, queries))
    near_dv = collapse(nn(p2.astype(BF), grads))
    yield
    near, far = token_masks(near_ref, far_ref, group, length)
    place_n, place_f = near_place(n, length), far_place(length)
    att = jnp.where(near, nn(place_n, near_out[:, cols]), base[0][:, cols].astype(F32))
    far_out += keep * nn(far_select(FM, length, 0), att.astype(BF) * onehot(far))
    yield

    def terms(near_part, far_part):
        return jnp.where(near, nn(place_n, near_part.astype(BF)), 0.0) + jnp.where(
            far, nn(place_f, far_part.astype(BF)), 0.0
        )

    outs[1][:, cols] = (base[1][:, cols].astype(F32) + terms(near_dq, far_dq)).astype(BF)
    done(1, cols)
    yield
    outs[2][:, cols] = (base[2][:, cols].astype(F32) + dk + terms(near_dk, far_dk)).astype(BF)
    done(2, cols)
    yield
    outs[3][:, cols] = (base[3][:, cols].astype(F32) + dv + terms(near_dv, far_dv)).astype(BF)
    done(3, cols)
    yield
    outs[0][:, cols] = jnp.where(far, nn(place_f, far_out.astype(BF)), att).astype(BF)
    done(0, cols)


def final_kernel(peers, stride, digits, near_ref, far_ref, *refs):
    near_end = 2 + peers
    count = near_end + 2 + 5
    held, results = refs[:count], refs[count : count + 4]
    outs, out_sems = refs[count + 4 : count + 8], refs[-1]
    length = results[0].shape[0]
    made = []

    def packed():
        if not made:
            made.append(unpack_rows(peers, stride, length // R2, length // R3, held[0]))
        return made[0]

    sent = []

    def done(which, cols):
        copy = pltpu.make_async_copy(
            outs[which].at[:, cols], results[which].at[:, cols], out_sems.at[which, cols.start // GW]
        )
        copy.start()
        sent.append(copy)

    near, local, base = held[1:near_end], held[near_end : near_end + 2], held[near_end + 2 :]
    groups = results[0].shape[1] // GW
    lockstep(
        final_group(
            peers, stride, digits, group, near_ref, far_ref, near, packed, held[0], *local,
            base[:4], base[4], outs, done,
        )
        for group in range(groups)
    )
    for copy in sent:
        copy.wait()


def smem():
    return pl.BlockSpec(memory_space=pltpu.SMEM)


def whole_block(rows, width):
    return pl.BlockSpec((rows, width), lambda g: (0, 0))


def group_block(rows):
    return pl.BlockSpec((rows, GW), lambda g: (0, g))


def params(limit=VMEM_LIMIT):
    return pltpu.CompilerParams(vmem_limit_bytes=limit * 1024 * 1024)


def shards(queries, key_vectors, value_vectors, out_grad, near_offsets, far_offsets):
    length, width = queries.shape
    row_count = lax.axis_size("row")
    col_count = lax.axis_size("col")
    peers = SEG2 // length
    n, f = length // R2, length // R3
    groups = width // GW
    pairs = width // PW

    def like(rows):
        return jax.ShapeDtypeStruct((rows, width), BF)

    def swap(x, axis, mask):
        size = lax.axis_size(axis)
        return lax.ppermute(x, axis, [(i, i ^ mask) for i in range(size)])

    picked = pl.pallas_call(
        functools.partial(pick_kernel, peers),
        grid=(groups,),
        in_specs=[smem(), smem()] + [group_block(length)] * 4,
        out_specs=[group_block(2 * n)] * 2 + [group_block(FM)] + [group_block(2 * n)] * (peers - 1),
        out_shape=[like(2 * n)] * 2 + [like(FM)] + [like(2 * n)] * (peers - 1),
        compiler_params=params(PICK_LIMIT),
        name="pick",
    )(near_offsets, far_offsets, queries, key_vectors, value_vectors, out_grad)
    kv, qg, fr, msgs = picked[0], picked[1], picked[2], picked[3:]
    got = [swap(msgs[s - 1], "row", s) for s in range(1, peers)]

    ops = 2 * H * length * length * HD
    stats = jax.ShapeDtypeStruct((pairs * 8, length), F32)
    per = 2

    def pair_block(first):
        return pl.BlockSpec((length, per * PW), lambda p: (0, first + p))

    def stat_block(first):
        return pl.BlockSpec((per * 8, length), lambda p: (first + p, 0))

    att1, st1 = pl.pallas_call(
        functools.partial(forward_kernel, 256, 2),
        grid=(pairs // per,),
        in_specs=[pair_block(0)] * 4,
        out_specs=[pair_block(0), stat_block(0)],
        out_shape=[like(length), stats],
        compiler_params=params(),
        cost_estimate=pl.CostEstimate(flops=2 * ops * 4, bytes_accessed=6 * length * width * 2, transcendentals=0),
        name="forward",
    )(queries, key_vectors, value_vectors, out_grad)

    mine, st12, near_out = pl.pallas_call(
        functools.partial(merge_kernel, peers),
        grid=(1,),
        in_specs=[smem(), smem()]
        + [whole_block(2 * n, width)] * (peers + 1)
        + [whole_block(*stats.shape), whole_block(length, width), whole_block(FM, width)],
        out_specs=[whole_block(FM, width), whole_block(*stats.shape), whole_block(n, width)],
        out_shape=[like(FM), stats, like(n)],
        compiler_params=params(),
        name="merge",
    )(near_offsets, far_offsets, kv, qg, *got, st1, att1, fr)

    grads = []
    pieces = pairs // per

    def backward(piece, grads):
        any_spec = pl.BlockSpec(memory_space=pl.ANY)
        aliased = len(grads)
        return pl.pallas_call(
            functools.partial(backward_kernel, 256, 1, aliased),
            grid=(1,),
            in_specs=[pair_block(piece)] * 4 + [stat_block(piece)] + [any_spec] * aliased,
            out_specs=[pair_block(piece)] * 3,
            out_shape=[like(length)] * 3,
            input_output_aliases={5 + i: i for i in range(aliased)},
            compiler_params=params(),
            cost_estimate=pl.CostEstimate(
                flops=5 * ops * 4 // pieces, bytes_accessed=8 * length * width * 2 // pieces, transcendentals=0
            ),
            name="backward",
        )(queries, key_vectors, value_vectors, out_grad, st12, *grads)

    def masks_of(size, least):
        mask = size // 2
        while mask >= least:
            yield mask
            mask //= 2

    steps = [("col", [m], 2, m * row_count) for m in masks_of(col_count, 2)]
    steps += [("row", [m], 2, m) for m in masks_of(row_count, peers)]
    stride = 2 ** len(steps)
    steps.append(("row", list(range(1, peers)), peers, 1))
    if col_count > 1:
        steps.append(("col", [1], 2, row_count))
    far_all = mine
    for at, (axis, masks, _, _) in enumerate(steps):
        others = [swap(far_all, axis, mask) for mask in masks]
        if at < pieces:
            grads = backward(at, grads)
            grads, others = lax.optimization_barrier((grads, others))
        far_all = jnp.concatenate([far_all, *others], axis=0)
    for at in range(len(steps), pieces):
        grads = backward(at, grads)
    digits = tuple((radix, unit) for _, _, radix, unit in steps)

    operands = (far_all, kv, qg, *got, key_vectors, value_vectors, att1, *grads, near_out)
    return pl.pallas_call(
        functools.partial(final_kernel, peers, stride, digits),
        in_specs=[smem(), smem()] + [pl.BlockSpec(memory_space=pltpu.VMEM)] * len(operands),
        out_specs=[pl.BlockSpec(memory_space=pl.ANY)] * 4,
        out_shape=[like(length)] * 4,
        scratch_shapes=[pltpu.VMEM((length, width), BF)] * 4 + [pltpu.SemaphoreType.DMA((4, groups))],
        compiler_params=params(),
        name="final",
    )(near_offsets, far_offsets, *operands)


def solution(mesh):
    placed = (
        P(("col", "row"), None),
        P(("col", "row"), None),
        P(("col", "row"), None),
        P(("col", "row"), None),
        P(),
        P(),
    )
    return jax.shard_map(
        shards,
        mesh=mesh,
        in_specs=placed,
        out_specs=(
            P(("col", "row"), None),
            P(("col", "row"), None),
            P(("col", "row"), None),
            P(("col", "row"), None),
        ),
        check_vma=False,
    )
```

```python
import functools

import jax
import jax.numpy as jnp
from jax import lax
from jax.experimental import pallas as pl
from jax.experimental.pallas import tpu as pltpu
from jax.sharding import PartitionSpec as P

H = 12
HD = 64
R2 = 16
R3 = 256
S1 = 512
SEG2 = 2048

NEG = -1e30
SCALE = HD**-0.5
GH = 4
GW = GH * HD
PW = 2 * HD
FM = 16
F32 = jnp.float32
BF = jnp.bfloat16
VMEM_LIMIT = 40
PICK_LIMIT = 58


def iota(shape, axis):
    return lax.broadcasted_iota(jnp.int32, shape, axis)


def nn(a, b):
    return lax.dot_general(a, b, (((1,), (0,)), ((), ())), preferred_element_type=F32)


def nt(a, b):
    return lax.dot_general(a, b, (((1,), (1,)), ((), ())), preferred_element_type=F32)


def tn(a, b):
    return lax.dot_general(a, b, (((0,), (0,)), ((), ())), preferred_element_type=F32)


def onehot(cond):
    return jnp.where(cond, 1.0, 0.0).astype(BF)


def lane_offsets(ref, group):
    head = iota((1, GW), 1) // HD
    out = jnp.zeros((1, GW), jnp.int32)
    for h in range(GH):
        out = jnp.where(head == h, ref[group * GH + h], out)
    return out


def expand(x):
    head = iota((1, GW), 1) // HD
    return jnp.concatenate([x * onehot(head == h) for h in range(GH)], axis=0)


def collapse(x):
    n = x.shape[0] // GH
    head = iota((1, GW), 1) // HD
    out = x[:n]
    for h in range(1, GH):
        out = jnp.where(head == h, x[h * n : (h + 1) * n], out)
    return out


def split3(x):
    hi = x.astype(BF)
    rest = x - hi.astype(F32)
    mid = rest.astype(BF)
    low = (rest - mid.astype(F32)).astype(BF)
    return hi.astype(F32), mid.astype(F32), low.astype(F32)


def pack_aux(log_total, row_dot):
    lane = iota((1, log_total.shape[1]), 1) % HD
    out = jnp.zeros(log_total.shape, F32)
    for at, piece in enumerate(split3(log_total) + split3(row_dot)):
        out = jnp.where(lane == at, piece, out)
    return out


def spread_sum(x, width):
    block = onehot(iota((width, width), 0) // HD == iota((width, width), 1) // HD)
    hi = x.astype(BF)
    low = (x - hi.astype(F32)).astype(BF)
    return nn(hi, block) + nn(low, block)


def piece_column(aux_expanded, which):
    a = iota((GW, 128), 0)
    return nn(aux_expanded, onehot(a % HD // 3 == which))[:, :1]


def near_select(n, length):
    return onehot(iota((n, length), 1) // R2 == iota((n, length), 0))


def near_place(n, length):
    return onehot(iota((length, n), 0) // R2 == iota((length, n), 1))


def far_select(rows, length, first):
    return onehot(iota((rows, length), 1) // R3 == iota((rows, length), 0) - first)


def far_place(length):
    return onehot(iota((length, FM), 0) // R3 == iota((length, FM), 1))


def token_masks(near_ref, far_ref, group, length):
    t = iota((length, GW), 0)
    near = t % R2 == lane_offsets(near_ref, group)
    far = t % R3 == lane_offsets(far_ref, group)
    return near, far


class HeadOffsets:
    def __init__(self, block, row, group):
        self.lanes = block[row : row + 1].astype(jnp.int32)
        self.first = group * GH

    def __getitem__(self, head):
        at = (head - self.first) * HD
        return self.lanes[:, at : at + 1]


def read_offsets(fr_ref, f, group):
    block = fr_ref[:, group_columns(group)].astype(F32)
    return HeadOffsets(block, 5 * f, group), HeadOffsets(block, 5 * f + 1, group)


def head_rows(n, stride, length, ref, group):
    r = iota((GH * n, 1), 0)
    token = r % n * stride
    for h in range(GH):
        token = jnp.where(r // n == h, token + ref[group * GH + h], token)
    return onehot(iota((GH * n, length), 1) == token)


def pick_kernel(peers, near_ref, far_ref, q_ref, k_ref, v_ref, g_ref, kv_ref, qg_ref, fr_ref, *msg_refs):
    group = pl.program_id(0)
    length = q_ref.shape[0]
    n, f = length // R2, length // R3
    sel = jnp.concatenate(
        [head_rows(n, R2, length, near_ref, group), head_rows(8, R3, length, far_ref, group)], axis=0
    )
    picked, far = [], []
    for ref in (q_ref, k_ref, v_ref, g_ref):
        rows = nn(sel, ref[...])
        picked.append(collapse(rows[: GH * n]).astype(BF))
        far.append(collapse(rows[GH * n :])[:f])
    offsets = [lane_offsets(ref, group).astype(F32) for ref in (near_ref, far_ref)]
    far += [jnp.zeros((f, GW), F32), *offsets, jnp.zeros((FM - 5 * f - 2, GW), F32)]
    fr_ref[...] = jnp.concatenate(far, axis=0).astype(BF)
    q, k, v, g = picked
    kv = jnp.concatenate([k, v], axis=0)
    qg = jnp.concatenate([q, g], axis=0)
    kv_ref[...] = kv
    qg_ref[...] = qg
    own = lax.axis_index("row") % peers
    for slot in range(1, peers):
        later = (own ^ slot) > own

        @pl.when(later)
        def _(slot=slot):
            msg_refs[slot - 1][...] = kv

        @pl.when(jnp.logical_not(later))
        def _(slot=slot):
            msg_refs[slot - 1][...] = qg


def staged(units, stages, skew):
    for t in range(len(units) + (len(stages) - 1) * skew):
        for i, stage in enumerate(stages):
            if 0 <= t - i * skew < len(units):
                stage(*units[t - i * skew])


def lockstep(bodies):
    bodies = list(bodies)
    while bodies:
        for body in list(bodies):
            try:
                next(body)
            except StopIteration:
                bodies.remove(body)


def head_masks():
    first = iota((1, PW), 1) < HD
    return first, (onehot(first), onehot(jnp.logical_not(first)))


def eye_of(n):
    return onehot(iota((n, n), 0) == iota((n, n), 1))


def pair_columns(p):
    return slice(p * PW, (p + 1) * PW)


def forward_kernel(strip, skew, q_ref, k_ref, v_ref, g_ref, att_ref, st_ref):
    length, width = q_ref.shape
    _, in_head = head_masks()
    diag = iota((strip, strip), 0) <= iota((strip, strip), 1)
    eye = eye_of(PW)
    kept = {}

    def score(p, r, h):
        cols, rows = pair_columns(p), slice(r * strip, (r + 1) * strip)
        if r == 0 and h == 0:
            kept["v", p] = nt(eye, v_ref[:, cols]).astype(BF)
            kept["g", p] = nt(eye, g_ref[:, cols])
        q = q_ref[rows, cols] * jnp.asarray(SCALE, BF) * in_head[h]
        kept["s", p, r, h] = nt(k_ref[: (r + 1) * strip, cols], q)

    def soften(p, r, h):
        s = kept.pop(("s", p, r, h))
        last = jnp.where(diag, s[r * strip :], NEG)
        s = jnp.concatenate([s[: r * strip], last], axis=0) if r else last
        top = jnp.max(s, axis=0, keepdims=True)
        w = jnp.exp(s - top)
        kept["w", p, r, h] = w.astype(BF), top, jnp.sum(w, axis=0, keepdims=True)

    def mix(p, r, h):
        cols, rows = pair_columns(p), slice(r * strip, (r + 1) * strip)
        lanes = slice(h * HD, (h + 1) * HD)
        w, top, total = kept.pop(("w", p, r, h))
        out = nn(kept["v", p][lanes, : (r + 1) * strip], w) / total
        kept["o", p, r, h] = out
        st_ref[p * 8 + h : p * 8 + h + 1, rows] = top + jnp.log(total)
        st_ref[p * 8 + 2 + h : p * 8 + 3 + h, rows] = jnp.sum(
            out * kept["g", p][lanes, rows], axis=0, keepdims=True
        )
        if h == 1:
            both = jnp.concatenate([kept.pop(("o", p, r, 0)), kept.pop(("o", p, r, 1))], axis=0)
            att_ref[rows, cols] = both.T.astype(BF)

    for p in range(width // PW):
        st_ref[p * 8 + 4 : p * 8 + 8, :] = jnp.zeros((4, length), F32)
    units = [(p, r, h) for p in range(width // PW) for r in range(length // strip) for h in range(2)]
    staged(units, (score, soften, mix), skew)


def near_valid_queries(shape, n, own):
    row, lane = iota(shape, 0) % n, iota(shape, 1)
    slot, key = lane // n, lane % n
    return ((slot ^ own) < own) | ((slot == 0) & (key <= row))


def near_valid_keys(shape, n, own):
    row, lane = iota(shape, 0) % n, iota(shape, 1)
    slot, query = lane // n, lane % n
    return ((slot ^ own) > own) | ((slot == 0) & (row <= query))


SR = GH // 2 * 8


def stat_row(shape, axis):
    r = iota(shape, axis) % SR
    return r // 8 * 2 + r % 2, r % 8 // 2


def stat_offsets(ref, group):
    head, _ = stat_row((SR, 1), 0)
    out = jnp.zeros((SR, 1), jnp.int32)
    for h in range(GH):
        out = jnp.where(head == h, ref[group * GH + h], out)
    return out


def pieces3(x):
    return jnp.concatenate([piece.astype(BF) for piece in split3(x)], axis=0)


def group_columns(group):
    return slice(group * GW, (group + 1) * GW)


def pack_lanes(group):
    l, m = iota((GW, 128), 0), iota((GW, 128), 1)
    return onehot((l % HD < 6) & (m == (group * GH + l // HD) * 6 + l % HD))


def unpack_lanes(group):
    l, m = iota((128, GW), 1), iota((128, GW), 0)
    return onehot((l % HD < 6) & (m == (group * GH + l // HD) * 6 + l % HD))


def unpack_rows(peers, stride, n, f, fa_ref):
    per = fa_ref.shape[1] // 128
    rows = peers * stride * FM
    r, c = iota((peers * n, rows), 0), iota((peers * n, rows), 1)
    at_row = c == r // n * (stride * FM) + 5 * f + r % n // per
    out = jnp.zeros((peers * n, 128), F32)
    for at in range(per):
        out += nn(onehot(at_row & (r % n % per == at)), fa_ref[:rows, at * 128 : (at + 1) * 128])
    return out.astype(BF)


def merge_group(peers, group, kv_ref, qg_ref, got, st_ref, att_ref, fr_ref, out_ref, st_out, near_out, blocks, packs):
    cols = group_columns(group)
    srows = slice(group * SR, (group + 1) * SR)
    length = att_ref.shape[0]
    n, f = length // R2, length // R3
    near_ref, far_ref = read_offsets(fr_ref, f, group)
    own = lax.axis_index("row") % peers
    heads = (kv_ref, *got)
    keys = jnp.concatenate([r[:n, cols] for r in heads], axis=0)
    values = jnp.concatenate([r[n:, cols] for r in heads], axis=0)
    s = nt(expand(qg_ref[:n, cols] * jnp.asarray(SCALE, BF)), keys)
    yield
    st = st_ref[srows, :]
    t = iota((SR, length), 1)
    near_st = t % R2 == stat_offsets(near_ref, group)
    far_st = t % R3 == stat_offsets(far_ref, group)
    sel = near_select(n, length)
    log1 = nt(sel, pieces3(jnp.where(near_st, st, 0.0)))
    out1 = collapse(nn(head_rows(n, R2, length, near_ref, group), att_ref[:, cols]))
    yield
    s = jnp.where(near_valid_queries(s.shape, n, own), s, NEG)
    top = jnp.max(s, axis=1, keepdims=True)
    yield
    w = jnp.exp(s - top)
    total = jnp.sum(w, axis=1, keepdims=True)
    out2 = nn(w.astype(BF), values)
    head, what = stat_row((3 * SR, GW), 0)
    lane = iota((3 * SR, GW), 1)
    log1 = nn(log1.astype(BF), onehot((lane // HD == head) & (what == 0)))
    yield
    out2 = collapse(out2 / total)
    log2 = collapse(jnp.broadcast_to(top + jnp.log(total), (GH * n, GW)))
    top = jnp.maximum(log1, log2)
    e1, e2 = jnp.exp(log1 - top), jnp.exp(log2 - top)
    both = e1 + e2
    log12 = top + jnp.log(both)
    out12 = (e1 * out1 + e2 * out2) / both
    near_out[:, cols] = out12.astype(BF)
    dot12 = spread_sum(qg_ref[n:, cols].astype(F32) * out12, GW)
    yield
    aux12 = pack_aux(log12, dot12).astype(BF)
    packs.append(nn(aux12, pack_lanes(group)))
    head, what = stat_row((SR, GW), 0)
    lane = iota((SR, GW), 1)
    compact = nt(onehot((lane // HD == head) & (lane % HD // 3 == what)), aux12)
    yield
    place = onehot(iota((n, length), 1) // R2 == iota((n, length), 0))
    placed = nn(pieces3(compact), place)
    yield
    placed = placed[:SR] + placed[SR : 2 * SR] + placed[2 * SR :]
    st = jnp.where(near_st, placed, st)
    st_out[srows, :] = jnp.where(far_st, -NEG, st)
    far_aux = nt(far_select(FM, length, 4 * f), pieces3(jnp.where(far_st, st, 0.0)))
    yield
    head, what = stat_row((3 * SR, GW), 0)
    lane, piece = iota((3 * SR, GW), 1), iota((3 * SR, GW), 0) // SR
    far_aux = nn(far_aux.astype(BF), onehot((lane // HD == head) & (lane % HD == what * 3 + piece)))
    raw = fr_ref[:, cols].astype(F32)
    blocks[group] = jnp.where(iota(raw.shape, 0) < 4 * f, raw, 0.0) + far_aux


def merge_kernel(peers, kv_ref, qg_ref, *rest):
    got, rest = rest[: peers - 1], rest[peers - 1 :]
    groups = kv_ref.shape[1] // GW
    out_ref = rest[3]
    blocks, packs = {}, []
    lockstep(
        merge_group(peers, group, kv_ref, qg_ref, got, *rest, blocks, packs)
        for group in range(groups)
    )
    packed = sum(packs[1:], packs[0]).astype(BF)
    n, length = packed.shape[0], rest[1].shape[0]
    per = out_ref.shape[1] // 128
    r, c = iota((FM, n), 0) - 5 * (length // R3), iota((FM, n), 1)
    for at in range(per):
        block = blocks[at * 128 // GW][:, at * 128 % GW :][:, :128]
        rows = nn(onehot((c // per == r) & (c % per == at)), packed)
        out_ref[:, at * 128 : (at + 1) * 128] = (block + rows).astype(BF)


def backward_kernel(strip, skew, span, aliased, q_ref, k_ref, v_ref, g_ref, st_ref, *rest):
    dq_ref, dk_ref, dv_ref = rest[aliased:]
    length = q_ref.shape[0]
    first, in_head = head_masks()
    diag = iota((strip, strip), 0) <= iota((strip, strip), 1)
    eye = eye_of(PW)
    strips = length // strip
    kept = {}

    def score(p, c, h):
        cols, rows = pair_columns(p), slice(c * strip, (c + 1) * strip)
        if c == 0 and h == 0:
            kept["k", p] = (nt(eye, k_ref[:, cols]) * SCALE).astype(BF)
            kept["q", p] = q_ref[:, cols] * jnp.asarray(SCALE, BF)
        s = nt(k_ref[rows, cols] * in_head[h], kept["q", p][c * strip :])
        dp = nt(v_ref[rows, cols] * in_head[h], g_ref[c * strip :, cols])
        kept["s", p, c, h] = s, dp

    def soften(p, c, h):
        s, dp = kept.pop(("s", p, c, h))
        prob = jnp.exp(s - st_ref[p * 8 + h : p * 8 + h + 1, c * strip :])
        head = jnp.where(diag, prob[:, :strip], 0.0)
        prob = jnp.concatenate([head, prob[:, strip:]], axis=1) if c + 1 < strips else head
        ds = prob * (dp - st_ref[p * 8 + 2 + h : p * 8 + 3 + h, c * strip :])
        kept["p", p, c, h] = prob.astype(BF), ds.astype(BF)

    def mix(p, c, h):
        cols, rows = pair_columns(p), slice(c * strip, (c + 1) * strip)
        prob, ds = kept.pop(("p", p, c, h))
        dv = nn(prob, g_ref[c * strip :, cols])
        dk = nn(ds, kept["q", p][c * strip :])
        part = nn(kept["k", p][h * HD : (h + 1) * HD, rows], ds)
        for r in range(c, strips):
            term = part[:, (r - c) * strip : (r - c + 1) * strip]
            kept["dq", p, r, h] = kept["dq", p, r, h] + term if c else term
        kept["dkv", p, c, h] = dk, dv
        if h == 1:
            one, two = kept.pop(("dkv", p, c, 0)), kept.pop(("dkv", p, c, 1))
            dk_ref[rows, cols] = jnp.where(first, one[0], two[0]).astype(BF)
            dv_ref[rows, cols] = jnp.where(first, one[1], two[1]).astype(BF)
            both = jnp.concatenate([kept.pop(("dq", p, c, 0)), kept.pop(("dq", p, c, 1))], axis=0)
            dq_ref[rows, cols] = both.T.astype(BF)

    units = [(p, c, h) for p in span for c in range(strips) for h in range(2)]
    staged(units, (score, soften, mix), skew)


def far_seq(index, f, digits, own):
    slot = index // f
    seq = own
    for radix, unit in digits:
        seq = seq ^ (slot % radix * unit)
        slot = slot // radix
    return seq * f + index % f


def row_offsets(n, ref, group):
    r = iota((GH * n, 1), 0)
    out = jnp.zeros((GH * n, 1), jnp.int32)
    for h in range(GH):
        out = jnp.where(r // n == h, ref[group * GH + h], out)
    return out


def place_columns(n, length, near_ref, far_ref, group):
    parts = []
    for count, stride, ref in ((n, R2, near_ref), (FM, R3, far_ref)):
        c = iota((1, GH * count), 1)
        token = c % count * stride
        for h in range(GH):
            token = jnp.where(c // count == h, token + ref[group * GH + h], token)
        parts.append(token)
    return onehot(iota((length, GH * (n + FM)), 0) == jnp.concatenate(parts, axis=1))


def own_lanes(x):
    n = x.shape[0] // GH
    return jnp.where(iota(x.shape, 1) // HD == iota(x.shape, 0) // n, x, 0.0)


def piece_columns(aux_expanded):
    a, c = iota((GW, 256), 0), iota((GW, 256), 1)
    both = nn(aux_expanded, onehot(a % HD // 3 == c // 128))
    return both[:, :1], both[:, 128:129]


def final_group(
    peers, stride, digits, group, fr_ref, got, packed, fa_ref, k_ref, v_ref, base, near_out, outs, done
):
    kv_ref, qg_ref, got = got[0], got[1], got[2:]
    cols = group_columns(group)
    length = k_ref.shape[0]
    n, f = length // R2, length // R3
    near_ref, far_ref = read_offsets(fr_ref, f, group)
    blocks = fa_ref.shape[0] // FM
    F = blocks * f
    row_here = lax.axis_index("row")
    own = row_here % peers
    seq = lax.axis_index("col") * lax.axis_size("row") + row_here
    scale = jnp.asarray(SCALE, BF)

    r, c = iota((5 * F, blocks * FM), 0), iota((5 * F, blocks * FM), 1)
    i, at = r // F, r % F
    sel = onehot(c == at // f * FM + i * f + at % f)
    fa = nn(sel, fa_ref[:, cols])
    yield
    fa = fa.astype(BF)
    fq, fk, fv, fg, faux = (fa[i * F : (i + 1) * F] for i in range(5))
    qx, gx, ax = expand(fq * scale), expand(fg), expand(faux)
    s = nt(qx, fk)
    dp = nt(gx, fv)
    log12, dot12 = piece_columns(ax)
    yield
    heads = [kv_ref, *got]
    keys = jnp.concatenate([x[:n, cols] for x in heads], axis=0)
    values = jnp.concatenate([x[n:, cols] for x in heads], axis=0)
    heads = [qg_ref, *got]
    queries = jnp.concatenate([x[:n, cols] for x in heads], axis=0) * scale
    grads = jnp.concatenate([x[n:, cols] for x in heads], axis=0)
    naux = nn(packed(), unpack_lanes(group))
    near_s = nt(expand(queries[:n]), keys)
    near_dp = nt(expand(grads[:n]), values)
    near_s2 = nt(expand(keys[:n]), queries)
    near_dp2 = nt(expand(values[:n]), grads)
    place_q = far_seq(iota((GH * F, 1), 0) % F, f, digits, seq)
    place_k = far_seq(iota((1, F), 1), f, digits, seq)
    s = jnp.where(place_k <= place_q, s, NEG)
    top = jnp.max(s, axis=1, keepdims=True)
    yield
    w = jnp.exp(s - top)
    total = jnp.sum(w, axis=1, keepdims=True)
    dot3 = jnp.sum(w * dp, axis=1, keepdims=True)
    k, v = k_ref[:, cols], v_ref[:, cols]

    def own_rows(x):
        return jnp.concatenate([x[h * F : h * F + FM] for h in range(GH)], axis=0)

    qo, go = own_rows(qx), own_rows(gx)
    local_s = nt(qo, k)
    local_dp = nt(go, v)
    roff, rnear = row_offsets(FM, far_ref, group), row_offsets(FM, near_ref, group)
    token = iota((GH * FM, 1), 0) % FM * R3 + roff
    att_far = nn(onehot(iota((GH * FM, length), 1) == token), base[0][:, cols])
    near_far = nn(onehot(iota((GH * FM, n), 1) * R2 + rnear == token), near_out[:, cols])
    att_far = jnp.where(roff % R2 == rnear, near_far, att_far)
    yield
    log3 = top + jnp.log(total)
    dot3 = dot3 / total
    top = jnp.maximum(log12, log3)
    e12, e3 = jnp.exp(log12 - top), jnp.exp(log3 - top)
    both = e12 + e3
    log_all = top + jnp.log(both)
    dot_all = (e12 * dot12 + e3 * dot3) / both
    p = jnp.exp(s - log_all)
    ds = p * (dp - dot_all)
    pb, dsb = p.astype(BF), ds.astype(BF)
    log_own, dot_own, keep = own_rows(log_all), own_rows(dot_all), own_rows(e12 / both)
    yield
    final_aux = collapse(
        pack_aux(jnp.broadcast_to(log_all, (GH * F, GW)), jnp.broadcast_to(dot_all, (GH * F, GW)))
    ).astype(BF)
    rows = peers * n
    r, c = iota((rows, F), 0), iota((rows, F), 1)
    subst = nn(onehot(c == r // n * (stride * f) + r % n * R2 // R3), final_aux)
    far_out = own_lanes(nn(own_rows(pb), fv) + keep * att_far)
    far_dq = nn(own_rows(dsb), fk)
    far_dv = tn(pb, gx)[:FM]
    far_dk = tn(dsb, qx)[:FM]
    yield
    r = iota((GH * FM, 1), 0)
    reach = jnp.where(r % FM < f, token, -1)
    ok = iota((GH * FM, length), 1) <= reach
    p = jnp.where(ok, jnp.exp(local_s - log_own), 0.0)
    ds = (p * (local_dp - dot_own)).astype(BF)
    pb = p.astype(BF)
    noff, foff = lane_offsets(near_ref, group), lane_offsets(far_ref, group)
    also_far = (iota((rows, GW), 0) % (R3 // R2) == foff // R2) & (foff % R2 == noff)
    naux = jnp.where(also_far, subst, naux).astype(BF)
    yield
    log_q, dot_q = piece_columns(expand(naux[:n]))
    r, c = iota((2 * GH * n, GW), 0), iota((2 * GH * n, GW), 1)
    head, which = r % (GH * n) // n, r // (GH * n)
    stats = nt(onehot((c // HD == head) & (c % HD // 3 == which)), naux)
    log_k, dot_k = stats[: GH * n], stats[GH * n :]
    far_dq = own_lanes(far_dq + nn(ds, k))
    place = place_columns(n, length, near_ref, far_ref, group)
    alone = jnp.where(also_far[:n], 0.0, near_out[:, cols].astype(F32)).astype(BF)
    placed = nn(place, jnp.concatenate([expand(alone), far_out.astype(BF)], axis=0))
    yield
    near, far = token_masks(near_ref, far_ref, group, length)
    outs[0][:, cols] = jnp.where(near | far, placed, base[0][:, cols].astype(F32)).astype(BF)
    done(0, cols)
    yield
    ok = near_valid_queries(near_s.shape, n, own)
    np = jnp.where(ok, jnp.exp(near_s - log_q), 0.0)
    nds = (np * (near_dp - dot_q)).astype(BF)
    ok = near_valid_keys(near_s2.shape, n, own)
    np2 = jnp.where(ok, jnp.exp(near_s2 - log_k), 0.0)
    nds2 = (np2 * (near_dp2 - dot_k)).astype(BF)
    dk = tn(ds, qo)
    dv = tn(pb, go)
    yield
    near_dq = own_lanes(nn(nds, keys))
    near_dk = own_lanes(nn(nds2, queries))
    near_dv = own_lanes(nn(np2.astype(BF), grads))
    yield
    terms = nn(place, (jnp.concatenate([near_dq, far_dq], axis=0) * SCALE).astype(BF))
    outs[1][:, cols] = (base[1][:, cols].astype(F32) + terms).astype(BF)
    done(1, cols)
    yield
    terms = dk + nn(place, jnp.concatenate([near_dk.astype(BF), expand(far_dk.astype(BF))], axis=0))
    outs[2][:, cols] = (base[2][:, cols].astype(F32) + terms).astype(BF)
    done(2, cols)
    yield
    terms = dv + nn(place, jnp.concatenate([near_dv.astype(BF), expand(far_dv.astype(BF))], axis=0))
    outs[3][:, cols] = (base[3][:, cols].astype(F32) + terms).astype(BF)
    done(3, cols)


def final_kernel(peers, stride, digits, fr_ref, *refs):
    near_end = 2 + peers
    count = near_end + 2 + 5
    held, results = refs[:count], refs[count : count + 4]
    outs, out_sems = refs[count + 4 : count + 8], refs[-1]
    length = results[0].shape[0]
    made = []

    def packed():
        if not made:
            made.append(unpack_rows(peers, stride, length // R2, length // R3, held[0]))
        return made[0]

    sent = []

    def done(which, cols):
        copy = pltpu.make_async_copy(
            outs[which].at[:, cols], results[which].at[:, cols], out_sems.at[which, cols.start // GW]
        )
        copy.start()
        sent.append(copy)

    near, local, base = held[1:near_end], held[near_end : near_end + 2], held[near_end + 2 :]
    groups = results[0].shape[1] // GW
    lockstep(
        final_group(
            peers, stride, digits, group, fr_ref, near, packed, held[0], *local,
            base[:4], base[4], outs, done,
        )
        for group in range(groups)
    )
    for copy in sent:
        copy.wait()


def smem():
    return pl.BlockSpec(memory_space=pltpu.SMEM)


def whole_block(rows, width):
    return pl.BlockSpec((rows, width), lambda g: (0, 0))


def group_block(rows):
    return pl.BlockSpec((rows, GW), lambda g: (0, g))


def params(limit=VMEM_LIMIT):
    return pltpu.CompilerParams(vmem_limit_bytes=limit * 1024 * 1024)


def shards(queries, key_vectors, value_vectors, out_grad, near_offsets, far_offsets):
    length, width = queries.shape
    row_count = lax.axis_size("row")
    col_count = lax.axis_size("col")
    peers = SEG2 // length
    n, f = length // R2, length // R3
    groups = width // GW
    pairs = width // PW

    def like(rows):
        return jax.ShapeDtypeStruct((rows, width), BF)

    def swap(x, axis, mask):
        size = lax.axis_size(axis)
        return lax.ppermute(x, axis, [(i, i ^ mask) for i in range(size)])

    picked = pl.pallas_call(
        functools.partial(pick_kernel, peers),
        grid=(groups,),
        in_specs=[smem(), smem()] + [group_block(length)] * 4,
        out_specs=[group_block(2 * n)] * 2 + [group_block(FM)] + [group_block(2 * n)] * (peers - 1),
        out_shape=[like(2 * n)] * 2 + [like(FM)] + [like(2 * n)] * (peers - 1),
        compiler_params=params(PICK_LIMIT),
        name="pick",
    )(near_offsets, far_offsets, queries, key_vectors, value_vectors, out_grad)
    kv, qg, fr, msgs = picked[0], picked[1], picked[2], picked[3:]
    got = [swap(msgs[s - 1], "row", s) for s in range(1, peers)]

    ops = 2 * H * length * length * HD
    stats = jax.ShapeDtypeStruct((pairs * 8, length), F32)
    per = 2

    vmem_spec = pl.BlockSpec(memory_space=pltpu.VMEM)

    def pair_block(first):
        return pl.BlockSpec((length, per * PW), lambda p: (0, first + p))

    def stat_block(first):
        return pl.BlockSpec((per * 8, length), lambda p: (first + p, 0))

    att1, st1 = pl.pallas_call(
        functools.partial(forward_kernel, 256, 2),
        in_specs=[vmem_spec] * 4,
        out_specs=[vmem_spec] * 2,
        out_shape=[like(length), stats],
        compiler_params=params(),
        cost_estimate=pl.CostEstimate(flops=2 * ops * 4, bytes_accessed=6 * length * width * 2, transcendentals=0),
        name="forward",
    )(queries, key_vectors, value_vectors, out_grad)

    mine, st12, near_out = pl.pallas_call(
        functools.partial(merge_kernel, peers),
        in_specs=[vmem_spec] * (peers + 4),
        out_specs=[vmem_spec] * 3,
        out_shape=[like(FM), stats, like(n)],
        compiler_params=params(),
        name="merge",
    )(kv, qg, *got, st1, att1, fr)

    grads = []
    pieces = pairs // per

    def backward(piece, grads):
        any_spec = pl.BlockSpec(memory_space=pl.ANY)
        aliased = len(grads)
        return pl.pallas_call(
            functools.partial(backward_kernel, 256, 1, range(piece * per, (piece + 1) * per), aliased),
            in_specs=[vmem_spec] * 5 + [vmem_spec] * aliased,
            out_specs=[vmem_spec] * 3,
            out_shape=[like(length)] * 3,
            input_output_aliases={5 + i: i for i in range(aliased)},
            compiler_params=params(),
            cost_estimate=pl.CostEstimate(
                flops=5 * ops * 4 // pieces, bytes_accessed=8 * length * width * 2 // pieces, transcendentals=0
            ),
            name="backward",
        )(queries, key_vectors, value_vectors, out_grad, st12, *grads)

    def bits_of(size, least):
        while size > least:
            pick = 4 if size >= 4 * least else 2
            size //= pick
            yield pick, size

    steps = [("col", radix, unit, unit * row_count) for radix, unit in bits_of(col_count, 2)]
    steps += [("row", radix, unit, unit) for radix, unit in bits_of(row_count, peers)]
    stride = 1
    for _, radix, _, _ in steps:
        stride *= radix
    steps.append(("row", peers, 1, 1))
    if col_count > 1:
        steps.append(("col", 2, 1, row_count))
    far_all = mine
    for at, (axis, radix, unit, _) in enumerate(steps):
        others = [swap(far_all, axis, digit * unit) for digit in range(1, radix)]
        if at < pieces:
            grads = backward(at, grads)
            grads, others = lax.optimization_barrier((grads, others))
        far_all = jnp.concatenate([far_all, *others], axis=0)
    for at in range(len(steps), pieces):
        grads = backward(at, grads)
    digits = tuple((radix, unit) for _, radix, _, unit in steps)

    operands = (fr, far_all, kv, qg, *got, key_vectors, value_vectors, att1, *grads, near_out)
    return pl.pallas_call(
        functools.partial(final_kernel, peers, stride, digits),
        in_specs=[vmem_spec] * len(operands),
        out_specs=[pl.BlockSpec(memory_space=pl.ANY)] * 4,
        out_shape=[like(length)] * 4,
        scratch_shapes=[pltpu.VMEM((length, width), BF)] * 4 + [pltpu.SemaphoreType.DMA((4, groups))],
        compiler_params=params(),
        name="final",
    )(*operands)


def solution(mesh):
    placed = (
        P(("col", "row"), None),
        P(("col", "row"), None),
        P(("col", "row"), None),
        P(("col", "row"), None),
        P(),
        P(),
    )
    return jax.shard_map(
        shards,
        mesh=mesh,
        in_specs=placed,
        out_specs=(
            P(("col", "row"), None),
            P(("col", "row"), None),
            P(("col", "row"), None),
            P(("col", "row"), None),
        ),
        check_vma=False,
    )
```

```python
import functools

import jax
import jax.numpy as jnp
from jax import lax
from jax.experimental import pallas as pl
from jax.experimental.pallas import tpu as pltpu
from jax.sharding import PartitionSpec as P

H = 12
HD = 64
R2 = 16
R3 = 256
S1 = 512
SEG2 = 2048

NEG = -1e30
SCALE = HD**-0.5
GH = 4
GW = GH * HD
PW = 2 * HD
FM = 16
F32 = jnp.float32
BF = jnp.bfloat16
VMEM_LIMIT = 40
PICK_LIMIT = 58


def div(x, by):
    return x >> (by.bit_length() - 1) if by & (by - 1) == 0 else lax.div(x, jnp.int32(by))


def mod(x, by):
    return x & (by - 1) if by & (by - 1) == 0 else lax.rem(x, jnp.int32(by))


def iota(shape, axis):
    return lax.broadcasted_iota(jnp.int32, shape, axis)


def nn(a, b):
    return lax.dot_general(a, b, (((1,), (0,)), ((), ())), preferred_element_type=F32)


def nt(a, b):
    return lax.dot_general(a, b, (((1,), (1,)), ((), ())), preferred_element_type=F32)


def tn(a, b):
    return lax.dot_general(a, b, (((0,), (0,)), ((), ())), preferred_element_type=F32)


def onehot(cond):
    return jnp.where(cond, 1.0, 0.0).astype(BF)


def lane_offsets(ref, group):
    head = div(iota((1, GW), 1), HD)
    out = jnp.zeros((1, GW), jnp.int32)
    for h in range(GH):
        out = jnp.where(head == h, ref[group * GH + h], out)
    return out


def expand(x):
    head = div(iota((1, GW), 1), HD)
    return jnp.concatenate([x * onehot(head == h) for h in range(GH)], axis=0)


def collapse(x):
    n = x.shape[0] // GH
    head = div(iota((1, GW), 1), HD)
    out = x[:n]
    for h in range(1, GH):
        out = jnp.where(head == h, x[h * n : (h + 1) * n], out)
    return out


def split3(x):
    hi = x.astype(BF)
    rest = x - hi.astype(F32)
    mid = rest.astype(BF)
    low = (rest - mid.astype(F32)).astype(BF)
    return hi.astype(F32), mid.astype(F32), low.astype(F32)


def pack_aux(log_total, row_dot):
    lane = mod(iota((1, log_total.shape[1]), 1), HD)
    out = jnp.zeros(log_total.shape, F32)
    for at, piece in enumerate(split3(log_total) + split3(row_dot)):
        out = jnp.where(lane == at, piece, out)
    return out


def spread_sum(x, width):
    block = onehot(div(iota((width, 1), 0), HD) == div(iota((1, width), 1), HD))
    hi = x.astype(BF)
    low = (x - hi.astype(F32)).astype(BF)
    return nn(hi, block) + nn(low, block)


def piece_column(aux_expanded, which):
    a = iota((GW, 1), 0)
    return nn(aux_expanded, onehot(a % HD // 3 == which))[:, :1]


def near_select(n, length):
    return onehot(div(iota((1, length), 1), R2) == iota((n, 1), 0))


def near_place(n, length):
    return onehot(iota((length, 1), 0) // R2 == iota((1, n), 1))


def far_select(rows, length, first):
    return onehot(div(iota((1, length), 1), R3) == iota((rows, 1), 0) - first)


def far_place(length):
    return onehot(iota((length, 1), 0) // R3 == iota((1, FM), 1))


def token_masks(near_ref, far_ref, group, length):
    t = iota((length, 1), 0)
    near = mod(t, R2) == lane_offsets(near_ref, group)
    far = mod(t, R3) == lane_offsets(far_ref, group)
    return near, far


class HeadOffsets:
    def __init__(self, block, row, group):
        self.lanes = block[row : row + 1].astype(jnp.int32)
        self.first = group * GH

    def __getitem__(self, head):
        at = (head - self.first) * HD
        return self.lanes[:, at : at + 1]


def read_offsets(fr_ref, f, group):
    block = fr_ref[:, group_columns(group)].astype(F32)
    return HeadOffsets(block, 5 * f, group), HeadOffsets(block, 5 * f + 1, group)


def head_rows(n, stride, length, ref, group):
    r = iota((GH * n, 1), 0)
    token = mod(r, n) * stride
    for h in range(GH):
        token = jnp.where(div(r, n) == h, token + ref[group * GH + h], token)
    return onehot(iota((1, length), 1) == token)


def pick_kernel(peers, near_ref, far_ref, q_ref, k_ref, v_ref, g_ref, kv_ref, qg_ref, fr_ref, *msg_refs):
    group = pl.program_id(0)
    length = q_ref.shape[0]
    n, f = length // R2, length // R3
    sel = jnp.concatenate(
        [head_rows(n, R2, length, near_ref, group), head_rows(8, R3, length, far_ref, group)], axis=0
    )
    picked, far = [], []
    for ref in (q_ref, k_ref, v_ref, g_ref):
        rows = nn(sel, ref[...])
        picked.append(collapse(rows[: GH * n]).astype(BF))
        far.append(collapse(rows[GH * n :])[:f])
    offsets = [lane_offsets(ref, group).astype(F32) for ref in (near_ref, far_ref)]
    far += [jnp.zeros((f, GW), F32), *offsets, jnp.zeros((FM - 5 * f - 2, GW), F32)]
    fr_ref[...] = jnp.concatenate(far, axis=0).astype(BF)
    q, k, v, g = picked
    kv = jnp.concatenate([k, v], axis=0)
    qg = jnp.concatenate([q, g], axis=0)
    kv_ref[...] = kv
    qg_ref[...] = qg
    own = lax.axis_index("row") % peers
    for slot in range(1, peers):
        later = (own ^ slot) > own

        @pl.when(later)
        def _(slot=slot):
            msg_refs[slot - 1][...] = kv

        @pl.when(jnp.logical_not(later))
        def _(slot=slot):
            msg_refs[slot - 1][...] = qg


def staged(units, stages, skew):
    for t in range(len(units) + (len(stages) - 1) * skew):
        for i, stage in enumerate(stages):
            if 0 <= t - i * skew < len(units):
                stage(*units[t - i * skew])


def lockstep(bodies):
    bodies = list(bodies)
    while bodies:
        for body in list(bodies):
            try:
                next(body)
            except StopIteration:
                bodies.remove(body)


def head_masks():
    first = iota((1, PW), 1) < HD
    return first, (onehot(first), onehot(jnp.logical_not(first)))


def eye_of(n):
    return onehot(iota((n, 1), 0) == iota((1, n), 1))


def pair_columns(p):
    return slice(p * PW, (p + 1) * PW)


def forward_kernel(strip, skew, q_ref, k_ref, v_ref, g_ref, att_ref, st_ref):
    length, width = q_ref.shape
    _, in_head = head_masks()
    diag = iota((strip, 1), 0) <= iota((1, strip), 1)
    eye = eye_of(PW)
    kept = {}

    def score(p, r, h):
        cols, rows = pair_columns(p), slice(r * strip, (r + 1) * strip)
        if r == 0 and h == 0:
            kept["v", p] = nt(eye, v_ref[:, cols]).astype(BF)
            kept["g", p] = nt(eye, g_ref[:, cols])
        q = q_ref[rows, cols] * jnp.asarray(SCALE, BF) * in_head[h]
        kept["s", p, r, h] = nt(k_ref[: (r + 1) * strip, cols], q)

    def soften(p, r, h):
        s = kept.pop(("s", p, r, h))
        last = jnp.where(diag, s[r * strip :], NEG)
        s = jnp.concatenate([s[: r * strip], last], axis=0) if r else last
        top = jnp.max(s, axis=0, keepdims=True)
        w = jnp.exp(s - top)
        kept["w", p, r, h] = w.astype(BF), top, jnp.sum(w, axis=0, keepdims=True)

    def mix(p, r, h):
        cols, rows = pair_columns(p), slice(r * strip, (r + 1) * strip)
        lanes = slice(h * HD, (h + 1) * HD)
        w, top, total = kept.pop(("w", p, r, h))
        out = nn(kept["v", p][lanes, : (r + 1) * strip], w) / total
        kept["o", p, r, h] = out
        st_ref[p * 8 + h : p * 8 + h + 1, rows] = top + jnp.log(total)
        st_ref[p * 8 + 2 + h : p * 8 + 3 + h, rows] = jnp.sum(
            out * kept["g", p][lanes, rows], axis=0, keepdims=True
        )
        if h == 1:
            both = jnp.concatenate([kept.pop(("o", p, r, 0)), kept.pop(("o", p, r, 1))], axis=0)
            att_ref[rows, cols] = both.T.astype(BF)

    for p in range(width // PW):
        st_ref[p * 8 + 4 : p * 8 + 8, :] = jnp.zeros((4, length), F32)
    units = [(p, r, h) for p in range(width // PW) for r in range(length // strip) for h in range(2)]
    staged(units, (score, soften, mix), skew)


def near_valid_queries(shape, n, own):
    row, lane = mod(iota((shape[0], 1), 0), n), iota((1, shape[1]), 1)
    slot, key = div(lane, n), mod(lane, n)
    return ((slot ^ own) < own) | ((slot == 0) & (key <= row))


def near_valid_keys(shape, n, own):
    row, lane = mod(iota((shape[0], 1), 0), n), iota((1, shape[1]), 1)
    slot, query = div(lane, n), mod(lane, n)
    return ((slot ^ own) > own) | ((slot == 0) & (row <= query))


SR = GH // 2 * 8


def stat_row(shape, axis):
    r = mod(iota((shape[0], 1), axis), SR)
    return div(r, 8) * 2 + mod(r, 2), div(mod(r, 8), 2)


def stat_offsets(ref, group):
    head, _ = stat_row((SR, 1), 0)
    out = jnp.zeros((SR, 1), jnp.int32)
    for h in range(GH):
        out = jnp.where(head == h, ref[group * GH + h], out)
    return out


def pieces3(x):
    return jnp.concatenate([piece.astype(BF) for piece in split3(x)], axis=0)


def group_columns(group):
    return slice(group * GW, (group + 1) * GW)


def pack_lanes(group):
    l, m = iota((GW, 1), 0), iota((1, 128), 1)
    return onehot((mod(l, HD) < 6) & (m == (group * GH + div(l, HD)) * 6 + mod(l, HD)))


def unpack_lanes(group):
    l, m = iota((1, GW), 1), iota((128, 1), 0)
    return onehot((mod(l, HD) < 6) & (m == (group * GH + div(l, HD)) * 6 + mod(l, HD)))


def unpack_rows(peers, stride, n, f, fa_ref):
    per = fa_ref.shape[1] // 128
    rows = peers * stride * FM
    r, c = iota((peers * n, 1), 0), iota((1, rows), 1)
    at_row = c == div(r, n) * (stride * FM) + 5 * f + div(mod(r, n), per)
    out = jnp.zeros((peers * n, 128), F32)
    for at in range(per):
        out += nn(onehot(at_row & (mod(mod(r, n), per) == at)), fa_ref[:rows, at * 128 : (at + 1) * 128])
    return out.astype(BF)


def merge_group(peers, group, kv_ref, qg_ref, got, st_ref, att_ref, fr_ref, out_ref, st_out, near_out, blocks, packs):
    cols = group_columns(group)
    srows = slice(group * SR, (group + 1) * SR)
    length = att_ref.shape[0]
    n, f = length // R2, length // R3
    near_ref, far_ref = read_offsets(fr_ref, f, group)
    own = lax.axis_index("row") % peers
    heads = (kv_ref, *got)
    keys = jnp.concatenate([r[:n, cols] for r in heads], axis=0)
    values = jnp.concatenate([r[n:, cols] for r in heads], axis=0)
    s = nt(expand(qg_ref[:n, cols] * jnp.asarray(SCALE, BF)), keys)
    yield
    st = st_ref[srows, :]
    t = iota((1, length), 1)
    near_st = mod(t, R2) == stat_offsets(near_ref, group)
    far_st = mod(t, R3) == stat_offsets(far_ref, group)
    sel = near_select(n, length)
    log1 = nt(sel, pieces3(jnp.where(near_st, st, 0.0)))
    out1 = collapse(nn(head_rows(n, R2, length, near_ref, group), att_ref[:, cols]))
    yield
    s = jnp.where(near_valid_queries(s.shape, n, own), s, NEG)
    top = jnp.max(s, axis=1, keepdims=True)
    yield
    w = jnp.exp(s - top)
    total = jnp.sum(w, axis=1, keepdims=True)
    out2 = nn(w.astype(BF), values)
    head, what = stat_row((3 * SR, GW), 0)
    lane = iota((1, GW), 1)
    log1 = nn(log1.astype(BF), onehot((div(lane, HD) == head) & (what == 0)))
    yield
    out2 = collapse(out2 / total)
    log2 = collapse(jnp.broadcast_to(top + jnp.log(total), (GH * n, GW)))
    top = jnp.maximum(log1, log2)
    e1, e2 = jnp.exp(log1 - top), jnp.exp(log2 - top)
    both = e1 + e2
    log12 = top + jnp.log(both)
    out12 = (e1 * out1 + e2 * out2) / both
    near_out[:, cols] = out12.astype(BF)
    dot12 = spread_sum(qg_ref[n:, cols].astype(F32) * out12, GW)
    yield
    aux12 = pack_aux(log12, dot12).astype(BF)
    packs.append(nn(aux12, pack_lanes(group)))
    head, what = stat_row((SR, GW), 0)
    lane = iota((1, GW), 1)
    compact = nt(onehot((div(lane, HD) == head) & (div(mod(lane, HD), 3) == what)), aux12)
    yield
    place = onehot(div(iota((1, length), 1), R2) == iota((n, 1), 0))
    placed = nn(pieces3(compact), place)
    yield
    placed = placed[:SR] + placed[SR : 2 * SR] + placed[2 * SR :]
    st = jnp.where(near_st, placed, st)
    st_out[srows, :] = jnp.where(far_st, -NEG, st)
    far_aux = nt(far_select(FM, length, 4 * f), pieces3(jnp.where(far_st, st, 0.0)))
    yield
    head, what = stat_row((3 * SR, GW), 0)
    lane, piece = iota((1, GW), 1), div(iota((3 * SR, 1), 0), SR)
    far_aux = nn(far_aux.astype(BF), onehot((div(lane, HD) == head) & (mod(lane, HD) == what * 3 + piece)))
    raw = fr_ref[:, cols].astype(F32)
    blocks[group] = jnp.where(iota(raw.shape, 0) < 4 * f, raw, 0.0) + far_aux


def merge_kernel(peers, kv_ref, qg_ref, *rest):
    got, rest = rest[: peers - 1], rest[peers - 1 :]
    groups = kv_ref.shape[1] // GW
    out_ref = rest[3]
    blocks, packs = {}, []
    lockstep(
        merge_group(peers, group, kv_ref, qg_ref, got, *rest, blocks, packs)
        for group in range(groups)
    )
    packed = sum(packs[1:], packs[0]).astype(BF)
    n, length = packed.shape[0], rest[1].shape[0]
    per = out_ref.shape[1] // 128
    r, c = iota((FM, 1), 0) - 5 * (length // R3), iota((1, n), 1)
    for at in range(per):
        block = blocks[at * 128 // GW][:, at * 128 % GW :][:, :128]
        rows = nn(onehot((div(c, per) == r) & (mod(c, per) == at)), packed)
        out_ref[:, at * 128 : (at + 1) * 128] = (block + rows).astype(BF)


def backward_kernel(strip, skew, span, aliased, q_ref, k_ref, v_ref, g_ref, st_ref, *rest):
    dq_ref, dk_ref, dv_ref = rest[aliased:]
    length = q_ref.shape[0]
    first, in_head = head_masks()
    diag = iota((strip, 1), 0) <= iota((1, strip), 1)
    eye = eye_of(PW)
    strips = length // strip
    kept = {}

    def score(p, c, h):
        cols, rows = pair_columns(p), slice(c * strip, (c + 1) * strip)
        if c == 0 and h == 0:
            kept["k", p] = (nt(eye, k_ref[:, cols]) * SCALE).astype(BF)
            kept["q", p] = q_ref[:, cols] * jnp.asarray(SCALE, BF)
        s = nt(k_ref[rows, cols] * in_head[h], kept["q", p][c * strip :])
        dp = nt(v_ref[rows, cols] * in_head[h], g_ref[c * strip :, cols])
        kept["s", p, c, h] = s, dp

    def soften(p, c, h):
        s, dp = kept.pop(("s", p, c, h))
        prob = jnp.exp(s - st_ref[p * 8 + h : p * 8 + h + 1, c * strip :])
        head = jnp.where(diag, prob[:, :strip], 0.0)
        prob = jnp.concatenate([head, prob[:, strip:]], axis=1) if c + 1 < strips else head
        ds = prob * (dp - st_ref[p * 8 + 2 + h : p * 8 + 3 + h, c * strip :])
        kept["p", p, c, h] = prob.astype(BF), ds.astype(BF)

    def mix(p, c, h):
        cols, rows = pair_columns(p), slice(c * strip, (c + 1) * strip)
        prob, ds = kept.pop(("p", p, c, h))
        dv = nn(prob, g_ref[c * strip :, cols])
        dk = nn(ds, kept["q", p][c * strip :])
        part = nn(kept["k", p][h * HD : (h + 1) * HD, rows], ds)
        for r in range(c, strips):
            term = part[:, (r - c) * strip : (r - c + 1) * strip]
            kept["dq", p, r, h] = kept["dq", p, r, h] + term if c else term
        kept["dkv", p, c, h] = dk, dv
        if h == 1:
            one, two = kept.pop(("dkv", p, c, 0)), kept.pop(("dkv", p, c, 1))
            dk_ref[rows, cols] = jnp.where(first, one[0], two[0]).astype(BF)
            dv_ref[rows, cols] = jnp.where(first, one[1], two[1]).astype(BF)
            both = jnp.concatenate([kept.pop(("dq", p, c, 0)), kept.pop(("dq", p, c, 1))], axis=0)
            dq_ref[rows, cols] = both.T.astype(BF)

    units = [(p, c, h) for p in span for c in range(strips) for h in range(2)]
    staged(units, (score, soften, mix), skew)


def far_seq(index, f, digits, own):
    slot = div(index, f)
    seq = own
    for radix, unit in digits:
        seq = seq ^ (mod(slot, radix) * unit)
        slot = div(slot, radix)
    return seq * f + mod(index, f)


def row_offsets(n, ref, group):
    r = iota((GH * n, 1), 0)
    out = jnp.zeros((GH * n, 1), jnp.int32)
    for h in range(GH):
        out = jnp.where(div(r, n) == h, ref[group * GH + h], out)
    return out


def place_columns(n, length, near_ref, far_ref, group):
    parts = []
    for count, stride, ref in ((n, R2, near_ref), (FM, R3, far_ref)):
        c = iota((1, GH * count), 1)
        token = mod(c, count) * stride
        for h in range(GH):
            token = jnp.where(div(c, count) == h, token + ref[group * GH + h], token)
        parts.append(token)
    return onehot(iota((length, 1), 0) == jnp.concatenate(parts, axis=1))


def own_lanes(x):
    n = x.shape[0] // GH
    return jnp.where(div(iota((1, x.shape[1]), 1), HD) == div(iota((x.shape[0], 1), 0), n), x, 0.0)


def piece_columns(aux_expanded):
    a, c = iota((GW, 1), 0), iota((1, 256), 1)
    both = nn(aux_expanded, onehot(div(mod(a, HD), 3) == div(c, 128)))
    return both[:, :1], both[:, 128:129]


def near_group(peers, group, fr_ref, packed, kv_ref, qg_ref, got, dq_ref, dk_ref, dv_ref):
    cols = group_columns(group)
    n = dq_ref.shape[0]
    f = n * R2 // R3
    near_ref, far_ref = read_offsets(fr_ref, f, group)
    own = lax.axis_index("row") % peers
    keys, values, queries, grads = near_operands(n, cols, kv_ref, qg_ref, got)
    naux = nn(packed(), unpack_lanes(group))
    s = nt(expand(queries[:n]), keys)
    dp = nt(expand(grads[:n]), values)
    yield
    s2 = nt(expand(keys[:n]), queries)
    dp2 = nt(expand(values[:n]), grads)
    noff, foff = lane_offsets(near_ref, group), lane_offsets(far_ref, group)
    also_far = (mod(iota((naux.shape[0], 1), 0), R3 // R2) == div(foff, R2)) & (mod(foff, R2) == noff)
    none = jnp.where(mod(iota((1, GW), 1), HD) == 0, -NEG, 0.0)
    naux = jnp.where(also_far, none, naux).astype(BF)
    yield
    log_q, dot_q = piece_columns(expand(naux[:n]))
    log_k, dot_k = piece_rows(n, naux)
    yield
    ok = near_valid_queries(s.shape, n, own)
    p = jnp.where(ok, jnp.exp(s - log_q), 0.0)
    ds = (p * (dp - dot_q)).astype(BF)
    yield
    ok = near_valid_keys(s2.shape, n, own)
    p = jnp.where(ok, jnp.exp(s2 - log_k), 0.0)
    ds2 = (p * (dp2 - dot_k)).astype(BF)
    yield
    dq_ref[:, cols] = (collapse(nn(ds, keys)) * SCALE).astype(BF)
    yield
    dk_ref[:, cols] = collapse(nn(ds2, queries)).astype(BF)
    dv_ref[:, cols] = collapse(nn(p.astype(BF), grads)).astype(BF)


def near_kernel(peers, stride, fr_ref, fa_ref, kv_ref, qg_ref, *rest):
    got, outs = rest[: peers - 1], rest[peers - 1 :]
    n, width = outs[0].shape
    made = []

    def packed():
        if not made:
            made.append(unpack_rows(peers, stride, n, n * R2 // R3, fa_ref))
        return made[0]

    lockstep(
        near_group(peers, group, fr_ref, packed, kv_ref, qg_ref, got, *outs) for group in range(width // GW)
    )


def near_operands(n, cols, kv_ref, qg_ref, got):
    heads = [kv_ref, *got]
    keys = jnp.concatenate([x[:n, cols] for x in heads], axis=0)
    values = jnp.concatenate([x[n:, cols] for x in heads], axis=0)
    heads = [qg_ref, *got]
    queries = jnp.concatenate([x[:n, cols] for x in heads], axis=0) * jnp.asarray(SCALE, BF)
    grads = jnp.concatenate([x[n:, cols] for x in heads], axis=0)
    return keys, values, queries, grads


def piece_rows(n, aux):
    r, c = iota((2 * GH * n, 1), 0), iota((1, GW), 1)
    head, which = div(mod(r, GH * n), n), div(r, GH * n)
    both = nt(onehot((div(c, HD) == head) & (div(mod(c, HD), 3) == which)), aux)
    return both[: GH * n], both[GH * n :]


def final_group(
    peers, stride, digits, group, fr_ref, got, fa_ref, k_ref, v_ref, base, near_out, near_grads, outs, done
):
    kv_ref, qg_ref, got = got[0], got[1], got[2:]
    cols = group_columns(group)
    length = k_ref.shape[0]
    n, f = length // R2, length // R3
    near_ref, far_ref = read_offsets(fr_ref, f, group)
    blocks = fa_ref.shape[0] // FM
    F = blocks * f
    row_here = lax.axis_index("row")
    own = row_here % peers
    seq = lax.axis_index("col") * lax.axis_size("row") + row_here
    scale = jnp.asarray(SCALE, BF)

    r, c = iota((5 * F, 1), 0), iota((1, blocks * FM), 1)
    i, at = div(r, F), mod(r, F)
    sel = onehot(c == div(at, f) * FM + i * f + mod(at, f))
    fa = nn(sel, fa_ref[:, cols])
    yield
    fa = fa.astype(BF)
    fq, fk, fv, fg, faux = (fa[i * F : (i + 1) * F] for i in range(5))
    qx, gx, ax = expand(fq * scale), expand(fg), expand(faux)
    s = nt(qx, fk)
    dp = nt(gx, fv)
    log12, dot12 = piece_columns(ax)
    yield
    keys, values, _, _ = near_operands(n, cols, kv_ref, qg_ref, got)
    kx, vx = expand(keys[:n]), expand(values[:n])
    fq = fq * scale
    part = peers * stride * f
    key_s, key_dp = nt(kx, fq[:part]), nt(vx, fg[:part])
    place_q = far_seq(mod(iota((GH * F, 1), 0), F), f, digits, seq)
    place_k = far_seq(iota((1, F), 1), f, digits, seq)
    s = jnp.where(place_k <= place_q, s, NEG)
    top = jnp.max(s, axis=1, keepdims=True)
    yield
    w = jnp.exp(s - top)
    total = jnp.sum(w, axis=1, keepdims=True)
    dot3 = jnp.sum(w * dp, axis=1, keepdims=True)
    k, v = k_ref[:, cols], v_ref[:, cols]

    def own_rows(x):
        return jnp.concatenate([x[h * F : h * F + FM] for h in range(GH)], axis=0)

    qo, go = own_rows(qx), own_rows(gx)
    local_s, local_dp = nt(qo, k), nt(go, v)
    near_s, near_dp = nt(qo, keys), nt(go, values)
    roff, rnear = row_offsets(FM, far_ref, group), row_offsets(FM, near_ref, group)
    token = mod(iota((GH * FM, 1), 0), FM) * R3 + roff
    att_far = nn(onehot(iota((1, length), 1) == token), base[0][:, cols])
    near_far = nn(onehot(iota((1, n), 1) * R2 + rnear == token), near_out[:, cols])
    att_far = jnp.where(mod(roff, R2) == rnear, near_far, att_far)
    yield
    log3 = top + jnp.log(total)
    dot3 = dot3 / total
    top = jnp.maximum(log12, log3)
    e12, e3 = jnp.exp(log12 - top), jnp.exp(log3 - top)
    both = e12 + e3
    log_all = top + jnp.log(both)
    dot_all = (e12 * dot12 + e3 * dot3) / both
    p = jnp.exp(s - log_all)
    ds = p * (dp - dot_all)
    pb, dsb = p.astype(BF), ds.astype(BF)
    log_own, dot_own, keep = own_rows(log_all), own_rows(dot_all), own_rows(e12 / both)
    yield
    final_aux = pack_aux(
        *(collapse(jnp.broadcast_to(x, (GH * F, GW)))[:part] for x in (log_all, dot_all))
    ).astype(BF)
    far_out = own_lanes(nn(own_rows(pb), fv) + keep * att_far)
    far_dq = nn(own_rows(dsb), fk)
    far_dv = tn(pb, gx)[:FM]
    far_dk = tn(dsb, qx)[:FM]
    yield
    r = iota((GH * FM, 1), 0)
    reach = jnp.where(mod(r, FM) < f, token, -1)
    ok = iota((1, length), 1) <= reach
    p = jnp.where(ok, jnp.exp(local_s - log_own), 0.0)
    ds = (p * (local_dp - dot_own)).astype(BF)
    pb = p.astype(BF)
    twice = mod(roff, R2) == rnear
    c = iota((1, peers * n), 1)
    slot = div(c, n)
    ok = twice & (reach >= 0) & (((slot ^ own) < own) | ((slot == 0) & (mod(c, n) <= div(reach, R2))))
    np = jnp.where(ok, jnp.exp(near_s - log_own), 0.0)
    nds = (np * (near_dp - dot_own)).astype(BF)
    yield
    log_k, dot_k = piece_rows(n, final_aux)
    far_dq += nn(nds, keys)
    far_dq = own_lanes(far_dq + nn(ds, k))
    place = place_columns(n, length, near_ref, far_ref, group)
    noff, foff = lane_offsets(near_ref, group), lane_offsets(far_ref, group)
    also_far = (mod(iota((n, 1), 0), R3 // R2) == div(foff, R2)) & (mod(foff, R2) == noff)
    alone = jnp.where(also_far, 0.0, near_out[:, cols].astype(F32)).astype(BF)
    placed = nn(place, jnp.concatenate([expand(alone), far_out.astype(BF)], axis=0))
    yield
    near, far = token_masks(near_ref, far_ref, group, length)
    outs[0][:, cols] = jnp.where(near | far, placed, base[0][:, cols].astype(F32)).astype(BF)
    done(0, cols)
    yield
    koff, knear = row_offsets(n, far_ref, group), row_offsets(n, near_ref, group)
    c = iota((1, part), 1)
    slot = div(c, f)
    other = div(slot, stride)
    late = ((other ^ own) > own) | ((other == 0) & (mod(iota((GH * n, 1), 0), n) <= div(mod(c, f) * R3 + koff, R2)))
    ok = (mod(koff, R2) == knear) & (mod(slot, stride) == 0) & late
    np = jnp.where(ok, jnp.exp(key_s - log_k), 0.0)
    nds = (np * (key_dp - dot_k)).astype(BF)
    dk = tn(ds, qo)
    dv = tn(pb, go)
    yield
    near_dq = expand(near_grads[0][:, cols]).astype(F32)
    near_dk = own_lanes(nn(nds, fq[:part])) + expand(near_grads[1][:, cols]).astype(F32)
    near_dv = own_lanes(nn(np.astype(BF), fg[:part])) + expand(near_grads[2][:, cols]).astype(F32)
    yield
    terms = nn(place, jnp.concatenate([near_dq, far_dq * SCALE], axis=0).astype(BF))
    outs[1][:, cols] = (base[1][:, cols].astype(F32) + terms).astype(BF)
    done(1, cols)
    yield
    terms = dk + nn(place, jnp.concatenate([near_dk.astype(BF), expand(far_dk.astype(BF))], axis=0))
    outs[2][:, cols] = (base[2][:, cols].astype(F32) + terms).astype(BF)
    done(2, cols)
    yield
    terms = dv + nn(place, jnp.concatenate([near_dv.astype(BF), expand(far_dv.astype(BF))], axis=0))
    outs[3][:, cols] = (base[3][:, cols].astype(F32) + terms).astype(BF)
    done(3, cols)


def final_kernel(peers, stride, digits, fr_ref, *refs):
    near_end = 2 + peers
    count = near_end + 2 + 8
    held, results = refs[:count], refs[count : count + 4]
    outs, out_sems = refs[count + 4 : count + 8], refs[-1]

    sent = []

    def done(which, cols):
        copy = pltpu.make_async_copy(
            outs[which].at[:, cols], results[which].at[:, cols], out_sems.at[which, cols.start // GW]
        )
        copy.start()
        sent.append(copy)

    near, local, base = held[1:near_end], held[near_end : near_end + 2], held[near_end + 2 :]
    groups = results[0].shape[1] // GW
    lockstep(
        final_group(
            peers, stride, digits, group, fr_ref, near, held[0], *local,
            base[:4], base[4], base[5:], outs, done,
        )
        for group in range(groups)
    )
    for copy in sent:
        copy.wait()


def smem():
    return pl.BlockSpec(memory_space=pltpu.SMEM)


def whole_block(rows, width):
    return pl.BlockSpec((rows, width), lambda g: (0, 0))


def group_block(rows):
    return pl.BlockSpec((rows, GW), lambda g: (0, g))


def params(limit=VMEM_LIMIT):
    return pltpu.CompilerParams(vmem_limit_bytes=limit * 1024 * 1024)


def shards(queries, key_vectors, value_vectors, out_grad, near_offsets, far_offsets):
    length, width = queries.shape
    row_count = lax.axis_size("row")
    col_count = lax.axis_size("col")
    peers = SEG2 // length
    n, f = length // R2, length // R3
    groups = width // GW
    pairs = width // PW

    def like(rows):
        return jax.ShapeDtypeStruct((rows, width), BF)

    def swap(x, axis, mask):
        size = lax.axis_size(axis)
        return lax.ppermute(x, axis, [(i, i ^ mask) for i in range(size)])

    picked = pl.pallas_call(
        functools.partial(pick_kernel, peers),
        grid=(groups,),
        in_specs=[smem(), smem()] + [group_block(length)] * 4,
        out_specs=[group_block(2 * n)] * 2 + [group_block(FM)] + [group_block(2 * n)] * (peers - 1),
        out_shape=[like(2 * n)] * 2 + [like(FM)] + [like(2 * n)] * (peers - 1),
        compiler_params=params(PICK_LIMIT),
        name="pick",
    )(near_offsets, far_offsets, queries, key_vectors, value_vectors, out_grad)
    kv, qg, fr, msgs = picked[0], picked[1], picked[2], picked[3:]
    got = [swap(msgs[s - 1], "row", s) for s in range(1, peers)]

    ops = 2 * H * length * length * HD
    stats = jax.ShapeDtypeStruct((pairs * 8, length), F32)
    per = 2

    vmem_spec = pl.BlockSpec(memory_space=pltpu.VMEM)

    def pair_block(first):
        return pl.BlockSpec((length, per * PW), lambda p: (0, first + p))

    def stat_block(first):
        return pl.BlockSpec((per * 8, length), lambda p: (first + p, 0))

    att1, st1 = pl.pallas_call(
        functools.partial(forward_kernel, 256, 2),
        in_specs=[vmem_spec] * 4,
        out_specs=[vmem_spec] * 2,
        out_shape=[like(length), stats],
        compiler_params=params(),
        cost_estimate=pl.CostEstimate(flops=2 * ops * 4, bytes_accessed=6 * length * width * 2, transcendentals=0),
        name="forward",
    )(queries, key_vectors, value_vectors, out_grad)

    mine, st12, near_out = pl.pallas_call(
        functools.partial(merge_kernel, peers),
        in_specs=[vmem_spec] * (peers + 4),
        out_specs=[vmem_spec] * 3,
        out_shape=[like(FM), stats, like(n)],
        compiler_params=params(),
        name="merge",
    )(kv, qg, *got, st1, att1, fr)

    grads = []
    pieces = pairs // per

    def backward(piece, grads):
        any_spec = pl.BlockSpec(memory_space=pl.ANY)
        aliased = len(grads)
        return pl.pallas_call(
            functools.partial(backward_kernel, 256, 1, range(piece * per, (piece + 1) * per), aliased),
            in_specs=[vmem_spec] * 5 + [vmem_spec] * aliased,
            out_specs=[vmem_spec] * 3,
            out_shape=[like(length)] * 3,
            input_output_aliases={5 + i: i for i in range(aliased)},
            compiler_params=params(),
            cost_estimate=pl.CostEstimate(
                flops=5 * ops * 4 // pieces, bytes_accessed=8 * length * width * 2 // pieces, transcendentals=0
            ),
            name="backward",
        )(queries, key_vectors, value_vectors, out_grad, st12, *grads)

    def beside(at, count):
        if at == count - 1:
            return range(pieces - 1 if count > 1 else 0, pieces)
        return range(pieces - 1) if at == 0 else ()

    def near_pass(far_all):
        return pl.pallas_call(
            functools.partial(near_kernel, peers, stride),
            in_specs=[vmem_spec] * (peers + 3),
            out_specs=[vmem_spec] * 3,
            out_shape=[like(n)] * 3,
            compiler_params=params(),
            cost_estimate=pl.CostEstimate(flops=ops, bytes_accessed=2 * length * width, transcendentals=0),
            name="near",
        )(fr, far_all, kv, qg, *got)

    def bits_of(size, least):
        while size > least:
            pick = 4 if size >= 4 * least else 2
            size //= pick
            yield pick, size

    steps = [("col", radix, unit, unit * row_count) for radix, unit in bits_of(col_count, 2)]
    steps += [("row", radix, unit, unit) for radix, unit in bits_of(row_count, peers)]
    stride = 1
    for _, radix, _, _ in steps:
        stride *= radix
    steps.append(("row", peers, 1, 1))
    if col_count > 1:
        steps.append(("col", 2, 1, row_count))
    far_all = mine
    for at, (axis, radix, unit, _) in enumerate(steps):
        others = [swap(far_all, axis, digit * unit) for digit in range(1, radix)]
        if at == len(steps) - 1 and col_count > 1:
            near_grads = near_pass(far_all)
            near_grads, others = lax.optimization_barrier((near_grads, others))
        else:
            for piece in beside(at, len(steps) - 1):
                grads = backward(piece, grads)
            grads, others = lax.optimization_barrier((grads, others))
        far_all = jnp.concatenate([far_all, *others], axis=0)
    if col_count == 1:
        near_grads = near_pass(far_all)
    digits = tuple((radix, unit) for _, radix, _, unit in steps)

    operands = (fr, far_all, kv, qg, *got, key_vectors, value_vectors, att1, *grads, near_out, *near_grads)
    return pl.pallas_call(
        functools.partial(final_kernel, peers, stride, digits),
        in_specs=[vmem_spec] * len(operands),
        out_specs=[pl.BlockSpec(memory_space=pl.ANY)] * 4,
        out_shape=[like(length)] * 4,
        scratch_shapes=[pltpu.VMEM((length, width), BF)] * 4 + [pltpu.SemaphoreType.DMA((4, groups))],
        compiler_params=params(),
        name="final",
    )(*operands)


def solution(mesh):
    placed = (
        P(("col", "row"), None),
        P(("col", "row"), None),
        P(("col", "row"), None),
        P(("col", "row"), None),
        P(),
        P(),
    )
    return jax.shard_map(
        shards,
        mesh=mesh,
        in_specs=placed,
        out_specs=(
            P(("col", "row"), None),
            P(("col", "row"), None),
            P(("col", "row"), None),
            P(("col", "row"), None),
        ),
        check_vma=False,
    )
```

```python
import functools

import jax
import jax.numpy as jnp
from jax import lax
from jax.experimental import pallas as pl
from jax.experimental.pallas import tpu as pltpu
from jax.sharding import PartitionSpec as P

H = 12
HD = 64
R2 = 16
R3 = 256
S1 = 512
SEG2 = 2048

NEG = -1e30
SCALE = HD**-0.5
GH = 4
GW = GH * HD
PW = 2 * HD
FM = 16
F32 = jnp.float32
BF = jnp.bfloat16
VMEM_LIMIT = 40
PICK_LIMIT = 58


def div(x, by):
    return x >> (by.bit_length() - 1) if by & (by - 1) == 0 else lax.div(x, jnp.int32(by))


def mod(x, by):
    return x & (by - 1) if by & (by - 1) == 0 else lax.rem(x, jnp.int32(by))


def iota(shape, axis):
    return lax.broadcasted_iota(jnp.int32, shape, axis)


def nn(a, b):
    return lax.dot_general(a, b, (((1,), (0,)), ((), ())), preferred_element_type=F32)


def nt(a, b):
    return lax.dot_general(a, b, (((1,), (1,)), ((), ())), preferred_element_type=F32)


def tn(a, b):
    return lax.dot_general(a, b, (((0,), (0,)), ((), ())), preferred_element_type=F32)


def onehot(cond):
    return jnp.where(cond, 1.0, 0.0).astype(BF)


def lane_offsets(ref, group):
    head = div(iota((1, GW), 1), HD)
    out = jnp.zeros((1, GW), jnp.int32)
    for h in range(GH):
        out = jnp.where(head == h, ref[group * GH + h], out)
    return out


def expand(x):
    head = div(iota((1, GW), 1), HD)
    return jnp.concatenate([x * onehot(head == h) for h in range(GH)], axis=0)


def collapse(x):
    n = x.shape[0] // GH
    head = div(iota((1, GW), 1), HD)
    out = x[:n]
    for h in range(1, GH):
        out = jnp.where(head == h, x[h * n : (h + 1) * n], out)
    return out


def split3(x):
    hi = x.astype(BF)
    rest = x - hi.astype(F32)
    mid = rest.astype(BF)
    low = (rest - mid.astype(F32)).astype(BF)
    return hi.astype(F32), mid.astype(F32), low.astype(F32)


def pack_aux(log_total, row_dot):
    lane = mod(iota((1, log_total.shape[1]), 1), HD)
    out = jnp.zeros(log_total.shape, F32)
    for at, piece in enumerate(split3(log_total) + split3(row_dot)):
        out = jnp.where(lane == at, piece, out)
    return out


def spread_sum(x, width):
    block = onehot(div(iota((width, 1), 0), HD) == div(iota((1, width), 1), HD))
    hi = x.astype(BF)
    low = (x - hi.astype(F32)).astype(BF)
    return nn(hi, block) + nn(low, block)


def near_select(n, length):
    return onehot(div(iota((1, length), 1), R2) == iota((n, 1), 0))


def far_select(rows, length, first):
    return onehot(div(iota((1, length), 1), R3) == iota((rows, 1), 0) - first)


def token_masks(near_ref, far_ref, group, length):
    t = iota((length, 1), 0)
    near = mod(t, R2) == lane_offsets(near_ref, group)
    far = mod(t, R3) == lane_offsets(far_ref, group)
    return near, far


class HeadOffsets:
    def __init__(self, block, row, group):
        self.lanes = block[row : row + 1].astype(jnp.int32)
        self.first = group * GH

    def __getitem__(self, head):
        at = (head - self.first) * HD
        return self.lanes[:, at : at + 1]


def read_offsets(fr_ref, f, group):
    block = fr_ref[:, group_columns(group)].astype(F32)
    return HeadOffsets(block, 5 * f, group), HeadOffsets(block, 5 * f + 1, group)


def head_rows(n, stride, length, ref, group):
    r = iota((GH * n, 1), 0)
    token = mod(r, n) * stride
    for h in range(GH):
        token = jnp.where(div(r, n) == h, token + ref[group * GH + h], token)
    return onehot(iota((1, length), 1) == token)


def pick_kernel(peers, near_ref, far_ref, q_ref, k_ref, v_ref, g_ref, kv_ref, qg_ref, fr_ref, *msg_refs):
    group = pl.program_id(0)
    length = q_ref.shape[0]
    n, f = length // R2, length // R3
    sel = jnp.concatenate(
        [head_rows(n, R2, length, near_ref, group), head_rows(8, R3, length, far_ref, group)], axis=0
    )
    picked, far = [], []
    for ref in (q_ref, k_ref, v_ref, g_ref):
        rows = nn(sel, ref[...])
        picked.append(collapse(rows[: GH * n]).astype(BF))
        far.append(collapse(rows[GH * n :])[:f])
    offsets = [lane_offsets(ref, group).astype(F32) for ref in (near_ref, far_ref)]
    far += [jnp.zeros((f, GW), F32), *offsets, jnp.zeros((FM - 5 * f - 2, GW), F32)]
    fr_ref[...] = jnp.concatenate(far, axis=0).astype(BF)
    q, k, v, g = picked
    kv = jnp.concatenate([k, v], axis=0)
    qg = jnp.concatenate([q, g], axis=0)
    kv_ref[...] = kv
    qg_ref[...] = qg
    own = lax.axis_index("row") % peers
    for slot in range(1, peers):
        later = (own ^ slot) > own

        @pl.when(later)
        def _(slot=slot):
            msg_refs[slot - 1][...] = kv

        @pl.when(jnp.logical_not(later))
        def _(slot=slot):
            msg_refs[slot - 1][...] = qg


def staged(units, stages, skew):
    for t in range(len(units) + (len(stages) - 1) * skew):
        for i, stage in enumerate(stages):
            if 0 <= t - i * skew < len(units):
                stage(*units[t - i * skew])


def lockstep(bodies):
    bodies = list(bodies)
    while bodies:
        for body in list(bodies):
            try:
                next(body)
            except StopIteration:
                bodies.remove(body)


def head_masks():
    first = iota((1, PW), 1) < HD
    return first, (onehot(first), onehot(jnp.logical_not(first)))


def eye_of(n):
    return onehot(iota((n, 1), 0) == iota((1, n), 1))


def pair_columns(p):
    return slice(p * PW, (p + 1) * PW)


def forward_kernel(strip, skew, q_ref, k_ref, v_ref, g_ref, att_ref, st_ref):
    length, width = q_ref.shape
    _, in_head = head_masks()
    diag = iota((strip, 1), 0) <= iota((1, strip), 1)
    eye = eye_of(PW)
    kept = {}

    def score(p, r, h):
        cols, rows = pair_columns(p), slice(r * strip, (r + 1) * strip)
        if r == 0 and h == 0:
            kept["v", p] = nt(eye, v_ref[:, cols]).astype(BF)
            kept["g", p] = nt(eye, g_ref[:, cols])
        q = q_ref[rows, cols] * jnp.asarray(SCALE, BF) * in_head[h]
        kept["s", p, r, h] = nt(k_ref[: (r + 1) * strip, cols], q)

    def soften(p, r, h):
        s = kept.pop(("s", p, r, h))
        last = jnp.where(diag, s[r * strip :], NEG)
        s = jnp.concatenate([s[: r * strip], last], axis=0) if r else last
        top = jnp.max(s, axis=0, keepdims=True)
        w = jnp.exp(s - top)
        kept["w", p, r, h] = w.astype(BF), top, jnp.sum(w, axis=0, keepdims=True)

    def mix(p, r, h):
        cols, rows = pair_columns(p), slice(r * strip, (r + 1) * strip)
        lanes = slice(h * HD, (h + 1) * HD)
        w, top, total = kept.pop(("w", p, r, h))
        out = nn(kept["v", p][lanes, : (r + 1) * strip], w) / total
        kept["o", p, r, h] = out
        st_ref[p * 8 + h : p * 8 + h + 1, rows] = top + jnp.log(total)
        st_ref[p * 8 + 2 + h : p * 8 + 3 + h, rows] = jnp.sum(
            out * kept["g", p][lanes, rows], axis=0, keepdims=True
        )
        if h == 1:
            both = jnp.concatenate([kept.pop(("o", p, r, 0)), kept.pop(("o", p, r, 1))], axis=0)
            att_ref[rows, cols] = both.T.astype(BF)

    for p in range(width // PW):
        st_ref[p * 8 + 4 : p * 8 + 8, :] = jnp.zeros((4, length), F32)
    units = [(p, r, h) for p in range(width // PW) for r in range(length // strip) for h in range(2)]
    staged(units, (score, soften, mix), skew)


def near_valid_queries(shape, n, own):
    row, lane = mod(iota((shape[0], 1), 0), n), iota((1, shape[1]), 1)
    slot, key = div(lane, n), mod(lane, n)
    return ((slot ^ own) < own) | ((slot == 0) & (key <= row))


def near_valid_keys(shape, n, own):
    row, lane = mod(iota((shape[0], 1), 0), n), iota((1, shape[1]), 1)
    slot, query = div(lane, n), mod(lane, n)
    return ((slot ^ own) > own) | ((slot == 0) & (row <= query))


SR = GH // 2 * 8


def stat_row(shape, axis):
    r = mod(iota((shape[0], 1), axis), SR)
    return div(r, 8) * 2 + mod(r, 2), div(mod(r, 8), 2)


def stat_offsets(ref, group):
    head, _ = stat_row((SR, 1), 0)
    out = jnp.zeros((SR, 1), jnp.int32)
    for h in range(GH):
        out = jnp.where(head == h, ref[group * GH + h], out)
    return out


def pieces3(x):
    return jnp.concatenate([piece.astype(BF) for piece in split3(x)], axis=0)


def group_columns(group):
    return slice(group * GW, (group + 1) * GW)


def pack_lanes(group):
    l, m = iota((GW, 1), 0), iota((1, 128), 1)
    return onehot((mod(l, HD) < 6) & (m == (group * GH + div(l, HD)) * 6 + mod(l, HD)))


def unpack_lanes(group):
    l, m = iota((1, GW), 1), iota((128, 1), 0)
    return onehot((mod(l, HD) < 6) & (m == (group * GH + div(l, HD)) * 6 + mod(l, HD)))


def unpack_rows(peers, stride, n, f, fa_ref):
    per = fa_ref.shape[1] // 128
    rows = peers * stride * FM
    r, c = iota((peers * n, 1), 0), iota((1, rows), 1)
    at_row = c == div(r, n) * (stride * FM) + 5 * f + div(mod(r, n), per)
    out = jnp.zeros((peers * n, 128), F32)
    for at in range(per):
        out += nn(onehot(at_row & (mod(mod(r, n), per) == at)), fa_ref[:rows, at * 128 : (at + 1) * 128])
    return out.astype(BF)


def merge_group(peers, group, kv_ref, qg_ref, got, st_ref, att_ref, fr_ref, out_ref, near_aux, near_out, blocks, packs):
    cols = group_columns(group)
    srows = slice(group * SR, (group + 1) * SR)
    length = att_ref.shape[0]
    n, f = length // R2, length // R3
    near_ref, far_ref = read_offsets(fr_ref, f, group)
    own = lax.axis_index("row") % peers
    heads = (kv_ref, *got)
    keys = jnp.concatenate([r[:n, cols] for r in heads], axis=0)
    values = jnp.concatenate([r[n:, cols] for r in heads], axis=0)
    s = nt(expand(qg_ref[:n, cols] * jnp.asarray(SCALE, BF)), keys)
    yield
    st = st_ref[srows, :]
    t = iota((1, length), 1)
    near_st = mod(t, R2) == stat_offsets(near_ref, group)
    far_st = mod(t, R3) == stat_offsets(far_ref, group)
    sel = near_select(n, length)
    log1 = nt(sel, pieces3(jnp.where(near_st, st, 0.0)))
    out1 = collapse(nn(head_rows(n, R2, length, near_ref, group), att_ref[:, cols]))
    far_aux = nt(far_select(FM, length, 4 * f), pieces3(jnp.where(far_st, st, 0.0)))
    yield
    s = jnp.where(near_valid_queries(s.shape, n, own), s, NEG)
    top = jnp.max(s, axis=1, keepdims=True)
    yield
    w = jnp.exp(s - top)
    total = jnp.sum(w, axis=1, keepdims=True)
    out2 = nn(w.astype(BF), values)
    head, what = stat_row((3 * SR, GW), 0)
    lane = iota((1, GW), 1)
    piece = div(iota((3 * SR, 1), 0), SR)
    log1 = nn(log1.astype(BF), onehot((div(lane, HD) == head) & (what == 0)))
    far_aux = nn(far_aux.astype(BF), onehot((div(lane, HD) == head) & (mod(lane, HD) == what * 3 + piece)))
    yield
    out2 = collapse(out2 / total)
    log2 = collapse(jnp.broadcast_to(top + jnp.log(total), (GH * n, GW)))
    top = jnp.maximum(log1, log2)
    e1, e2 = jnp.exp(log1 - top), jnp.exp(log2 - top)
    both = e1 + e2
    log12 = top + jnp.log(both)
    out12 = (e1 * out1 + e2 * out2) / both
    near_out[:, cols] = out12.astype(BF)
    dot12 = spread_sum(qg_ref[n:, cols].astype(F32) * out12, GW)
    yield
    aux12 = pack_aux(log12, dot12).astype(BF)
    packs.append(nn(aux12, pack_lanes(group)))
    near_aux[:, cols] = aux12
    r = iota((GH * FM, 1), 0)
    j = mod(r, FM) - 4 * f
    foff, noff = row_offsets(FM, far_ref, group), row_offsets(FM, near_ref, group)
    row = jnp.where((j >= 0) & (j < f) & (mod(foff, R2) == noff), j * (R3 // R2) + div(foff, R2), -1)
    from_near = collapse(nn(onehot(iota((1, n), 1) == row), aux12))
    yield
    twice = mod(lane_offsets(far_ref, group), R2) == lane_offsets(near_ref, group)
    raw = fr_ref[:, cols].astype(F32)
    raw = jnp.where(iota((FM, 1), 0) < 4 * f, raw, 0.0)
    blocks[group] = raw + jnp.where(twice, from_near, far_aux)


def merge_kernel(peers, kv_ref, qg_ref, *rest):
    got, rest = unturned(rest[: peers - 1]), rest[peers - 1 :]
    groups = kv_ref.shape[1] // GW
    out_ref = rest[3]
    blocks, packs = {}, []
    lockstep(
        merge_group(peers, group, kv_ref, qg_ref, got, *rest, blocks, packs)
        for group in range(groups)
    )
    packed = sum(packs[1:], packs[0]).astype(BF)
    n, length = packed.shape[0], rest[1].shape[0]
    per = out_ref.shape[1] // 128
    r, c = iota((FM, 1), 0) - 5 * (length // R3), iota((1, n), 1)
    for at in range(per):
        block = blocks[at * 128 // GW][:, at * 128 % GW :][:, :128]
        rows = nn(onehot((div(c, per) == r) & (mod(c, per) == at)), packed)
        out_ref[:, at * 128 : (at + 1) * 128] = (block + rows).astype(BF)


def pair_statistics(p, st_ref, aux_ref, fr_ref):
    length = st_ref.shape[1]
    n, f = length // R2, length // R3
    near, far = read_offsets(fr_ref, f, p * 2 // GH)
    r, lane, t = iota((8, 1), 0), iota((1, PW), 1), iota((1, length), 1)
    noff, foff = (jnp.where(mod(r, 2) == 0, ref[2 * p], ref[2 * p + 1]) for ref in (near, far))
    mine = (div(lane, HD) == mod(r, 2)) & (div(mod(lane, HD), 3) == div(r, 2)) & (r < 4)
    merged = nt(onehot(mine), aux_ref[:, pair_columns(p)])
    place = onehot(div(t, R2) == iota((n, 1), 0))
    merged = nn(pieces3(merged), place)
    merged = merged[:8] + merged[8:16] + merged[16:]
    st = jnp.where(mod(t, R2) == noff, merged, st_ref[p * 8 : p * 8 + 8, :])
    return jnp.where(mod(t, R3) == foff, -NEG, st)


def backward_kernel(strip, skew, span, aliased, q_ref, k_ref, v_ref, g_ref, st_ref, aux_ref, fr_ref, *rest):
    dq_ref, dk_ref, dv_ref = rest[aliased:]
    length = q_ref.shape[0]
    first, in_head = head_masks()
    diag = iota((strip, 1), 0) <= iota((1, strip), 1)
    eye = eye_of(PW)
    strips = length // strip
    kept = {}

    def score(p, c, h):
        cols, rows = pair_columns(p), slice(c * strip, (c + 1) * strip)
        if c == 0 and h == 0:
            kept["k", p] = (nt(eye, k_ref[:, cols]) * SCALE).astype(BF)
            kept["q", p] = q_ref[:, cols] * jnp.asarray(SCALE, BF)
            kept["st", p] = pair_statistics(p, st_ref, aux_ref, fr_ref)
        s = nt(k_ref[rows, cols] * in_head[h], kept["q", p][c * strip :])
        dp = nt(v_ref[rows, cols] * in_head[h], g_ref[c * strip :, cols])
        kept["s", p, c, h] = s, dp

    def soften(p, c, h):
        s, dp = kept.pop(("s", p, c, h))
        st = kept["st", p][:, c * strip :]
        prob = jnp.exp(s - st[h : h + 1])
        head = jnp.where(diag, prob[:, :strip], 0.0)
        prob = jnp.concatenate([head, prob[:, strip:]], axis=1) if c + 1 < strips else head
        ds = prob * (dp - st[2 + h : 3 + h])
        kept["p", p, c, h] = prob.astype(BF), ds.astype(BF)

    def mix(p, c, h):
        cols, rows = pair_columns(p), slice(c * strip, (c + 1) * strip)
        prob, ds = kept.pop(("p", p, c, h))
        dv = nn(prob, g_ref[c * strip :, cols])
        dk = nn(ds, kept["q", p][c * strip :])
        part = nn(kept["k", p][h * HD : (h + 1) * HD, rows], ds)
        for r in range(c, strips):
            term = part[:, (r - c) * strip : (r - c + 1) * strip]
            kept["dq", p, r, h] = kept["dq", p, r, h] + term if c else term
        kept["dkv", p, c, h] = dk, dv
        if h == 1:
            one, two = kept.pop(("dkv", p, c, 0)), kept.pop(("dkv", p, c, 1))
            dk_ref[rows, cols] = jnp.where(first, one[0], two[0]).astype(BF)
            dv_ref[rows, cols] = jnp.where(first, one[1], two[1]).astype(BF)
            both = jnp.concatenate([kept.pop(("dq", p, c, 0)), kept.pop(("dq", p, c, 1))], axis=0)
            dq_ref[rows, cols] = both.T.astype(BF)

    units = [(p, c, h) for p in span for c in range(strips) for h in range(2)]
    staged(units, (score, soften, mix), skew)


def far_seq(index, f, digits, own):
    slot = div(index, f)
    seq = own
    for radix, unit in digits:
        seq = seq ^ (mod(slot, radix) * unit)
        slot = div(slot, radix)
    return seq * f + mod(index, f)


def row_offsets(n, ref, group):
    r = iota((GH * n, 1), 0)
    out = jnp.zeros((GH * n, 1), jnp.int32)
    for h in range(GH):
        out = jnp.where(div(r, n) == h, ref[group * GH + h], out)
    return out


def place_columns(n, length, near_ref, far_ref, group):
    parts = []
    for count, stride, ref in ((n, R2, near_ref), (FM, R3, far_ref)):
        c = iota((1, GH * count), 1)
        token = mod(c, count) * stride
        for h in range(GH):
            token = jnp.where(div(c, count) == h, token + ref[group * GH + h], token)
        parts.append(token)
    return onehot(iota((length, 1), 0) == jnp.concatenate(parts, axis=1))


def own_lanes(x):
    n = x.shape[0] // GH
    return jnp.where(div(iota((1, x.shape[1]), 1), HD) == div(iota((x.shape[0], 1), 0), n), x, 0.0)


def piece_columns(aux_expanded):
    a, c = iota((GW, 1), 0), iota((1, 256), 1)
    both = nn(aux_expanded, onehot(div(mod(a, HD), 3) == div(c, 128)))
    return both[:, :1], both[:, 128:129]


def near_group(peers, group, fr_ref, packed, kv_ref, qg_ref, got, dq_ref, dk_ref, dv_ref):
    cols = group_columns(group)
    n = dq_ref.shape[0]
    f = n * R2 // R3
    near_ref, far_ref = read_offsets(fr_ref, f, group)
    own = lax.axis_index("row") % peers
    keys, values, queries, grads = near_operands(n, cols, kv_ref, qg_ref, got)
    naux = nn(packed(), unpack_lanes(group))
    s = nt(expand(queries[:n]), keys)
    dp = nt(expand(grads[:n]), values)
    yield
    s2 = nt(expand(keys[:n]), queries)
    dp2 = nt(expand(values[:n]), grads)
    noff, foff = lane_offsets(near_ref, group), lane_offsets(far_ref, group)
    also_far = (mod(iota((naux.shape[0], 1), 0), R3 // R2) == div(foff, R2)) & (mod(foff, R2) == noff)
    none = jnp.where(mod(iota((1, GW), 1), HD) == 0, -NEG, 0.0)
    naux = jnp.where(also_far, none, naux).astype(BF)
    yield
    log_q, dot_q = piece_columns(expand(naux[:n]))
    log_k, dot_k = piece_rows(n, naux)
    yield
    ok = near_valid_queries(s.shape, n, own)
    p = jnp.where(ok, jnp.exp(s - log_q), 0.0)
    ds = (p * (dp - dot_q)).astype(BF)
    yield
    ok = near_valid_keys(s2.shape, n, own)
    p = jnp.where(ok, jnp.exp(s2 - log_k), 0.0)
    ds2 = (p * (dp2 - dot_k)).astype(BF)
    yield
    dq_ref[:, cols] = (collapse(nn(ds, keys)) * SCALE).astype(BF)
    yield
    dk_ref[:, cols] = collapse(nn(ds2, queries)).astype(BF)
    dv_ref[:, cols] = collapse(nn(p.astype(BF), grads)).astype(BF)


def near_kernel(peers, stride, fr_ref, fa_ref, kv_ref, qg_ref, *rest):
    got, outs = unturned(rest[: peers - 1]), rest[peers - 1 :]
    n, width = outs[0].shape
    made = []

    def packed():
        if not made:
            made.append(unpack_rows(peers, stride, n, n * R2 // R3, fa_ref))
        return made[0]

    lockstep(
        near_group(peers, group, fr_ref, packed, kv_ref, qg_ref, got, *outs) for group in range(width // GW)
    )


def near_operands(n, cols, kv_ref, qg_ref, got):
    heads = [kv_ref, *got]
    keys = jnp.concatenate([x[:n, cols] for x in heads], axis=0)
    values = jnp.concatenate([x[n:, cols] for x in heads], axis=0)
    heads = [qg_ref, *got]
    queries = jnp.concatenate([x[:n, cols] for x in heads], axis=0) * jnp.asarray(SCALE, BF)
    grads = jnp.concatenate([x[n:, cols] for x in heads], axis=0)
    return keys, values, queries, grads


def piece_rows(n, aux):
    r, c = iota((2 * GH * n, 1), 0), iota((1, GW), 1)
    head, which = div(mod(r, GH * n), n), div(r, GH * n)
    both = nt(onehot((div(c, HD) == head) & (div(mod(c, HD), 3) == which)), aux)
    return both[: GH * n], both[GH * n :]


def final_group(
    peers, stride, digits, group, fr_ref, got, fa_ref, k_ref, v_ref, base, near_out, near_grads, outs, done
):
    kv_ref, qg_ref, got = got[0], got[1], unturned(got[2:])
    cols = group_columns(group)
    length = k_ref.shape[0]
    n, f = length // R2, length // R3
    near_ref, far_ref = read_offsets(fr_ref, f, group)
    blocks = fa_ref.shape[0] // FM
    F = blocks * f
    row_here = lax.axis_index("row")
    own = row_here % peers
    seq = lax.axis_index("col") * lax.axis_size("row") + row_here
    scale = jnp.asarray(SCALE, BF)

    r, c = iota((5 * F, 1), 0), iota((1, blocks * FM), 1)
    i, at = div(r, F), mod(r, F)
    sel = onehot(c == div(at, f) * FM + i * f + mod(at, f))
    fa = nn(sel, fa_ref[:, cols])
    yield
    fa = fa.astype(BF)
    fq, fk, fv, fg, faux = (fa[i * F : (i + 1) * F] for i in range(5))
    qx, gx, ax = expand(fq * scale), expand(fg), expand(faux)
    s = nt(qx, fk)
    dp = nt(gx, fv)
    log12, dot12 = piece_columns(ax)
    yield
    keys, values, _, _ = near_operands(n, cols, kv_ref, qg_ref, got)
    kx, vx = expand(keys[:n]), expand(values[:n])
    fq = fq * scale
    part = peers * stride * f
    key_s, key_dp = nt(kx, fq[:part]), nt(vx, fg[:part])
    place_q = far_seq(mod(iota((GH * F, 1), 0), F), f, digits, seq)
    place_k = far_seq(iota((1, F), 1), f, digits, seq)
    s = jnp.where(place_k <= place_q, s, NEG)
    top = jnp.max(s, axis=1, keepdims=True)
    yield
    w = jnp.exp(s - top)
    total = jnp.sum(w, axis=1, keepdims=True)
    dot3 = jnp.sum(w * dp, axis=1, keepdims=True)
    k, v = k_ref[:, cols], v_ref[:, cols]

    def own_rows(x):
        return jnp.concatenate([x[h * F : h * F + FM] for h in range(GH)], axis=0)

    qo, go = own_rows(qx), own_rows(gx)
    local_s, local_dp = nt(qo, k), nt(go, v)
    near_s, near_dp = nt(qo, keys), nt(go, values)
    roff, rnear = row_offsets(FM, far_ref, group), row_offsets(FM, near_ref, group)
    token = mod(iota((GH * FM, 1), 0), FM) * R3 + roff
    att_far = nn(onehot(iota((1, length), 1) == token), base[0][:, cols])
    near_far = nn(onehot(iota((1, n), 1) * R2 + rnear == token), near_out[:, cols])
    att_far = jnp.where(mod(roff, R2) == rnear, near_far, att_far)
    yield
    log3 = top + jnp.log(total)
    dot3 = dot3 / total
    top = jnp.maximum(log12, log3)
    e12, e3 = jnp.exp(log12 - top), jnp.exp(log3 - top)
    both = e12 + e3
    log_all = top + jnp.log(both)
    dot_all = (e12 * dot12 + e3 * dot3) / both
    p = jnp.exp(s - log_all)
    ds = p * (dp - dot_all)
    pb, dsb = p.astype(BF), ds.astype(BF)
    log_own, dot_own, keep = own_rows(log_all), own_rows(dot_all), own_rows(e12 / both)
    yield
    final_aux = pack_aux(
        *(collapse(jnp.broadcast_to(x, (GH * F, GW)))[:part] for x in (log_all, dot_all))
    ).astype(BF)
    far_out = own_lanes(nn(own_rows(pb), fv) + keep * att_far)
    far_dq = nn(own_rows(dsb), fk)
    far_dv = tn(pb, gx)[:FM]
    far_dk = tn(dsb, qx)[:FM]
    yield
    r = iota((GH * FM, 1), 0)
    reach = jnp.where(mod(r, FM) < f, token, -1)
    ok = iota((1, length), 1) <= reach
    p = jnp.where(ok, jnp.exp(local_s - log_own), 0.0)
    ds = (p * (local_dp - dot_own)).astype(BF)
    pb = p.astype(BF)
    twice = mod(roff, R2) == rnear
    c = iota((1, peers * n), 1)
    slot = div(c, n)
    ok = twice & (reach >= 0) & (((slot ^ own) < own) | ((slot == 0) & (mod(c, n) <= div(reach, R2))))
    np = jnp.where(ok, jnp.exp(near_s - log_own), 0.0)
    nds = (np * (near_dp - dot_own)).astype(BF)
    yield
    log_k, dot_k = piece_rows(n, final_aux)
    far_dq += nn(nds, keys)
    far_dq = own_lanes(far_dq + nn(ds, k))
    place = place_columns(n, length, near_ref, far_ref, group)
    noff, foff = lane_offsets(near_ref, group), lane_offsets(far_ref, group)
    also_far = (mod(iota((n, 1), 0), R3 // R2) == div(foff, R2)) & (mod(foff, R2) == noff)
    alone = jnp.where(also_far, 0.0, near_out[:, cols].astype(F32)).astype(BF)
    placed = nn(place, jnp.concatenate([expand(alone), far_out.astype(BF)], axis=0))
    yield
    near, far = token_masks(near_ref, far_ref, group, length)
    outs[0][:, cols] = jnp.where(near | far, placed, base[0][:, cols].astype(F32)).astype(BF)
    done(0, cols)
    yield
    koff, knear = row_offsets(n, far_ref, group), row_offsets(n, near_ref, group)
    c = iota((1, part), 1)
    slot = div(c, f)
    other = div(slot, stride)
    late = ((other ^ own) > own) | ((other == 0) & (mod(iota((GH * n, 1), 0), n) <= div(mod(c, f) * R3 + koff, R2)))
    ok = (mod(koff, R2) == knear) & (mod(slot, stride) == 0) & late
    np = jnp.where(ok, jnp.exp(key_s - log_k), 0.0)
    nds = (np * (key_dp - dot_k)).astype(BF)
    dk = tn(ds, qo)
    dv = tn(pb, go)
    yield
    near_dq = expand(near_grads[0][:, cols]).astype(F32)
    near_dk = own_lanes(nn(nds, fq[:part])) + expand(near_grads[1][:, cols]).astype(F32)
    near_dv = own_lanes(nn(np.astype(BF), fg[:part])) + expand(near_grads[2][:, cols]).astype(F32)
    yield
    terms = nn(place, jnp.concatenate([near_dq, far_dq * SCALE], axis=0).astype(BF))
    outs[1][:, cols] = (base[1][:, cols].astype(F32) + terms).astype(BF)
    done(1, cols)
    yield
    terms = dk + nn(place, jnp.concatenate([near_dk.astype(BF), expand(far_dk.astype(BF))], axis=0))
    outs[2][:, cols] = (base[2][:, cols].astype(F32) + terms).astype(BF)
    done(2, cols)
    yield
    terms = dv + nn(place, jnp.concatenate([near_dv.astype(BF), expand(far_dv.astype(BF))], axis=0))
    outs[3][:, cols] = (base[3][:, cols].astype(F32) + terms).astype(BF)
    done(3, cols)


def final_kernel(peers, stride, digits, fr_ref, *refs):
    near_end = 2 + peers
    count = near_end + 2 + 8
    held, results = refs[:count], refs[count : count + 4]
    outs, out_sems = refs[count + 4 : count + 8], refs[-1]

    sent = []

    def done(which, cols):
        copy = pltpu.make_async_copy(
            outs[which].at[:, cols], results[which].at[:, cols], out_sems.at[which, cols.start // GW]
        )
        copy.start()
        sent.append(copy)

    near, local, base = held[1:near_end], held[near_end : near_end + 2], held[near_end + 2 :]
    groups = results[0].shape[1] // GW
    lockstep(
        final_group(
            peers, stride, digits, group, fr_ref, near, held[0], *local,
            base[:4], base[4], base[5:], outs, done,
        )
        for group in range(groups)
    )
    for copy in sent:
        copy.wait()


def turned(x):
    return [x[-1], *x[:-1]]


def unturned(x):
    return [*x[1:], x[0]]


def smem():
    return pl.BlockSpec(memory_space=pltpu.SMEM)


def whole_block(rows, width):
    return pl.BlockSpec((rows, width), lambda g: (0, 0))


def group_block(rows):
    return pl.BlockSpec((rows, GW), lambda g: (0, g))


def params(limit=VMEM_LIMIT):
    return pltpu.CompilerParams(vmem_limit_bytes=limit * 1024 * 1024)


def shards(queries, key_vectors, value_vectors, out_grad, near_offsets, far_offsets):
    length, width = queries.shape
    row_count = lax.axis_size("row")
    col_count = lax.axis_size("col")
    peers = SEG2 // length
    n, f = length // R2, length // R3
    groups = width // GW
    pairs = width // PW

    def like(rows):
        return jax.ShapeDtypeStruct((rows, width), BF)

    def swap(x, axis, mask):
        size = lax.axis_size(axis)
        return lax.ppermute(x, axis, [(i, i ^ mask) for i in range(size)])

    picked = pl.pallas_call(
        functools.partial(pick_kernel, peers),
        grid=(groups,),
        in_specs=[smem(), smem()] + [group_block(length)] * 4,
        out_specs=[group_block(2 * n)] * 2 + [group_block(FM)] + [group_block(2 * n)] * (peers - 1),
        out_shape=[like(2 * n)] * 2 + [like(FM)] + [like(2 * n)] * (peers - 1),
        compiler_params=params(PICK_LIMIT),
        name="pick",
    )(near_offsets, far_offsets, queries, key_vectors, value_vectors, out_grad)
    kv, qg, fr, msgs = picked[0], picked[1], picked[2], picked[3:]
    got = [swap(msgs[s - 1], "row", s) for s in range(1, peers)]

    ops = 2 * H * length * length * HD
    stats = jax.ShapeDtypeStruct((pairs * 8, length), F32)
    per = 3

    vmem_spec = pl.BlockSpec(memory_space=pltpu.VMEM)

    def pair_block(first):
        return pl.BlockSpec((length, per * PW), lambda p: (0, first + p))

    def stat_block(first):
        return pl.BlockSpec((per * 8, length), lambda p: (first + p, 0))

    att1, st1 = pl.pallas_call(
        functools.partial(forward_kernel, 256, 2),
        in_specs=[vmem_spec] * 4,
        out_specs=[vmem_spec] * 2,
        out_shape=[like(length), stats],
        compiler_params=params(),
        cost_estimate=pl.CostEstimate(flops=2 * ops * 4, bytes_accessed=6 * length * width * 2, transcendentals=0),
        name="forward",
    )(queries, key_vectors, value_vectors, out_grad)

    mine, near_aux, near_out = pl.pallas_call(
        functools.partial(merge_kernel, peers),
        in_specs=[vmem_spec] * (peers + 4),
        out_specs=[vmem_spec] * 3,
        out_shape=[like(FM), like(n), like(n)],
        compiler_params=params(),
        name="merge",
    )(kv, qg, *turned(got), st1, att1, fr)

    grads = []
    pieces = pairs // per

    def backward(piece, grads):
        any_spec = pl.BlockSpec(memory_space=pl.ANY)
        aliased = len(grads)
        return pl.pallas_call(
            functools.partial(backward_kernel, 256, 1, range(piece * per, (piece + 1) * per), aliased),
            in_specs=[vmem_spec] * (7 + aliased),
            out_specs=[vmem_spec] * 3,
            out_shape=[like(length)] * 3,
            input_output_aliases={7 + i: i for i in range(aliased)},
            compiler_params=params(),
            cost_estimate=pl.CostEstimate(
                flops=5 * ops * 4 // pieces, bytes_accessed=8 * length * width * 2 // pieces, transcendentals=0
            ),
            name="backward",
        )(queries, key_vectors, value_vectors, out_grad, st1, near_aux, fr, *grads)

    def beside(at, count):
        if at == count - 1:
            return range(pieces - 1 if count > 1 else 0, pieces)
        return range(pieces - 1) if at == 0 else ()

    def near_pass(far_all):
        return pl.pallas_call(
            functools.partial(near_kernel, peers, stride),
            in_specs=[vmem_spec] * (peers + 3),
            out_specs=[vmem_spec] * 3,
            out_shape=[like(n)] * 3,
            compiler_params=params(),
            cost_estimate=pl.CostEstimate(flops=ops, bytes_accessed=2 * length * width, transcendentals=0),
            name="near",
        )(fr, far_all, kv, qg, *turned(got))

    def bits_of(size, least):
        while size > least:
            pick = 4 if size >= 4 * least else 2
            size //= pick
            yield pick, size

    steps = [("col", radix, unit, unit * row_count) for radix, unit in bits_of(col_count, 2)]
    steps += [("row", radix, unit, unit) for radix, unit in bits_of(row_count, peers)]
    stride = 1
    for _, radix, _, _ in steps:
        stride *= radix
    steps.append(("row", peers, 1, 1))
    if col_count > 1:
        steps.append(("col", 2, 1, row_count))
    far_all = mine
    for at, (axis, radix, unit, _) in enumerate(steps):
        others = [swap(far_all, axis, digit * unit) for digit in range(1, radix)]
        if at == len(steps) - 1 and col_count > 1:
            near_grads = near_pass(far_all)
            near_grads, others = lax.optimization_barrier((near_grads, others))
        else:
            for piece in beside(at, len(steps) - 1):
                grads = backward(piece, grads)
            grads, others = lax.optimization_barrier((grads, others))
        far_all = jnp.concatenate([far_all, *others], axis=0)
    if col_count == 1:
        near_grads = near_pass(far_all)
    digits = tuple((radix, unit) for _, radix, _, unit in steps)

    operands = (fr, far_all, kv, qg, *turned(got), key_vectors, value_vectors, att1, *grads, near_out, *near_grads)
    return pl.pallas_call(
        functools.partial(final_kernel, peers, stride, digits),
        in_specs=[vmem_spec] * len(operands),
        out_specs=[pl.BlockSpec(memory_space=pl.ANY)] * 4,
        out_shape=[like(length)] * 4,
        scratch_shapes=[pltpu.VMEM((length, width), BF)] * 4 + [pltpu.SemaphoreType.DMA((4, groups))],
        compiler_params=params(),
        name="final",
    )(*operands)


def solution(mesh):
    placed = (
        P(("col", "row"), None),
        P(("col", "row"), None),
        P(("col", "row"), None),
        P(("col", "row"), None),
        P(),
        P(),
    )
    return jax.shard_map(
        shards,
        mesh=mesh,
        in_specs=placed,
        out_specs=(
            P(("col", "row"), None),
            P(("col", "row"), None),
            P(("col", "row"), None),
            P(("col", "row"), None),
        ),
        check_vma=False,
    )
```

```python
import functools

import jax
import jax.numpy as jnp
from jax import lax
from jax.experimental import pallas as pl
from jax.experimental.pallas import tpu as pltpu
from jax.sharding import PartitionSpec as P

H = 12
HD = 64
R2 = 16
R3 = 256
S1 = 512
SEG2 = 2048

NEG = -1e30
SCALE = HD**-0.5
GH = 4
GW = GH * HD
PW = 2 * HD
FM = 16
F32 = jnp.float32
BF = jnp.bfloat16
VMEM_LIMIT = 40
PICK_LIMIT = 58


def div(x, by):
    return x >> (by.bit_length() - 1) if by & (by - 1) == 0 else lax.div(x, jnp.int32(by))


def mod(x, by):
    return x & (by - 1) if by & (by - 1) == 0 else lax.rem(x, jnp.int32(by))


def iota(shape, axis):
    return lax.broadcasted_iota(jnp.int32, shape, axis)


def nn(a, b):
    return lax.dot_general(a, b, (((1,), (0,)), ((), ())), preferred_element_type=F32)


def nt(a, b):
    return lax.dot_general(a, b, (((1,), (1,)), ((), ())), preferred_element_type=F32)


def tn(a, b):
    return lax.dot_general(a, b, (((0,), (0,)), ((), ())), preferred_element_type=F32)


def onehot(cond):
    return jnp.where(cond, 1.0, 0.0).astype(BF)


def lane_offsets(ref, group):
    head = div(iota((1, GW), 1), HD)
    out = jnp.zeros((1, GW), jnp.int32)
    for h in range(GH):
        out = jnp.where(head == h, ref[group * GH + h], out)
    return out


def expand(x):
    head = div(iota((1, GW), 1), HD)
    return jnp.concatenate([x * onehot(head == h) for h in range(GH)], axis=0)


def collapse(x):
    n = x.shape[0] // GH
    head = div(iota((1, GW), 1), HD)
    out = x[:n]
    for h in range(1, GH):
        out = jnp.where(head == h, x[h * n : (h + 1) * n], out)
    return out


def split3(x):
    hi = x.astype(BF)
    rest = x - hi.astype(F32)
    mid = rest.astype(BF)
    low = (rest - mid.astype(F32)).astype(BF)
    return hi.astype(F32), mid.astype(F32), low.astype(F32)


def pack_aux(log_total, row_dot):
    lane = mod(iota((1, log_total.shape[1]), 1), HD)
    out = jnp.zeros(log_total.shape, F32)
    for at, piece in enumerate(split3(log_total) + split3(row_dot)):
        out = jnp.where(lane == at, piece, out)
    return out


def spread_sum(x, width):
    block = onehot(div(iota((width, 1), 0), HD) == div(iota((1, width), 1), HD))
    hi = x.astype(BF)
    low = (x - hi.astype(F32)).astype(BF)
    return nn(hi, block) + nn(low, block)


def near_select(n, length):
    return onehot(div(iota((1, length), 1), R2) == iota((n, 1), 0))


def far_select(rows, length, first):
    return onehot(div(iota((1, length), 1), R3) == iota((rows, 1), 0) - first)


def token_masks(near_ref, far_ref, group, length):
    t = iota((length, 1), 0)
    near = mod(t, R2) == lane_offsets(near_ref, group)
    far = mod(t, R3) == lane_offsets(far_ref, group)
    return near, far


class HeadOffsets:
    def __init__(self, block, row, group):
        self.lanes = block[row : row + 1].astype(jnp.int32)
        self.first = group * GH

    def __getitem__(self, head):
        at = (head - self.first) * HD
        return self.lanes[:, at : at + 1]


def read_offsets(fr_ref, f, group):
    block = fr_ref[:, group_columns(group)].astype(F32)
    return HeadOffsets(block, 5 * f, group), HeadOffsets(block, 5 * f + 1, group)


def head_rows(n, stride, length, ref, group):
    r = iota((GH * n, 1), 0)
    token = mod(r, n) * stride
    for h in range(GH):
        token = jnp.where(div(r, n) == h, token + ref[group * GH + h], token)
    return onehot(iota((1, length), 1) == token)


def pick_kernel(peers, near_ref, far_ref, q_ref, k_ref, v_ref, g_ref, kv_ref, qg_ref, fr_ref, *msg_refs):
    group = pl.program_id(0)
    length = q_ref.shape[0]
    n, f = length // R2, length // R3
    sel = jnp.concatenate(
        [head_rows(n, R2, length, near_ref, group), head_rows(8, R3, length, far_ref, group)], axis=0
    )
    picked, far = [], []
    for ref in (q_ref, k_ref, v_ref, g_ref):
        rows = nn(sel, ref[...])
        picked.append(collapse(rows[: GH * n]).astype(BF))
        far.append(collapse(rows[GH * n :])[:f])
    offsets = [lane_offsets(ref, group).astype(F32) for ref in (near_ref, far_ref)]
    far += [jnp.zeros((f, GW), F32), *offsets, jnp.zeros((FM - 5 * f - 2, GW), F32)]
    fr_ref[...] = jnp.concatenate(far, axis=0).astype(BF)
    q, k, v, g = picked
    kv = jnp.concatenate([k, v], axis=0)
    qg = jnp.concatenate([q, g], axis=0)
    kv_ref[...] = kv
    qg_ref[...] = qg
    own = lax.axis_index("row") % peers
    for slot in range(1, peers):
        later = (own ^ slot) > own

        @pl.when(later)
        def _(slot=slot):
            msg_refs[slot - 1][...] = kv

        @pl.when(jnp.logical_not(later))
        def _(slot=slot):
            msg_refs[slot - 1][...] = qg


def staged(units, stages, skew):
    for t in range(len(units) + (len(stages) - 1) * skew):
        for i, stage in enumerate(stages):
            if 0 <= t - i * skew < len(units):
                stage(*units[t - i * skew])


def lockstep(bodies):
    bodies = list(bodies)
    while bodies:
        for body in list(bodies):
            try:
                next(body)
            except StopIteration:
                bodies.remove(body)


def head_masks():
    first = iota((1, PW), 1) < HD
    return first, (onehot(first), onehot(jnp.logical_not(first)))


def eye_of(n):
    return onehot(iota((n, 1), 0) == iota((1, n), 1))


def pair_columns(p):
    return slice(p * PW, (p + 1) * PW)


def forward_kernel(strip, skew, q_ref, k_ref, v_ref, g_ref, att_ref, st_ref):
    length, width = q_ref.shape
    _, in_head = head_masks()
    diag = iota((strip, 1), 0) <= iota((1, strip), 1)
    eye = eye_of(PW)
    kept = {}

    def score(p, r, h):
        cols, rows = pair_columns(p), slice(r * strip, (r + 1) * strip)
        if r == 0 and h == 0:
            kept["v", p] = nt(eye, v_ref[:, cols]).astype(BF)
            kept["g", p] = nt(eye, g_ref[:, cols])
        q = q_ref[rows, cols] * jnp.asarray(SCALE, BF) * in_head[h]
        kept["s", p, r, h] = nt(k_ref[: (r + 1) * strip, cols], q)

    def soften(p, r, h):
        s = kept.pop(("s", p, r, h))
        last = jnp.where(diag, s[r * strip :], NEG)
        s = jnp.concatenate([s[: r * strip], last], axis=0) if r else last
        top = jnp.max(s, axis=0, keepdims=True)
        w = jnp.exp(s - top)
        kept["w", p, r, h] = w.astype(BF), top, jnp.sum(w, axis=0, keepdims=True)

    def mix(p, r, h):
        cols, rows = pair_columns(p), slice(r * strip, (r + 1) * strip)
        lanes = slice(h * HD, (h + 1) * HD)
        w, top, total = kept.pop(("w", p, r, h))
        out = nn(kept["v", p][lanes, : (r + 1) * strip], w) / total
        kept["o", p, r, h] = out
        st_ref[p * 8 + h : p * 8 + h + 1, rows] = top + jnp.log(total)
        st_ref[p * 8 + 2 + h : p * 8 + 3 + h, rows] = jnp.sum(
            out * kept["g", p][lanes, rows], axis=0, keepdims=True
        )
        if h == 1:
            both = jnp.concatenate([kept.pop(("o", p, r, 0)), kept.pop(("o", p, r, 1))], axis=0)
            att_ref[rows, cols] = both.T.astype(BF)

    for p in range(width // PW):
        st_ref[p * 8 + 4 : p * 8 + 8, :] = jnp.zeros((4, length), F32)
    units = [(p, r, h) for p in range(width // PW) for r in range(length // strip) for h in range(2)]
    staged(units, (score, soften, mix), skew)


def near_valid_queries(shape, n, own):
    row, lane = mod(iota((shape[0], 1), 0), n), iota((1, shape[1]), 1)
    slot, key = div(lane, n), mod(lane, n)
    return ((slot ^ own) < own) | ((slot == 0) & (key <= row))


def near_valid_keys(shape, n, own):
    row, lane = mod(iota((shape[0], 1), 0), n), iota((1, shape[1]), 1)
    slot, query = div(lane, n), mod(lane, n)
    return ((slot ^ own) > own) | ((slot == 0) & (row <= query))


SR = GH // 2 * 8


def stat_row(shape, axis):
    r = mod(iota((shape[0], 1), axis), SR)
    return div(r, 8) * 2 + mod(r, 2), div(mod(r, 8), 2)


def stat_offsets(ref, group):
    head, _ = stat_row((SR, 1), 0)
    out = jnp.zeros((SR, 1), jnp.int32)
    for h in range(GH):
        out = jnp.where(head == h, ref[group * GH + h], out)
    return out


def pieces3(x):
    return jnp.concatenate([piece.astype(BF) for piece in split3(x)], axis=0)


def group_columns(group):
    return slice(group * GW, (group + 1) * GW)


def pack_lanes(group):
    l, m = iota((GW, 1), 0), iota((1, 128), 1)
    return onehot((mod(l, HD) < 6) & (m == (group * GH + div(l, HD)) * 6 + mod(l, HD)))


def unpack_lanes(group):
    l, m = iota((1, GW), 1), iota((128, 1), 0)
    return onehot((mod(l, HD) < 6) & (m == (group * GH + div(l, HD)) * 6 + mod(l, HD)))


def unpack_rows(peers, stride, n, f, fa_ref):
    per = fa_ref.shape[1] // 128
    rows = peers * stride * FM
    r, c = iota((peers * n, 1), 0), iota((1, rows), 1)
    at_row = c == div(r, n) * (stride * FM) + 5 * f + div(mod(r, n), per)
    out = jnp.zeros((peers * n, 128), F32)
    for at in range(per):
        out += nn(onehot(at_row & (mod(mod(r, n), per) == at)), fa_ref[:rows, at * 128 : (at + 1) * 128])
    return out.astype(BF)


def merge_group(peers, group, kv_ref, qg_ref, got, st_ref, att_ref, fr_ref, out_ref, near_aux, near_out, blocks, packs):
    cols = group_columns(group)
    srows = slice(group * SR, (group + 1) * SR)
    length = att_ref.shape[0]
    n, f = length // R2, length // R3
    near_ref, far_ref = read_offsets(fr_ref, f, group)
    own = lax.axis_index("row") % peers
    heads = (kv_ref, *got)
    keys = jnp.concatenate([r[:n, cols] for r in heads], axis=0)
    values = jnp.concatenate([r[n:, cols] for r in heads], axis=0)
    s = nt(expand(qg_ref[:n, cols] * jnp.asarray(SCALE, BF)), keys)
    yield
    st = st_ref[srows, :]
    t = iota((1, length), 1)
    near_st = mod(t, R2) == stat_offsets(near_ref, group)
    far_st = mod(t, R3) == stat_offsets(far_ref, group)
    sel = near_select(n, length)
    log1 = nt(sel, pieces3(jnp.where(near_st, st, 0.0)))
    out1 = collapse(nn(head_rows(n, R2, length, near_ref, group), att_ref[:, cols]))
    far_aux = nt(far_select(FM, length, 4 * f), pieces3(jnp.where(far_st, st, 0.0)))
    yield
    s = jnp.where(near_valid_queries(s.shape, n, own), s, NEG)
    top = jnp.max(s, axis=1, keepdims=True)
    yield
    w = jnp.exp(s - top)
    total = jnp.sum(w, axis=1, keepdims=True)
    out2 = nn(w.astype(BF), values)
    head, what = stat_row((3 * SR, GW), 0)
    lane = iota((1, GW), 1)
    piece = div(iota((3 * SR, 1), 0), SR)
    log1 = nn(log1.astype(BF), onehot((div(lane, HD) == head) & (what == 0)))
    far_aux = nn(far_aux.astype(BF), onehot((div(lane, HD) == head) & (mod(lane, HD) == what * 3 + piece)))
    yield
    out2 = collapse(out2 / total)
    log2 = collapse(jnp.broadcast_to(top + jnp.log(total), (GH * n, GW)))
    top = jnp.maximum(log1, log2)
    e1, e2 = jnp.exp(log1 - top), jnp.exp(log2 - top)
    both = e1 + e2
    log12 = top + jnp.log(both)
    out12 = (e1 * out1 + e2 * out2) / both
    near_out[:, cols] = out12.astype(BF)
    dot12 = spread_sum(qg_ref[n:, cols].astype(F32) * out12, GW)
    yield
    aux12 = pack_aux(log12, dot12).astype(BF)
    packs.append(nn(aux12, pack_lanes(group)))
    near_aux[:, cols] = aux12
    r = iota((GH * FM, 1), 0)
    j = mod(r, FM) - 4 * f
    foff, noff = row_offsets(FM, far_ref, group), row_offsets(FM, near_ref, group)
    row = jnp.where((j >= 0) & (j < f) & (mod(foff, R2) == noff), j * (R3 // R2) + div(foff, R2), -1)
    from_near = collapse(nn(onehot(iota((1, n), 1) == row), aux12))
    yield
    twice = mod(lane_offsets(far_ref, group), R2) == lane_offsets(near_ref, group)
    raw = fr_ref[:, cols].astype(F32)
    raw = jnp.where(iota((FM, 1), 0) < 4 * f, raw, 0.0)
    blocks[group] = raw + jnp.where(twice, from_near, far_aux)


def merge_kernel(peers, kv_ref, qg_ref, *rest):
    got, rest = unturned(rest[: peers - 1]), rest[peers - 1 :]
    groups = kv_ref.shape[1] // GW
    out_ref = rest[3]
    blocks, packs = {}, []
    lockstep(
        merge_group(peers, group, kv_ref, qg_ref, got, *rest, blocks, packs)
        for group in range(groups)
    )
    packed = sum(packs[1:], packs[0]).astype(BF)
    n, length = packed.shape[0], rest[1].shape[0]
    per = out_ref.shape[1] // 128
    r, c = iota((FM, 1), 0) - 5 * (length // R3), iota((1, n), 1)
    for at in range(per):
        block = blocks[at * 128 // GW][:, at * 128 % GW :][:, :128]
        rows = nn(onehot((div(c, per) == r) & (mod(c, per) == at)), packed)
        out_ref[:, at * 128 : (at + 1) * 128] = (block + rows).astype(BF)


def pair_statistics(p, st_ref, aux_ref, fr_ref):
    length = st_ref.shape[1]
    n, f = length // R2, length // R3
    near, far = read_offsets(fr_ref, f, p * 2 // GH)
    r, lane, t = iota((8, 1), 0), iota((1, PW), 1), iota((1, length), 1)
    noff, foff = (jnp.where(mod(r, 2) == 0, ref[2 * p], ref[2 * p + 1]) for ref in (near, far))
    mine = (div(lane, HD) == mod(r, 2)) & (div(mod(lane, HD), 3) == div(r, 2)) & (r < 4)
    merged = nt(onehot(mine), aux_ref[:, pair_columns(p)])
    place = onehot(div(t, R2) == iota((n, 1), 0))
    merged = nn(pieces3(merged), place)
    merged = merged[:8] + merged[8:16] + merged[16:]
    st = jnp.where(mod(t, R2) == noff, merged, st_ref[p * 8 : p * 8 + 8, :])
    return jnp.where(mod(t, R3) == foff, -NEG, st)


def backward_kernel(strip, skew, span, aliased, q_ref, k_ref, v_ref, g_ref, st_ref, aux_ref, fr_ref, *rest):
    dq_ref, dk_ref, dv_ref = rest[aliased:]
    length = q_ref.shape[0]
    first, in_head = head_masks()
    diag = iota((strip, 1), 0) <= iota((1, strip), 1)
    eye = eye_of(PW)
    strips = length // strip
    kept = {}

    def score(p, c, h):
        cols, rows = pair_columns(p), slice(c * strip, (c + 1) * strip)
        if c == 0 and h == 0:
            kept["k", p] = (nt(eye, k_ref[:, cols]) * SCALE).astype(BF)
            kept["q", p] = q_ref[:, cols] * jnp.asarray(SCALE, BF)
        s = nt(k_ref[rows, cols] * in_head[h], kept["q", p][c * strip :])
        dp = nt(v_ref[rows, cols] * in_head[h], g_ref[c * strip :, cols])
        kept["s", p, c, h] = s, dp

    def soften(p, c, h):
        s, dp = kept.pop(("s", p, c, h))
        st = kept["st", p][:, c * strip :]
        prob = jnp.exp(s - st[h : h + 1])
        head = jnp.where(diag, prob[:, :strip], 0.0)
        prob = jnp.concatenate([head, prob[:, strip:]], axis=1) if c + 1 < strips else head
        ds = prob * (dp - st[2 + h : 3 + h])
        kept["p", p, c, h] = prob.astype(BF), ds.astype(BF)

    def mix(p, c, h):
        cols, rows = pair_columns(p), slice(c * strip, (c + 1) * strip)
        prob, ds = kept.pop(("p", p, c, h))
        dv = nn(prob, g_ref[c * strip :, cols])
        dk = nn(ds, kept["q", p][c * strip :])
        part = nn(kept["k", p][h * HD : (h + 1) * HD, rows], ds)
        for r in range(c, strips):
            term = part[:, (r - c) * strip : (r - c + 1) * strip]
            kept["dq", p, r, h] = kept["dq", p, r, h] + term if c else term
        kept["dkv", p, c, h] = dk, dv
        if h == 1:
            one, two = kept.pop(("dkv", p, c, 0)), kept.pop(("dkv", p, c, 1))
            dk_ref[rows, cols] = jnp.where(first, one[0], two[0]).astype(BF)
            dv_ref[rows, cols] = jnp.where(first, one[1], two[1]).astype(BF)
            both = jnp.concatenate([kept.pop(("dq", p, c, 0)), kept.pop(("dq", p, c, 1))], axis=0)
            dq_ref[rows, cols] = both.T.astype(BF)

    for p in span:
        kept["st", p] = pair_statistics(p, st_ref, aux_ref, fr_ref)
    units = [(p, c, h) for p in span for c in range(strips) for h in range(2)]
    staged(units, (score, soften, mix), skew)


def far_seq(index, f, digits, own):
    slot = div(index, f)
    seq = own
    for radix, unit in digits:
        seq = seq ^ (mod(slot, radix) * unit)
        slot = div(slot, radix)
    return seq * f + mod(index, f)


def row_offsets(n, ref, group):
    r = iota((GH * n, 1), 0)
    out = jnp.zeros((GH * n, 1), jnp.int32)
    for h in range(GH):
        out = jnp.where(div(r, n) == h, ref[group * GH + h], out)
    return out


def place_columns(n, length, near_ref, far_ref, group):
    parts = []
    for count, stride, ref in ((n, R2, near_ref), (FM, R3, far_ref)):
        c = iota((1, GH * count), 1)
        token = mod(c, count) * stride
        for h in range(GH):
            token = jnp.where(div(c, count) == h, token + ref[group * GH + h], token)
        parts.append(token)
    return onehot(iota((length, 1), 0) == jnp.concatenate(parts, axis=1))


def own_lanes(x):
    n = x.shape[0] // GH
    return jnp.where(div(iota((1, x.shape[1]), 1), HD) == div(iota((x.shape[0], 1), 0), n), x, 0.0)


def piece_columns(aux_expanded):
    a, c = iota((GW, 1), 0), iota((1, 256), 1)
    both = nn(aux_expanded, onehot(div(mod(a, HD), 3) == div(c, 128)))
    return both[:, :1], both[:, 128:129]


def near_group(peers, group, fr_ref, packed, kv_ref, qg_ref, got, dq_ref, dk_ref, dv_ref, keep_ref):
    cols = group_columns(group)
    n = dq_ref.shape[0]
    f = n * R2 // R3
    near_ref, far_ref = read_offsets(fr_ref, f, group)
    own = lax.axis_index("row") % peers
    keys, values, queries, grads = near_operands(n, cols, kv_ref, qg_ref, got)
    naux = nn(packed(), unpack_lanes(group))
    s = nt(expand(queries[:n]), keys)
    dp = nt(expand(grads[:n]), values)
    yield
    s2 = nt(expand(keys[:n]), queries)
    dp2 = nt(expand(values[:n]), grads)
    noff, foff = lane_offsets(near_ref, group), lane_offsets(far_ref, group)
    also_far = (mod(iota((naux.shape[0], 1), 0), R3 // R2) == div(foff, R2)) & (mod(foff, R2) == noff)
    none = jnp.where(mod(iota((1, GW), 1), HD) == 0, -NEG, 0.0)
    naux = jnp.where(also_far, none, naux).astype(BF)
    yield
    log_q, dot_q = piece_columns(expand(naux[:n]))
    log_k, dot_k = piece_rows(n, naux)
    yield
    ok = near_valid_queries(s.shape, n, own)
    p = jnp.where(ok, jnp.exp(s - log_q), 0.0)
    ds = (p * (dp - dot_q)).astype(BF)
    yield
    ok = near_valid_keys(s2.shape, n, own)
    p = jnp.where(ok, jnp.exp(s2 - log_k), 0.0)
    ds2 = (p * (dp2 - dot_k)).astype(BF)
    yield
    dq_ref[:, cols] = (collapse(nn(ds, keys)) * SCALE).astype(BF)
    yield
    dk_ref[:, cols] = collapse(nn(ds2, queries)).astype(BF)
    dv_ref[:, cols] = collapse(nn(p.astype(BF), grads)).astype(BF)
    yield
    near, far = token_masks(near_ref, far_ref, group, n * R2)
    keep_ref[:, cols] = onehot(jnp.logical_not(near | far))


def near_kernel(peers, stride, fr_ref, fa_ref, kv_ref, qg_ref, *rest):
    got, outs = unturned(rest[: peers - 1]), rest[peers - 1 :]
    n, width = outs[0].shape
    made = []

    def packed():
        if not made:
            made.append(unpack_rows(peers, stride, n, n * R2 // R3, fa_ref))
        return made[0]

    lockstep(
        near_group(peers, group, fr_ref, packed, kv_ref, qg_ref, got, *outs) for group in range(width // GW)
    )


def near_operands(n, cols, kv_ref, qg_ref, got):
    heads = [kv_ref, *got]
    keys = jnp.concatenate([x[:n, cols] for x in heads], axis=0)
    values = jnp.concatenate([x[n:, cols] for x in heads], axis=0)
    heads = [qg_ref, *got]
    queries = jnp.concatenate([x[:n, cols] for x in heads], axis=0) * jnp.asarray(SCALE, BF)
    grads = jnp.concatenate([x[n:, cols] for x in heads], axis=0)
    return keys, values, queries, grads


def piece_rows(n, aux):
    r, c = iota((2 * GH * n, 1), 0), iota((1, GW), 1)
    head, which = div(mod(r, GH * n), n), div(r, GH * n)
    both = nt(onehot((div(c, HD) == head) & (div(mod(c, HD), 3) == which)), aux)
    return both[: GH * n], both[GH * n :]


def final_group(
    peers, stride, digits, group, fr_ref, got, fa_ref, k_ref, v_ref, base, near_out, near_grads, sel, outs, done
):
    kv_ref, qg_ref, got = got[0], got[1], unturned(got[2:])
    cols = group_columns(group)
    length = k_ref.shape[0]
    n, f = length // R2, length // R3
    near_ref, far_ref = read_offsets(fr_ref, f, group)
    blocks = fa_ref.shape[0] // FM
    F = blocks * f
    row_here = lax.axis_index("row")
    own = row_here % peers
    seq = lax.axis_index("col") * lax.axis_size("row") + row_here
    scale = jnp.asarray(SCALE, BF)

    fa = nn(sel, fa_ref[:, cols])
    yield
    fa = fa.astype(BF)
    fq, fk, fv, fg, faux = (fa[i * F : (i + 1) * F] for i in range(5))
    qx, gx, ax = expand(fq * scale), expand(fg), expand(faux)
    s = nt(qx, fk)
    dp = nt(gx, fv)
    log12, dot12 = piece_columns(ax)
    yield
    keys, values, _, _ = near_operands(n, cols, kv_ref, qg_ref, got)
    kx, vx = expand(keys[:n]), expand(values[:n])
    fq = fq * scale
    part = peers * stride * f
    key_s, key_dp = nt(kx, fq[:part]), nt(vx, fg[:part])
    place_q = far_seq(mod(iota((GH * F, 1), 0), F), f, digits, seq)
    place_k = far_seq(iota((1, F), 1), f, digits, seq)
    s = jnp.where(place_k <= place_q, s, NEG)
    top = jnp.max(s, axis=1, keepdims=True)
    yield
    w = jnp.exp(s - top)
    total = jnp.sum(w, axis=1, keepdims=True)
    dot3 = jnp.sum(w * dp, axis=1, keepdims=True)
    k, v = k_ref[:, cols], v_ref[:, cols]

    def own_rows(x):
        return jnp.concatenate([x[h * F : h * F + FM] for h in range(GH)], axis=0)

    qo, go = own_rows(qx), own_rows(gx)
    local_s, local_dp = nt(qo, k), nt(go, v)
    near_s, near_dp = nt(qo, keys), nt(go, values)
    roff, rnear = row_offsets(FM, far_ref, group), row_offsets(FM, near_ref, group)
    token = mod(iota((GH * FM, 1), 0), FM) * R3 + roff
    att_far = nn(onehot(iota((1, length), 1) == token), base[0][:, cols])
    near_far = nn(onehot(iota((1, n), 1) * R2 + rnear == token), near_out[:, cols])
    att_far = jnp.where(mod(roff, R2) == rnear, near_far, att_far)
    yield
    log3 = top + jnp.log(total)
    dot3 = dot3 / total
    top = jnp.maximum(log12, log3)
    e12, e3 = jnp.exp(log12 - top), jnp.exp(log3 - top)
    both = e12 + e3
    log_all = top + jnp.log(both)
    dot_all = (e12 * dot12 + e3 * dot3) / both
    p = jnp.exp(s - log_all)
    ds = p * (dp - dot_all)
    pb, dsb = p.astype(BF), ds.astype(BF)
    log_own, dot_own, keep = own_rows(log_all), own_rows(dot_all), own_rows(e12 / both)
    yield
    final_aux = pack_aux(
        *(collapse(jnp.broadcast_to(x, (GH * F, GW)))[:part] for x in (log_all, dot_all))
    ).astype(BF)
    far_out = own_lanes(nn(own_rows(pb), fv) + keep * att_far)
    far_dq = nn(own_rows(dsb), fk)
    far_dv = tn(pb, gx)[:FM]
    far_dk = tn(dsb, qx)[:FM]
    yield
    r = iota((GH * FM, 1), 0)
    reach = jnp.where(mod(r, FM) < f, token, -1)
    ok = iota((1, length), 1) <= reach
    p = jnp.where(ok, jnp.exp(local_s - log_own), 0.0)
    ds = (p * (local_dp - dot_own)).astype(BF)
    pb = p.astype(BF)
    twice = mod(roff, R2) == rnear
    c = iota((1, peers * n), 1)
    slot = div(c, n)
    ok = twice & (reach >= 0) & (((slot ^ own) < own) | ((slot == 0) & (mod(c, n) <= div(reach, R2))))
    np = jnp.where(ok, jnp.exp(near_s - log_own), 0.0)
    nds = (np * (near_dp - dot_own)).astype(BF)
    yield
    log_k, dot_k = piece_rows(n, final_aux)
    far_dq += nn(nds, keys)
    far_dq = own_lanes(far_dq + nn(ds, k))
    place = place_columns(n, length, near_ref, far_ref, group)
    noff, foff = lane_offsets(near_ref, group), lane_offsets(far_ref, group)
    also_far = (mod(iota((n, 1), 0), R3 // R2) == div(foff, R2)) & (mod(foff, R2) == noff)
    alone = jnp.where(also_far, 0.0, near_out[:, cols].astype(F32)).astype(BF)
    placed = nn(place, jnp.concatenate([expand(alone), far_out.astype(BF)], axis=0))
    yield
    outs[0][:, cols] = ((base[0][:, cols] * near_grads[3][:, cols]).astype(F32) + placed).astype(BF)
    done(0, cols)
    yield
    koff, knear = row_offsets(n, far_ref, group), row_offsets(n, near_ref, group)
    c = iota((1, part), 1)
    slot = div(c, f)
    other = div(slot, stride)
    late = ((other ^ own) > own) | ((other == 0) & (mod(iota((GH * n, 1), 0), n) <= div(mod(c, f) * R3 + koff, R2)))
    ok = (mod(koff, R2) == knear) & (mod(slot, stride) == 0) & late
    np = jnp.where(ok, jnp.exp(key_s - log_k), 0.0)
    nds = (np * (key_dp - dot_k)).astype(BF)
    dk = tn(ds, qo)
    dv = tn(pb, go)
    yield
    near_dq = expand(near_grads[0][:, cols]).astype(F32)
    near_dk = own_lanes(nn(nds, fq[:part])) + expand(near_grads[1][:, cols]).astype(F32)
    near_dv = own_lanes(nn(np.astype(BF), fg[:part])) + expand(near_grads[2][:, cols]).astype(F32)
    yield
    terms = nn(place, jnp.concatenate([near_dq, far_dq * SCALE], axis=0).astype(BF))
    outs[1][:, cols] = (base[1][:, cols].astype(F32) + terms).astype(BF)
    done(1, cols)
    yield
    terms = dk + nn(place, jnp.concatenate([near_dk.astype(BF), expand(far_dk.astype(BF))], axis=0))
    outs[2][:, cols] = (base[2][:, cols].astype(F32) + terms).astype(BF)
    done(2, cols)
    yield
    terms = dv + nn(place, jnp.concatenate([near_dv.astype(BF), expand(far_dv.astype(BF))], axis=0))
    outs[3][:, cols] = (base[3][:, cols].astype(F32) + terms).astype(BF)
    done(3, cols)


def final_kernel(peers, stride, digits, fr_ref, *refs):
    near_end = 2 + peers
    count = near_end + 2 + 9
    held, results = refs[:count], refs[count : count + 4]
    outs, out_sems = refs[count + 4 : count + 8], refs[-1]

    sent = []

    def done(which, cols):
        copy = pltpu.make_async_copy(
            outs[which].at[:, cols], results[which].at[:, cols], out_sems.at[which, cols.start // GW]
        )
        copy.start()
        sent.append(copy)

    near, local, base = held[1:near_end], held[near_end : near_end + 2], held[near_end + 2 :]
    groups = results[0].shape[1] // GW
    length = results[0].shape[0]
    f, rows = length // R3, held[0].shape[0]
    F = rows // FM * f
    r, c = iota((5 * F, 1), 0), iota((1, rows), 1)
    i, at = div(r, F), mod(r, F)
    sel = onehot(c == div(at, f) * FM + i * f + mod(at, f))
    lockstep(
        final_group(
            peers, stride, digits, group, fr_ref, near, held[0], *local,
            base[:4], base[4], base[5:], sel, outs, done,
        )
        for group in range(groups)
    )
    for copy in sent:
        copy.wait()


def turned(x):
    return [x[-1], *x[:-1]]


def unturned(x):
    return [*x[1:], x[0]]


def smem():
    return pl.BlockSpec(memory_space=pltpu.SMEM)


def whole_block(rows, width):
    return pl.BlockSpec((rows, width), lambda g: (0, 0))


def group_block(rows):
    return pl.BlockSpec((rows, GW), lambda g: (0, g))


def params(limit=VMEM_LIMIT):
    return pltpu.CompilerParams(vmem_limit_bytes=limit * 1024 * 1024)


def shards(queries, key_vectors, value_vectors, out_grad, near_offsets, far_offsets):
    length, width = queries.shape
    row_count = lax.axis_size("row")
    col_count = lax.axis_size("col")
    peers = SEG2 // length
    n, f = length // R2, length // R3
    groups = width // GW
    pairs = width // PW

    def like(rows):
        return jax.ShapeDtypeStruct((rows, width), BF)

    def swap(x, axis, mask):
        size = lax.axis_size(axis)
        return lax.ppermute(x, axis, [(i, i ^ mask) for i in range(size)])

    picked = pl.pallas_call(
        functools.partial(pick_kernel, peers),
        grid=(groups,),
        in_specs=[smem(), smem()] + [group_block(length)] * 4,
        out_specs=[group_block(2 * n)] * 2 + [group_block(FM)] + [group_block(2 * n)] * (peers - 1),
        out_shape=[like(2 * n)] * 2 + [like(FM)] + [like(2 * n)] * (peers - 1),
        compiler_params=params(PICK_LIMIT),
        name="pick",
    )(near_offsets, far_offsets, queries, key_vectors, value_vectors, out_grad)
    kv, qg, fr, msgs = picked[0], picked[1], picked[2], picked[3:]
    got = [swap(msgs[s - 1], "row", s) for s in range(1, peers)]

    ops = 2 * H * length * length * HD
    stats = jax.ShapeDtypeStruct((pairs * 8, length), F32)
    per = 3

    vmem_spec = pl.BlockSpec(memory_space=pltpu.VMEM)

    def pair_block(first):
        return pl.BlockSpec((length, per * PW), lambda p: (0, first + p))

    def stat_block(first):
        return pl.BlockSpec((per * 8, length), lambda p: (first + p, 0))

    att1, st1 = pl.pallas_call(
        functools.partial(forward_kernel, 256, 2),
        in_specs=[vmem_spec] * 4,
        out_specs=[vmem_spec] * 2,
        out_shape=[like(length), stats],
        compiler_params=params(),
        cost_estimate=pl.CostEstimate(flops=2 * ops * 4, bytes_accessed=6 * length * width * 2, transcendentals=0),
        name="forward",
    )(queries, key_vectors, value_vectors, out_grad)

    mine, near_aux, near_out = pl.pallas_call(
        functools.partial(merge_kernel, peers),
        in_specs=[vmem_spec] * (peers + 4),
        out_specs=[vmem_spec] * 3,
        out_shape=[like(FM), like(n), like(n)],
        compiler_params=params(),
        name="merge",
    )(kv, qg, *turned(got), st1, att1, fr)

    grads = []
    pieces = pairs // per

    def backward(piece, grads):
        any_spec = pl.BlockSpec(memory_space=pl.ANY)
        aliased = len(grads)
        return pl.pallas_call(
            functools.partial(backward_kernel, 256, 1, range(piece * per, (piece + 1) * per), aliased),
            in_specs=[vmem_spec] * (7 + aliased),
            out_specs=[vmem_spec] * 3,
            out_shape=[like(length)] * 3,
            input_output_aliases={7 + i: i for i in range(aliased)},
            compiler_params=params(),
            cost_estimate=pl.CostEstimate(
                flops=5 * ops * 4 // pieces, bytes_accessed=8 * length * width * 2 // pieces, transcendentals=0
            ),
            name="backward",
        )(queries, key_vectors, value_vectors, out_grad, st1, near_aux, fr, *grads)

    def beside(at, count):
        if at == count - 1:
            return range(pieces - 1 if count > 1 else 0, pieces)
        return range(pieces - 1) if at == 0 else ()

    def near_pass(far_all):
        return pl.pallas_call(
            functools.partial(near_kernel, peers, stride),
            in_specs=[vmem_spec] * (peers + 3),
            out_specs=[vmem_spec] * 4,
            out_shape=[like(n)] * 3 + [like(length)],
            compiler_params=params(),
            cost_estimate=pl.CostEstimate(flops=ops, bytes_accessed=2 * length * width, transcendentals=0),
            name="near",
        )(fr, far_all, kv, qg, *turned(got))

    def bits_of(size, least):
        while size > least:
            pick = 4 if size >= 4 * least else 2
            size //= pick
            yield pick, size

    steps = [("col", radix, unit, unit * row_count) for radix, unit in bits_of(col_count, 2)]
    steps += [("row", radix, unit, unit) for radix, unit in bits_of(row_count, peers)]
    stride = 1
    for _, radix, _, _ in steps:
        stride *= radix
    steps.append(("row", peers, 1, 1))
    if col_count > 1:
        steps.append(("col", 2, 1, row_count))
    far_all = mine
    for at, (axis, radix, unit, _) in enumerate(steps):
        others = [swap(far_all, axis, digit * unit) for digit in range(1, radix)]
        if at == len(steps) - 1 and col_count > 1:
            near_grads = near_pass(far_all)
            near_grads, others = lax.optimization_barrier((near_grads, others))
        else:
            for piece in beside(at, len(steps) - 1):
                grads = backward(piece, grads)
            grads, others = lax.optimization_barrier((grads, others))
        far_all = jnp.concatenate([far_all, *others], axis=0)
    if col_count == 1:
        near_grads = near_pass(far_all)
    digits = tuple((radix, unit) for _, radix, _, unit in steps)

    operands = (fr, far_all, kv, qg, *turned(got), key_vectors, value_vectors, att1, *grads, near_out, *near_grads)
    return pl.pallas_call(
        functools.partial(final_kernel, peers, stride, digits),
        in_specs=[vmem_spec] * len(operands),
        out_specs=[pl.BlockSpec(memory_space=pl.ANY)] * 4,
        out_shape=[like(length)] * 4,
        scratch_shapes=[pltpu.VMEM((length, width), BF)] * 4 + [pltpu.SemaphoreType.DMA((4, groups))],
        compiler_params=params(),
        name="final",
    )(*operands)


def solution(mesh):
    placed = (
        P(("col", "row"), None),
        P(("col", "row"), None),
        P(("col", "row"), None),
        P(("col", "row"), None),
        P(),
        P(),
    )
    return jax.shard_map(
        shards,
        mesh=mesh,
        in_specs=placed,
        out_specs=(
            P(("col", "row"), None),
            P(("col", "row"), None),
            P(("col", "row"), None),
            P(("col", "row"), None),
        ),
        check_vma=False,
    )
```
